32 devices in a mesh: dp: 2 (over y), row: 4 (over z), col: 4 (over x, core).
Axes of the slice: x: 2, y: 2, z: 4, core: 2. Of those that a mesh axis runs over, the one named last changes fastest.
Arguments:
- block_input: bfloat16 [2048, 2048], P(('dp', 'row'), 'col'), may hold values from -6 to 6
- mixer_gain: float32 [2048], P('col'), may hold values from 0.25 to 1.75
- ssm_gate_weight: bfloat16 [2048, 3072], P('col', 'row'), may hold values from -0.125 to 0.125
- ssm_input_weight: bfloat16 [2048, 3072], P('col', 'row'), may hold values from -0.125 to 0.125
- ssm_bc_weight: bfloat16 [2048, 512], P('col', 'row'), may hold values from -0.125 to 0.125
- ssm_step_weight: bfloat16 [2048, 48], P('col', 'row'), may hold values from -0.125 to 0.125
- query_weight: bfloat16 [2048, 1024], P('col', 'row'), may hold values from -0.125 to 0.125
- keyval_weight: bfloat16 [2048, 512], P('col', 'row'), may hold values from -0.125 to 0.125
- conv_input: float32 [4, 3072], P(None, ('row', 'col')), may hold values from -0.5 to 0.5
- conv_states: float32 [4, 512], P(None, ('row', 'col')), may hold values from -0.5 to 0.5
- step_bias: float32 [48], P(('row', 'col')), may hold values from -6 to -2
- decay_log: float32 [48], P(('row', 'col')), may hold values from 0 to 2.8
- skip_gain: float32 [48], P(('row', 'col')), may hold values from 0.5 to 4
- ssm_norm_gain: float32 [3072], P(('row', 'col')), may hold values from 0.25 to 1.75
- ssm_out_weight: bfloat16 [3072, 2048], P('row', 'col'), may hold values from -0.109375 to 0.109375
- attn_out_weight: bfloat16 [1024, 2048], P('row', 'col'), may hold values from -3 to 3
- ffn_gain: float32 [2048], P('col'), may hold values from 0.25 to 1.75
- gate_up_weight: bfloat16 [2048, 2, 4096], P('col', None, 'row'), may hold values from -0.125 to 0.125
- down_weight: bfloat16 [4096, 2048], P('row', 'col'), may hold values from -0.09375 to 0.09375
- cotangent: float32 [2048, 2048], P(('dp', 'row'), 'col'), may hold values from -6 to 6
Outputs:
- output: bfloat16 [2048, 2048], P(('dp', 'row'), 'col')
- input_grad: float32 [2048, 2048], P(('dp', 'row'), 'col')
- mixer_gain_grad: float32 [2048], P('col')
- ssm_gate_grad: float32 [2048, 3072], P('col', 'row')
- ssm_input_grad: float32 [2048, 3072], P('col', 'row')
- ssm_bc_grad: float32 [2048, 512], P('col', 'row')
- ssm_step_grad: float32 [2048, 48], P('col', 'row')
- query_grad: float32 [2048, 1024], P('col', 'row')
- keyval_grad: float32 [2048, 512], P('col', 'row')
- conv_input_grad: float32 [4, 3072], P(None, ('row', 'col'))
- conv_states_grad: float32 [4, 512], P(None, ('row', 'col'))
- step_bias_grad: float32 [48], P(('row', 'col'))
- decay_log_grad: float32 [48], P(('row', 'col'))
- skip_gain_grad: float32 [48], P(('row', 'col'))
- ssm_norm_gain_grad: float32 [3072], P(('row', 'col'))
- ssm_out_grad: float32 [3072, 2048], P('row', 'col')
- attn_out_grad: float32 [1024, 2048], P('row', 'col')
- ffn_gain_grad: float32 [2048], P('col')
- gate_up_grad: float32 [2048, 2, 4096], P('col', None, 'row')
- down_grad: float32 [4096, 2048], P('row', 'col')
The draws below stay inside these ranges and needn't reach their ends.
All inputs are finite; a program needn't handle non-finite values.
Results may differ from the reference program's by a relative error of at most 0.012.
Values may be sent and summed in bfloat16 or wider, within the bound.
A program may use at most 192 MiB of HBM per device.

```python
import jax
import jax.numpy as jnp
from jax import lax

D = 2048
HEADS = 48
HDIM = 64
STATE = 256
CONV = 4
QHEADS = 8
KVHEADS = 2
ADIM = 128
FF = 4096
LEN = 1024
SPAN = 256
TOKENS = 2048
N_DP = 2


def levels(own_key, shape, split, low, top_value):
    def one(axis_at, shards_of):
        draws = jax.random.uniform(jax.random.fold_in(jax.random.fold_in(own_key, 6), axis_at), (shards_of,), jnp.float32, low / len(split), top_value / len(split))
        return jnp.repeat(jnp.exp(draws), shape[axis_at] // shards_of).reshape((-1,) + (1,) * (len(shape) - axis_at - 1))

    loudness = one(*split[0])
    for cut in split[1:]:
        loudness = loudness * one(*cut)
    return loudness


def bell_draw(own_key, dims, spread, limit, shards=(), kind=jnp.bfloat16):
    drawn = jax.random.normal(own_key, dims, jnp.float32) * spread
    if len(shards) > 0:
        drawn = levels(own_key, dims, shards, -0.22, 0.18) * drawn
    return jnp.clip(drawn, min=-limit, max=limit).astype(kind)


def setup_inputs(seed: int = 0) -> dict:
    key_list = jax.random.split(jax.random.key(seed), 21)
    return {
        "block_input": bell_draw(key_list[0], (TOKENS, D), 1.0, 6.0, ((0, 8), (1, 4))),
        "mixer_gain": jnp.clip(1.0 + 0.15 * jax.random.normal(key_list[1], (D,), jnp.float32), 0.25, 1.75),
        "ssm_gate_weight": bell_draw(key_list[2], (D, HEADS * HDIM), D ** -0.5, 0.125, ((0, 4), (1, 4))),
        "ssm_input_weight": bell_draw(key_list[3], (D, HEADS * HDIM), D ** -0.5, 0.125, ((0, 4), (1, 4))),
        "ssm_bc_weight": bell_draw(key_list[4], (D, 2 * STATE), D ** -0.5, 0.125, ((0, 4), (1, 4))),
        "ssm_step_weight": bell_draw(key_list[5], (D, HEADS), D ** -0.5, 0.125, ((0, 4), (1, 4))),
        "query_weight": bell_draw(key_list[6], (D, QHEADS * ADIM), D ** -0.5, 0.125, ((0, 4), (1, 4))),
        "keyval_weight": bell_draw(key_list[7], (D, 2 * KVHEADS * ADIM), D ** -0.5, 0.125, ((0, 4), (1, 4))),
        "conv_input": jnp.clip(jax.random.uniform(key_list[8], (CONV, HEADS * HDIM), jnp.float32, -0.5, 0.5) * levels(key_list[8], (CONV, HEADS * HDIM), ((1, 16),), -0.4, 0.0), -0.5, 0.5),
        "conv_states": jnp.clip(jax.random.uniform(key_list[9], (CONV, 2 * STATE), jnp.float32, -0.5, 0.5) * levels(key_list[9], (CONV, 2 * STATE), ((1, 16),), -0.4, 0.0), -0.5, 0.5),
        "step_bias": jnp.clip(-6.0 + 4.0 * jax.random.uniform(key_list[10], (HEADS,), jnp.float32) ** levels(key_list[10], (HEADS,), ((0, 16),), -0.2, 0.2), -6.0, -2.0),
        "decay_log": jnp.clip(2.8 * jax.random.uniform(key_list[11], (HEADS,), jnp.float32) ** levels(key_list[11], (HEADS,), ((0, 16),), -0.2, 0.2), 0.0, 2.8),
        "skip_gain": jnp.clip(0.5 + 3.5 * jax.random.uniform(key_list[12], (HEADS,), jnp.float32) ** levels(key_list[12], (HEADS,), ((0, 16),), -0.2, 0.2), 0.5, 4.0),
        "ssm_norm_gain": jnp.clip(1.0 + 0.15 * jax.random.normal(key_list[13], (HEADS * HDIM,), jnp.float32), 0.25, 1.75),
        "ssm_out_weight": bell_draw(key_list[14], (HEADS * HDIM, D), (HEADS * HDIM) ** -0.5, 0.109375, ((0, 4), (1, 4))),
        "attn_out_weight": bell_draw(key_list[15], (QHEADS * ADIM, D), (max(QHEADS * ADIM // 256, 1)) ** -0.5, 3.0, ((0, 4), (1, 4))),
        "ffn_gain": jnp.clip(1.0 + 0.15 * jax.random.normal(key_list[16], (D,), jnp.float32), 0.25, 1.75),
        "gate_up_weight": bell_draw(key_list[17], (D, 2, FF), D ** -0.5, 0.125, ((0, 4), (2, 4))),
        "down_weight": bell_draw(key_list[18], (FF, D), FF ** -0.5, 0.09375, ((0, 4), (1, 4))),
        "cotangent": bell_draw(key_list[19], (TOKENS, D), 1.0, 6.0, ((0, 8), (1, 4)), jnp.float32),
    }


EPSILON = 1e-05
ROPE_BASE = 100000000000.0
HIGHEST = lax.Precision.HIGHEST
NEGATIVE = -1e+30

@jax.custom_vjp
def low(v):
    return lax.optimization_barrier(v.astype(jnp.bfloat16)).astype(jnp.float32)

@jax.custom_vjp
def low_back(v):
    return v

def low_keep(v):
    return (low(v), None)

def low_pass(kept, grad):
    return (grad,)

def back_keep(v):
    return (v, None)

def back_low(kept, grad):
    return (low(grad),)
low.defvjp(low_keep, low_pass)
low_back.defvjp(back_keep, back_low)

def matmul_high(left, right):
    return jnp.dot(left, right, precision=HIGHEST, preferred_element_type=jnp.float32)

def softplus(values):
    return jnp.maximum(values, 0.0) + jnp.log1p(jnp.exp(-jnp.abs(values)))

def causal_conv(series, kernel):
    taps = kernel.shape[0]
    length = series.shape[1]
    padded = jnp.pad(series, ((0, 0), (taps - 1, 0), (0, 0)))
    total = jnp.zeros(series.shape, jnp.float32)
    for kernel_row in range(taps):
        total = total + padded[:, kernel_row:kernel_row + length, :] * kernel[kernel_row]
    return total

def conv_piece(raw_cols, kernel, seq_count):
    tokens = raw_cols.shape[0]
    shaped = raw_cols.reshape(seq_count, tokens // seq_count, raw_cols.shape[1])
    return jax.nn.silu(causal_conv(shaped, kernel)).reshape(tokens, raw_cols.shape[1])

def ssd_block(state, block):
    xdt, b_rows, c_rows, rates = block
    size_q = rates.shape[1]
    within = jnp.cumsum(rates, axis=1)
    rows_i = lax.broadcasted_iota(jnp.int32, (size_q, size_q), 0)
    cols_j = lax.broadcasted_iota(jnp.int32, (size_q, size_q), 1)
    lower = (cols_j <= rows_i)[None, :, :, None]
    gaps = within[:, :, None, :] - within[:, None, :, :]
    decay = jnp.where(lower, jnp.exp(jnp.where(lower, gaps, 0.0)), 0.0)
    scores = jnp.einsum('sin,sjn->sij', c_rows, b_rows, precision=HIGHEST)
    inner = jnp.einsum('sijh,sjhp->sihp', scores[..., None] * decay, xdt, precision=HIGHEST)
    carried = jnp.einsum('sin,shpn->sihp', c_rows, state, precision=HIGHEST) * jnp.exp(within)[..., None]
    last_sum = within[:, -1, :]
    weights = jnp.exp(last_sum[:, None, :] - within)
    fresh = jnp.einsum('sjhp,sjn->shpn', xdt * weights[..., None], b_rows, precision=HIGHEST)
    new_state = state * jnp.exp(last_sum)[:, :, None, None] + fresh
    return (new_state, inner + carried)

def ssd_scan(xdt, b_rows, c_rows, rates):
    seq_count, length, heads, head_dim = xdt.shape
    blocks = length // SPAN

    def split_blocks(values):
        shaped = values.reshape((seq_count, blocks, SPAN) + values.shape[2:])
        return jnp.moveaxis(shaped, 1, 0)
    state = jnp.zeros((seq_count, heads, head_dim, b_rows.shape[2]), jnp.float32)
    _, outputs = lax.scan(jax.checkpoint(ssd_block), state, (split_blocks(xdt), split_blocks(b_rows), split_blocks(c_rows), split_blocks(rates)))
    return jnp.moveaxis(outputs, 0, 1).reshape(seq_count, length, heads, head_dim)

def mamba_core(seq_count, x_raw, z_cols, step_raw, bc_full, conv_input, step_bias, decay_log, skip_gain):
    tokens, breadth = x_raw.shape
    heads = step_raw.shape[1]
    head_dim = breadth // heads
    length = tokens // seq_count
    states_n = bc_full.shape[1] // 2
    mixed_x = conv_piece(x_raw, conv_input, seq_count).reshape(seq_count, length, heads, head_dim)
    steps_dt = softplus(step_raw + step_bias).reshape(seq_count, length, heads)
    rates = -steps_dt * jnp.exp(decay_log)
    b_rows = bc_full[:, :states_n].reshape(seq_count, length, states_n)
    c_rows = bc_full[:, states_n:].reshape(seq_count, length, states_n)
    scanned = ssd_scan(mixed_x * steps_dt[..., None], b_rows, c_rows, rates)
    outputs = scanned + skip_gain[:, None] * mixed_x
    return outputs.reshape(tokens, breadth) * jax.nn.silu(z_cols)

def rope(values, positions):
    half_dim = values.shape[-1] // 2
    freqs = ROPE_BASE ** (-jnp.arange(half_dim, dtype=jnp.float32) / half_dim)
    angles = positions.astype(jnp.float32)[:, None] * freqs
    cosine = jnp.cos(angles)[:, None, :]
    sine = jnp.sin(angles)[:, None, :]
    first = values[..., :half_dim]
    second = values[..., half_dim:]
    return jnp.concatenate([first * cosine - second * sine, second * cosine + first * sine], axis=-1)

def attention(queries, keys, values):
    scale_qk = queries.shape[-1] ** (-0.5)
    group = queries.shape[2] // keys.shape[2]

    def one_seq(block):
        q_seq, k_seq, v_seq = block
        length = q_seq.shape[0]
        k_rep = jnp.repeat(k_seq, group, axis=1)
        v_rep = jnp.repeat(v_seq, group, axis=1)
        scores = jnp.einsum('qha,kha->hqk', q_seq, k_rep, precision=HIGHEST) * scale_qk
        causal = lax.broadcasted_iota(jnp.int32, (length, length), 1) <= lax.broadcasted_iota(jnp.int32, (length, length), 0)
        scores = jnp.where(causal[None], scores, NEGATIVE)
        row_top = lax.optimization_barrier(jnp.max(scores, axis=2, keepdims=True))
        expd = jnp.exp(scores - row_top)
        probs = expd / lax.optimization_barrier(jnp.sum(expd, axis=2, keepdims=True))
        return jnp.einsum('hqk,kha->qha', low(probs), v_rep, precision=HIGHEST)
    return lax.map(jax.checkpoint(one_seq), (queries, keys, values))

def layer(rows_in, mixer_gain, ssm_gate_weight, ssm_input_weight, ssm_bc_weight, ssm_step_weight, query_weight, keyval_weight, conv_input, conv_states, step_bias, decay_log, skip_gain, ssm_norm_gain, ssm_out_weight, attn_out_weight, ffn_gain, gate_up_weight, down_weight):
    tokens = rows_in.shape[0]
    seq_count = tokens // LEN
    positions = (jnp.arange(tokens, dtype=jnp.int32) % LEN).astype(jnp.int32)
    scale_mix = lax.rsqrt(lax.optimization_barrier(jnp.mean(rows_in * rows_in, axis=1)) + EPSILON)
    normed_mix = low(rows_in * scale_mix[:, None] * mixer_gain)
    z_cols = low_back(matmul_high(normed_mix, ssm_gate_weight))
    x_raw = low_back(matmul_high(normed_mix, ssm_input_weight))
    bc_raw = low_back(matmul_high(normed_mix, ssm_bc_weight))
    step_raw = low_back(matmul_high(normed_mix, ssm_step_weight))
    q_raw = low_back(matmul_high(normed_mix, query_weight))
    kv_raw = low_back(matmul_high(normed_mix, keyval_weight))
    bc_full = low(conv_piece(bc_raw, conv_states, seq_count))
    gated = mamba_core(seq_count, x_raw, z_cols, step_raw, bc_full, conv_input, step_bias, decay_log, skip_gain)
    scale_ssm = lax.rsqrt(lax.optimization_barrier(jnp.mean(gated * gated, axis=1)) + EPSILON)
    ssm_out = low(gated * scale_ssm[:, None] * ssm_norm_gain)
    key_width = kv_raw.shape[1] // 2
    queries = low(rope(low(q_raw).reshape(tokens, QHEADS, ADIM), positions))
    kv_low = low(kv_raw)
    keys = low(rope(kv_low[:, :key_width].reshape(tokens, KVHEADS, ADIM), positions))
    values = kv_low[:, key_width:].reshape(tokens, KVHEADS, ADIM)
    attended = attention(queries.reshape(seq_count, LEN, QHEADS, ADIM), keys.reshape(seq_count, LEN, KVHEADS, ADIM), values.reshape(seq_count, LEN, KVHEADS, ADIM)).reshape(tokens, QHEADS * ADIM)
    attended = low_back(low(attended))
    mixed = low_back(matmul_high(ssm_out, ssm_out_weight) + matmul_high(attended, attn_out_weight))
    after_mix = rows_in + mixed
    scale_ffn = lax.rsqrt(lax.optimization_barrier(jnp.mean(after_mix * after_mix, axis=1)) + EPSILON)
    normed_ffn = low(after_mix * scale_ffn[:, None] * ffn_gain)
    ff_width = gate_up_weight.shape[2]
    gate_up = low_back(matmul_high(normed_ffn, gate_up_weight.reshape(gate_up_weight.shape[0], 2 * ff_width)))
    hidden = low(jax.nn.silu(gate_up[:, :ff_width]) * gate_up[:, ff_width:])
    ffn_out = low_back(matmul_high(hidden, down_weight))
    return after_mix + ffn_out

def reference(block_input, mixer_gain, ssm_gate_weight, ssm_input_weight, ssm_bc_weight, ssm_step_weight, query_weight, keyval_weight, conv_input, conv_states, step_bias, decay_log, skip_gain, ssm_norm_gain, ssm_out_weight, attn_out_weight, ffn_gain, gate_up_weight, down_weight, cotangent):
    params = [weight_arg.astype(jnp.float32) for weight_arg in (mixer_gain, ssm_gate_weight, ssm_input_weight, ssm_bc_weight, ssm_step_weight, query_weight, keyval_weight, conv_input, conv_states, step_bias, decay_log, skip_gain, ssm_norm_gain, ssm_out_weight, attn_out_weight, ffn_gain, gate_up_weight, down_weight)]
    grouped = block_input.astype(jnp.float32).reshape(N_DP, -1, D)

    def forward(rows_all, *weights):

        def one_group(carry, rows_in):
            return (carry, jax.checkpoint(layer)(rows_in, *weights))
        _, outputs = lax.scan(one_group, jnp.zeros((), jnp.float32), rows_all)
        return outputs
    result, pullback = jax.vjp(forward, grouped, *params)
    grads = pullback(cotangent.astype(jnp.float32).reshape(N_DP, -1, D))
    return (result.reshape(-1, D).astype(jnp.bfloat16), grads[0].reshape(-1, D), grads[1], grads[2], grads[3], grads[4], grads[5], grads[6], grads[7], grads[8], grads[9], grads[10], grads[11], grads[12], grads[13], grads[14], grads[15], grads[16], grads[17], grads[18])
```

```python
import types

import jax
import jax.numpy as jnp
import numpy as np
from jax import lax
from jax.experimental import pallas as pl
from jax.experimental.pallas import tpu as pltpu
from jax.sharding import PartitionSpec as P

D = 2048
HEADS = 48
HDIM = 64
STATE = 256
ADIM = 128
LEN = 1024
SPAN = 256
SIDE = 4
BLK = LEN // SIDE
HALO = 16
HH = 3
HW = HH * HDIM
EPSILON = 1e-05
ROPE_BASE = 100000000000.0
HIGHEST = lax.Precision.HIGHEST
NEGATIVE = -1e30
BF = jnp.bfloat16
F32 = jnp.float32
MESH = pl.DeviceIdType.MESH
SCALE = ADIM ** (-0.5)


def dot_nn(a, b, precision=None):
    return lax.dot_general(a, b, (((1,), (0,)), ((), ())), precision=precision, preferred_element_type=F32)


def dot_nt(a, b, precision=None):
    return lax.dot_general(a, b, (((1,), (1,)), ((), ())), precision=precision, preferred_element_type=F32)


def dot_tn(a, b, precision=None):
    return lax.dot_general(a, b, (((0,), (0,)), ((), ())), precision=precision, preferred_element_type=F32)


def sigmoid(v):
    return 1.0 / (1.0 + jnp.exp(-v))


def softplus(v):
    return jnp.maximum(v, 0.0) + jnp.log1p(jnp.exp(-jnp.abs(v)))


def iota(shape, axis):
    return lax.broadcasted_iota(jnp.int32, shape, axis)


def flip(v, d):
    v0, v1 = lax.rem(v, 2), lax.div(v, 2)
    if isinstance(d, int):
        d0, d1 = d % 2, d // 2
    else:
        d0, d1 = lax.rem(d, 2), lax.div(d, 2)
    return 2 * (v1 + d1 - 2 * v1 * d1) + (v0 + d0 - 2 * v0 * d0)


def here():
    return lax.axis_index("row"), lax.axis_index("col")


def greet(r, c, rows=False, cols=(), grid=False, dp=False):
    sem = pltpu.get_barrier_semaphore()
    peers = []
    if grid:
        for d in range(SIDE):
            for e in range(SIDE):
                if d or e:
                    peers.append({"row": flip(r, d), "col": flip(c, e)})
    else:
        if rows:
            peers += [{"row": flip(r, d)} for d in (1, 2, 3)]
        peers += [{"col": flip(c, e)} for e in cols]
    if dp:
        peers.append({"dp": 1 - lax.axis_index("dp")})
    for peer in peers:
        pl.semaphore_signal(sem, inc=1, device_id=peer, device_id_type=MESH)
    pl.semaphore_wait(sem, len(peers))


def hop(src, dst, ssem, rsem, **where):
    return pltpu.make_async_remote_copy(
        src_ref=src, dst_ref=dst, send_sem=ssem, recv_sem=rsem, device_id=where, device_id_type=MESH
    )


def rows_at(ref, block, pad=0):
    return ref.at[pl.ds(pl.multiple_of(block * BLK + pad, 16), BLK)]


def dma(*shape):
    return pltpu.SemaphoreType.DMA(shape)


def launch(body, ins, outs, scratch, cid, smem=None):
    smem = smem or {}
    shapes = []
    for item in scratch.values():
        shapes += list(item.values()) if isinstance(item, dict) else [item]

    def kernel(*refs):
        refs = list(refs)
        found = {}
        for key in (*ins, *smem, *outs):
            found[key] = refs.pop(0)
        for key, item in scratch.items():
            if isinstance(item, dict):
                found[key] = types.SimpleNamespace(**{name: refs.pop(0) for name in item})
            else:
                found[key] = refs.pop(0)
        body(types.SimpleNamespace(**found))

    vector = pl.BlockSpec(memory_space=pltpu.VMEM)
    results = pl.pallas_call(
        kernel,
        out_shape=[jax.ShapeDtypeStruct(*o) for o in outs.values()],
        in_specs=[vector] * len(ins) + [pl.BlockSpec(memory_space=pltpu.SMEM)] * len(smem),
        out_specs=[vector] * len(outs),
        scratch_shapes=shapes,
        compiler_params=pltpu.CompilerParams(
            collective_id=cid, has_side_effects=True, vmem_limit_bytes=58 << 20
        ),
        name=body.__name__,
    )(*ins.values(), *smem.values())
    return types.SimpleNamespace(**dict(zip(outs, results)))


def rows_scratch(padded=False):
    size = LEN + 2 * HALO if padded else LEN
    return dict(g=pltpu.VMEM((size, D // SIDE), BF), zs=dma(3), zr=dma(3))


def gather_rows(S, r, pad=0):
    own = rows_at(S.g, r, pad)
    for d in (1, 2, 3):
        hop(own, own, S.zs.at[d - 1], S.zr.at[d - 1], row=flip(r, d)).start()


def wait_rows(S, r, d, pad=0):
    block = flip(r, d)
    part = rows_at(S.g, block, pad)
    hop(part, part, S.zs.at[d - 1], S.zr.at[d - 1], row=block).wait_recv()


def wait_rows_sent(S, r, pad=0):
    own = rows_at(S.g, r, pad)
    for d in (1, 2, 3):
        hop(own, own, S.zs.at[d - 1], S.zr.at[d - 1], row=flip(r, d)).wait_send()


def cols_scratch(w):
    return dict(
        cs=pltpu.VMEM((SIDE, 2, BLK, w), F32),
        cr=pltpu.VMEM((SIDE, 2, BLK, w), F32),
        xs=pltpu.VMEM((SIDE, BLK, w), BF),
        xr=pltpu.VMEM((SIDE, BLK, w), BF),
        acc=pltpu.VMEM((SIDE, BLK, w), F32),
        mine=pltpu.VMEM((SIDE, BLK, w), F32),
        ks=dma(SIDE),
        kr=dma(SIDE),
        ss=dma(SIDE),
        sr=dma(SIDE),
    )


def scatter_cols(S, G, r, c, product, pad=0, finish=None, apart=False):
    cs, cr, xs, xr, acc = (S.cs, S.cr, S.xs, S.xr, S.acc)

    def core_hop(d):
        return hop(cs.at[d], cr.at[d], S.ks.at[d], S.kr.at[d], col=flip(c, 1))

    def x_hop(d):
        return hop(xs.at[d], xr.at[d], S.ss.at[d], S.sr.at[d], col=flip(c, 2))

    def first(d):
        @pl.when(d > 0)
        def _():
            wait_rows(G, r, d, pad)

        rows = rows_at(G.g, flip(r, d), pad)[...]
        cs[d, 1] = product(rows, flip(c, 3))
        cs[d, 0] = product(rows, flip(c, 1))
        core_hop(d).start()
        S.mine[d] = product(rows, flip(c, 2))
        acc[d] = product(rows, c)

    def second(d):
        core_hop(d).wait_recv()
        xs[d] = (S.mine[d] + cr[d, 1]).astype(BF)
        x_hop(d).start()
        acc[d] = acc[d] + cr[d, 0]

    def both(d, carry):
        first(d)
        second(d)
        return carry

    def only(phase):
        def step(d, carry):
            phase(d)
            return carry

        return step

    if apart:
        lax.fori_loop(0, SIDE, only(first), 0)
        lax.fori_loop(0, SIDE, only(second), 0)
    else:
        lax.fori_loop(0, SIDE, both, 0)

    def end(d, carry):
        x_hop(d).wait_recv()
        finish(flip(r, d), acc[d] + xr[d].astype(F32))
        x_hop(d).wait_send()
        core_hop(d).wait_send()
        return carry

    def close():
        lax.fori_loop(0, SIDE, end, 0)

    return close


def tokens_scratch(*shape, low=F32):
    return dict(
        cs=pltpu.VMEM((2, *shape), low),
        cr=pltpu.VMEM((2, *shape), low),
        xs=pltpu.VMEM(shape, low),
        xr=pltpu.VMEM(shape, low),
        acc=pltpu.VMEM(shape, F32),
        ks=dma(),
        kr=dma(),
        ss=dma(),
        sr=dma(),
    )


def scatter_tokens(S, c, product):
    low = S.xs.dtype
    core = hop(S.cs, S.cr, S.ks, S.kr, col=flip(c, 1))
    over = hop(S.xs, S.xr, S.ss, S.sr, col=flip(c, 2))
    S.cs[1] = product(flip(c, 3)).astype(low)
    S.cs[0] = product(flip(c, 1)).astype(low)
    core.start()
    mine = product(flip(c, 2))
    S.acc[...] = product(c)
    core.wait_recv()
    S.xs[...] = (mine + S.cr[1].astype(F32)).astype(low)
    over.start()
    S.acc[...] = S.acc[...] + S.cr[0].astype(F32)

    def close():
        over.wait_recv()
        total = S.acc[...] + S.xr[...].astype(F32)
        over.wait_send()
        core.wait_send()
        return total

    return close


def trio_scratch():
    return dict(xs=dma(), xr=dma(), ks=dma(), kr=dma(), fs=dma(), fr=dma())


def trio(S, c, part):
    own, over = part(c), part(flip(c, 2))
    return (
        hop(own, own, S.xs, S.xr, col=flip(c, 2)),
        hop(own, own, S.ks, S.kr, col=flip(c, 1)),
        hop(over, over, S.fs, S.fr, col=flip(c, 1)),
    )


def trio_end(hops):
    over, core, forward = hops
    over.wait_recv()
    forward.start()
    core.wait_recv()
    forward.wait_recv()


def gcols_scratch(w):
    return dict(
        g=pltpu.VMEM((SIDE, LEN, w), BF),
        xs=dma(SIDE),
        xr=dma(SIDE),
        ks=dma(SIDE),
        kr=dma(SIDE),
        fs=dma(SIDE),
        fr=dma(SIDE),
    )


def col_part(S, j, t):
    return S.g.at[j, pl.ds(pl.multiple_of(t * BLK, BLK), BLK)]


def col_hop(S, c, kind, t, d):
    part = col_part(S, flip(c, 2) if kind == "f" else c, t)
    to = flip(c, 2) if kind == "x" else flip(c, 1)
    return hop(part, part, getattr(S, kind + "s").at[d], getattr(S, kind + "r").at[d], col=to)


def gather_cols(S, r, c, order=(3, 2, 1, 0)):
    for d in order:
        t = flip(r, d)
        col_hop(S, c, "x", t, d).start()
        col_hop(S, c, "k", t, d).start()


def wait_cols(S, r, c, d):
    t = flip(r, d)
    col_hop(S, c, "x", t, d).wait_recv()
    col_hop(S, c, "f", t, d).start()
    col_hop(S, c, "k", t, d).wait_recv()
    col_hop(S, c, "f", t, d).wait_recv()


def wait_cols_sent(S, r, c):
    def step(d, carry):
        t = flip(r, d)
        for kind in "xkf":
            col_hop(S, c, kind, t, d).wait_send()
        return carry

    lax.fori_loop(0, SIDE, step, 0)


def srows_scratch():
    w = D // SIDE
    return dict(
        ps=pltpu.VMEM((3, BLK, w), BF),
        pr=pltpu.VMEM((3, BLK, w), BF),
        pa=pltpu.VMEM((BLK, w), F32),
        rs=dma(3),
        rr=dma(3),
    )


def scatter_rows(S, r, product, ready):
    ps, pr, acc = S.ps, S.pr, S.pa

    def row_hop(d):
        return hop(ps.at[d - 1], pr.at[d - 1], S.rs.at[d - 1], S.rr.at[d - 1], row=flip(r, d))

    def step(i, carry):
        d = 3 - i
        ready(d)
        acc[...] = product(flip(r, d))

        @pl.when(d > 0)
        def _():
            ps[d - 1] = acc[...].astype(BF)
            row_hop(d).start()

        return carry

    lax.fori_loop(0, SIDE, step, 0)

    def close():
        total = acc[...]
        for d in (1, 2, 3):
            row_hop(d).wait_recv()
            total = total + pr[d - 1].astype(F32)
        for d in (1, 2, 3):
            row_hop(d).wait_send()
        return total

    return close


def row_sums(v):
    return dot_nt(jnp.ones((8, v.shape[1]), F32), v, HIGHEST)


def stat_scratch():
    return dict(st=pltpu.VMEM((SIDE, 8, BLK), F32), sts=dma(3), str=dma(3))


def col_sum(S, c, v):
    st = S.st
    st[c] = v
    hops = [
        hop(st.at[c], st.at[c], S.sts.at[e - 1], S.str.at[e - 1], col=flip(c, e)) for e in (1, 2, 3)
    ]
    for one in hops:
        one.start()
    for one in hops:
        one.wait_recv()
    total = (st[0] + st[1]) + (st[2] + st[3])
    for one in hops:
        one.wait_send()
    return total


def grid_scratch():
    return dict(st=pltpu.VMEM((SIDE, SIDE, 8, BLK), F32), sts=dma(16), str=dma(16))


def grid_sum(S, r, c):
    st = S.st
    hops = []
    for d in range(SIDE):
        for e in range(SIDE):
            if d or e:
                k = SIDE * d + e
                hops.append(
                    hop(
                        st.at[r, c],
                        st.at[r, c],
                        S.sts.at[k],
                        S.str.at[k],
                        row=flip(r, d),
                        col=flip(c, e),
                    )
                )
    for one in hops:
        one.start()

    def close():
        for one in hops:
            one.wait_recv()
        total = jnp.zeros((8, BLK), F32)
        for d in range(SIDE):
            for e in range(SIDE):
                total = total + st[d, e]
        for one in hops:
            one.wait_send()
        return total

    return close


def to_column(v):
    return jnp.transpose(v)[:, :1]


def pick_column(v, b):
    return jnp.sum(jnp.where(iota(v.shape, 1) == b, v, 0.0), axis=1, keepdims=True)


def cut(v, j, w):
    return v[:, j * w : (j + 1) * w]


def cut(v, j, w):
    return v[:, j * w : (j + 1) * w]


def project_kernel(x, gain, wz, wx, wbc, wq, wkv, ws, cw):
    def project(R):
        r, c = here()
        greet(r, c, rows=True, cols=(1, 2, 3))
        tap_hops = [
            hop(R.taps.at[c], R.taps.at[c], R.tss.at[e - 1], R.tsr.at[e - 1], col=flip(c, e)) for e in (1, 2, 3)
        ]
        R.taps[c] = jnp.zeros((8, 128), F32)
        R.taps[c, 0:4, 0:32] = R.cw[...]
        for one in tap_hops:
            one.start()
        x = R.x[...].astype(F32)
        total = col_sum(R.n, c, row_sums(x * x))
        scale = to_column(lax.rsqrt(total / D + EPSILON))
        g = R.p.g
        g[pl.ds(0, HALO)] = jnp.zeros((HALO, D // SIDE), BF)
        g[pl.ds(LEN + HALO, HALO)] = jnp.zeros((HALO, D // SIDE), BF)
        rows_at(g, r, HALO)[...] = (x * scale * R.gain[...]).astype(BF)
        gather_rows(R.p, r, HALO)
        wa, wb = R.wa, R.wb
        for j in range(SIDE):
            wa[j, :, 0:HW] = cut(R.wz, j, HW)
            wa[j, :, HW : 2 * HW] = cut(R.wx, j, HW)
        wb[:, 0:128] = R.wbc[...]
        wb[:, 128:384] = R.wq[...]
        wb[:, 384:512] = R.wkv[...]

        def finish(block, v):
            at = pl.ds(pl.multiple_of(block * BLK, BLK), BLK)
            R.z[at] = v[:, 0:HW]
            R.xr[at] = v[:, HW : 2 * HW]

        close_a = scatter_cols(R.a, R.p, r, c, lambda rows, j: dot_nn(rows, wa[j]), HALO, finish)
        steps = dot_nt(R.ws[...], g[pl.ds(HALO, LEN)])
        for j in range(SIDE):
            R.ps[j] = steps[16 * j : 16 * j + 8]
        step_hops = [
            hop(
                R.ps.at[flip(c, e)],
                R.pr.at[e - 1],
                R.pss.at[e - 1],
                R.psr.at[e - 1],
                col=flip(c, e),
            )
            for e in (1, 2, 3)
        ]
        for one in step_hops:
            one.start()

        def token_rows(j):
            return dot_nn(g[pl.ds(pl.multiple_of(j * BLK, BLK), BLK + 2 * HALO)], wb[...])

        close_b = scatter_tokens(R.b, c, token_rows)
        R.n1[...] = g[pl.ds(HALO, LEN)]
        R.s1[...] = total
        R.wa_o[...] = wa[...]
        R.wb_o[...] = wb[...]
        close_a()
        for one in step_hops:
            one.wait_recv()
        R.sr[...] = (R.ps[c] + R.pr[0]) + (R.pr[1] + R.pr[2])
        for one in step_hops:
            one.wait_send()
        R.br[...] = close_b()
        for one in tap_hops:
            one.wait_recv()
        R.wcs[...] = jnp.concatenate([R.taps[j, 0:4, 0:32] for j in range(SIDE)], axis=1)
        for one in tap_hops:
            one.wait_send()
        wait_rows_sent(R.p, r, HALO)

    n = BLK + 2 * HALO
    scratch = dict(
        p=rows_scratch(True),
        n=stat_scratch(),
        a=cols_scratch(2 * HW),
        b=tokens_scratch(n, 512),
        wa=pltpu.VMEM((SIDE, 512, 2 * HW), BF),
        wb=pltpu.VMEM((512, 512), BF),
        ps=pltpu.VMEM((SIDE, 8, LEN), F32),
        pr=pltpu.VMEM((3, 8, LEN), F32),
        pss=dma(3),
        psr=dma(3),
        taps=pltpu.VMEM((SIDE, 8, 128), F32),
        tss=dma(3),
        tsr=dma(3),
    )
    outs = dict(
        n1=((LEN, 512), BF),
        s1=((8, BLK), F32),
        z=((LEN, HW), F32),
        xr=((LEN, HW), F32),
        br=((n, 512), F32),
        sr=((8, LEN), F32),
        wa_o=((SIDE, 512, 2 * HW), BF),
        wb_o=((512, 512), BF),
        wcs=((4, 128), F32),
    )
    ins = dict(x=x, gain=gain, wz=wz, wx=wx, wbc=wbc, wq=wq, wkv=wkv, ws=ws, cw=cw)
    return launch(project, ins, outs, scratch, 1)


SMALL = 32


def forward_kernel(m, o, x, gain, wo, wt, wg, wu, dh):
    def forward(R):
        r, c = here()
        greet(r, c, rows=True, cols=(1, 2, 3))
        R.mc.g[c] = R.m[...]
        og = R.og
        og[c] = R.o[...]
        o_hops = trio(R.ot, c, lambda j: og.at[j])
        o_hops[0].start()
        o_hops[1].start()
        gather_cols(R.mc, r, c)
        trio_end(o_hops)

        def product(t):
            total = dot_nn(og[t], R.wt[...])
            for j in range(SIDE):
                total = total + dot_nn(col_part(R.mc, j, t)[...], R.wo[j * HW : (j + 1) * HW])
            return total

        close = scatter_rows(R.s, r, product, lambda d: wait_cols(R.mc, r, c, d))
        R.m_all[...] = R.mc.g[...]
        R.o_all[...] = og[...]
        x1 = R.x[...].astype(F32) + close()
        R.x1[...] = x1
        total = col_sum(R.n, c, row_sums(x1 * x1))
        R.s2[...] = total
        scale = to_column(lax.rsqrt(total / D + EPSILON))
        rows_at(R.p.g, r)[...] = (R.x1[...] * scale * R.gain[...]).astype(BF)
        gather_rows(R.p, r)

        def gate_up(rows, j):
            at = pl.ds(pl.multiple_of(j * BLK, BLK), BLK)
            return jnp.concatenate([dot_nn(rows, R.wg[:, at]), dot_nn(rows, R.wu[:, at])], axis=1)

        def finish(block, v):
            at = pl.ds(pl.multiple_of(block * BLK, BLK), BLK)
            gate, up = v[:, :256], v[:, 256:]
            sig = sigmoid(gate)
            act = gate * sig
            dh = R.dh[at]
            R.hid[at] = (act * up).astype(BF)
            R.dgu[at, 0:256] = (dh * up * sig * (1.0 + gate * (1.0 - sig))).astype(BF)
            R.dgu[at, 256:512] = (dh * act).astype(BF)

        close = scatter_cols(R.a, R.p, r, c, gate_up, 0, finish)
        R.n2_all[...] = R.p.g[...]
        close()
        for one in o_hops:
            one.wait_send()
        wait_cols_sent(R.mc, r, c)
        wait_rows_sent(R.p, r)

    scratch = dict(
        mc=gcols_scratch(HW),
        s=srows_scratch(),
        n=stat_scratch(),
        og=pltpu.VMEM((SIDE, BLK, 256), BF),
        ot=trio_scratch(),
        p=rows_scratch(),
        a=cols_scratch(512),
    )
    outs = dict(
        x1=((BLK, 512), F32),
        s2=((8, BLK), F32),
        m_all=((SIDE, LEN, HW), BF),
        o_all=((SIDE, BLK, 256), BF),
        n2_all=((LEN, 512), BF),
        hid=((LEN, 256), BF),
        dgu=((LEN, 512), BF),
    )
    return launch(forward, dict(m=m, o=o, x=x, gain=gain, wo=wo, wt=wt, wg=wg, wu=wu, dh=dh), outs, scratch, 3)


def norm_back(S, c, dn, v, scale, gain):
    gain_grad = jnp.sum(dn * v * scale, axis=0, keepdims=True)
    weighted = dn * gain
    total = col_sum(S, c, row_sums(weighted * v))
    inner = to_column(total)
    return scale * weighted - v * (scale * scale * scale * inner / D), gain_grad


def backward_kernel(dgu, wg, wu, x1, s2, gain, cot, n2, wo, wt):
    def backward(R):
        r, c = here()
        greet(r, c, rows=True, cols=(1, 2, 3))
        R.gc.g[c] = R.dgu[...]
        gather_cols(R.gc, r, c)

        def product(t):
            total = jnp.zeros((BLK, 512), F32)
            for j in range(SIDE):
                part = col_part(R.gc, j, t)[...]
                total = total + dot_nt(part[:, :256], R.wg[:, 256 * j : 256 * j + 256])
                total = total + dot_nt(part[:, 256:], R.wu[:, 256 * j : 256 * j + 256])
            return total

        close = scatter_rows(R.s, r, product, lambda d: wait_cols(R.gc, r, c, d))

        def grads(j, carry):
            at = pl.ds(pl.multiple_of(j * BLK, BLK), BLK)
            both = dot_tn(R.n2[...], R.gc.g[j])
            R.gate_w[:, at] = both[:, :256].astype(BF)
            R.up_w[:, at] = both[:, 256:].astype(BF)
            return carry

        lax.fori_loop(0, SIDE, grads, 0)
        dn = close()
        scale = to_column(lax.rsqrt(R.s2[...] / D + EPSILON))
        dv, dgain = norm_back(R.n, c, dn, R.x1[...], scale, R.gain[...])
        dx1 = R.cot[...] + dv
        R.dx1[...] = dx1
        R.dgain[...] = dgain
        rows_at(R.p.g, r)[...] = dx1.astype(BF)
        gather_rows(R.p, r)

        def out_back(rows, j):
            return dot_nt(rows, R.wo[pl.ds(pl.multiple_of(j * HW, 64), HW)])

        def finish(block, v):
            R.dm[pl.ds(pl.multiple_of(block * BLK, BLK), BLK)] = v

        close_a = scatter_cols(R.a, R.p, r, c, out_back, 0, finish)
        close_b = scatter_tokens(R.b, c, lambda j: dot_nt(rows_at(R.p.g, j)[...], R.wt[...]))
        R.dx_all[...] = R.p.g[...]
        close_a()
        R.do[...] = close_b().astype(BF)
        wait_cols_sent(R.gc, r, c)
        wait_rows_sent(R.p, r)

    scratch = dict(
        gc=gcols_scratch(512),
        s=srows_scratch(),
        n=stat_scratch(),
        p=rows_scratch(),
        a=cols_scratch(HW),
        b=tokens_scratch(BLK, 256, low=BF),
    )
    outs = dict(
        gate_w=((512, 1024), BF),
        up_w=((512, 1024), BF),
        dx1=((BLK, 512), F32),
        dgain=((1, 512), F32),
        dx_all=((LEN, 512), BF),
        dm=((LEN, HW), F32),
        do=((BLK, 256), BF),
    )
    ins = dict(dgu=dgu, wg=wg, wu=wu, x1=x1, s2=s2, gain=gain, cot=cot, n2=n2, wo=wo, wt=wt)
    return launch(backward, ins, outs, scratch, 6)


def project_back_kernel(da, db, ds, wa, wb, ws, x, s1, gain, dx1, n1, ffn_grad, dconv, dgain, dhead, dstates):
    pair = lax.axis_size("dp") == 2

    def project_back(R):
        r, c = here()
        greet(r, c, rows=True, cols=(1, 2, 3), dp=pair)
        R.ac.g[c] = R.da[...]
        bg, sg, tg = R.bg, R.sg, R.tg
        bg[c] = R.db[...]
        sg[c] = R.ds[...]
        tg[c] = jnp.zeros((8, 128), F32)
        tg[c, 0:4] = R.dstates[...]
        b_hops = trio(R.bt, c, lambda j: bg.at[j])
        s_hops = []
        for e in (1, 2, 3):
            to = flip(c, e)
            s_hops.append(hop(sg.at[c], sg.at[c], R.sgs.at[e - 1], R.sgr.at[e - 1], col=to))
            s_hops.append(hop(tg.at[c], tg.at[c], R.tgs.at[e - 1], R.tgr.at[e - 1], col=to))
        b_hops[0].start()
        b_hops[1].start()
        for one in s_hops:
            one.start()
        gather_cols(R.ac, r, c)

        peer = 1 - lax.axis_index("dp")
        owns, theirs = (R.bw, R.sw, R.zw, R.xw), (R.bp, R.sp, R.zp, R.xp)
        w_hops = [hop(a, b, R.wss.at[k], R.wsr.at[k], dp=peer) for k, (a, b) in enumerate(zip(owns, theirs))]
        small_hop = hop(R.small, R.small_p, R.mss, R.msr, dp=peer)

        trio_end(b_hops)
        for one in s_hops:
            one.wait_recv()
        R.bw[...] = dot_tn(R.n1[...], bg[...].reshape(LEN, 512)).astype(BF)
        R.sw[...] = dot_nn(sg[...].reshape(16 * SIDE, LEN), R.n1[...]).astype(BF)
        if pair:
            w_hops[0].start()
            w_hops[1].start()

        def product(t):
            total = dot_nt(bg[t], R.wb[...])
            at = pl.ds(pl.multiple_of(t * BLK, BLK), BLK)
            for j in range(SIDE):
                total = total + dot_nt(col_part(R.ac, j, t)[...], R.wa[j])
                total = total + dot_tn(sg[j, :, at], R.ws[16 * j : 16 * j + 16])
            return total

        close = scatter_rows(R.s, r, product, lambda d: wait_cols(R.ac, r, c, d))
        for j in range(SIDE):
            both = dot_tn(R.n1[...], R.ac.g[j]).astype(BF)
            R.zw[:, j * HW : (j + 1) * HW] = both[:, :HW]
            R.xw[:, j * HW : (j + 1) * HW] = both[:, HW:]
        if pair:
            w_hops[2].start()
            w_hops[3].start()
        dn = close()
        scale = to_column(lax.rsqrt(R.s1[...] / D + EPSILON))
        dv, mixer_grad = norm_back(R.n, c, dn, R.x[...].astype(F32), scale, R.gain[...])
        gg = R.gg
        gg[r] = jnp.zeros((8, 512), F32)
        gg[r, 0:1] = mixer_grad
        gg[r, 1:2] = R.ffn_grad[...]
        g_hops = [hop(gg.at[r], gg.at[r], R.ggs.at[d - 1], R.ggr.at[d - 1], row=flip(r, d)) for d in (1, 2, 3)]
        for one in g_hops:
            one.start()
        R.dx[...] = R.dx1[...] + dv
        small = R.small
        small[...] = jnp.zeros((SMALL, 512), F32)
        small[8:12, 0:HW] = R.dconv[...]
        small[12:13, 0:HW] = R.dgain[...]
        small[16:24, 0:128] = R.dhead[...]
        small[24:32, 0:128] = (tg[0] + tg[1]) + (tg[2] + tg[3])
        for one in g_hops:
            one.wait_recv()
        small[0:8] = (gg[0] + gg[1]) + (gg[2] + gg[3])
        if pair:
            small_hop.start()
        for one in (*b_hops, *s_hops, *g_hops):
            one.wait_send()
        wait_cols_sent(R.ac, r, c)
        if pair:
            small_hop.wait_recv()
            R.total[...] = small[...] + R.small_p[...]
            small_hop.wait_send()
        else:
            R.total[...] = small[...]
        for own, their, one, out_own, out_their in zip(
            owns, theirs, w_hops, (R.bo, R.so, R.zo, R.xo), (R.bq, R.sq, R.zq, R.xq)
        ):
            out_own[...] = own[...]
            if pair:
                one.wait_recv()
                out_their[...] = their[...]
                one.wait_send()
            else:
                out_their[...] = jnp.zeros_like(out_their)

    low = dict(b=((512, 512), BF), s=((16 * SIDE, 512), BF), z=((512, 768), BF), x=((512, 768), BF))
    scratch = dict(
        ac=gcols_scratch(2 * HW),
        s=srows_scratch(),
        n=stat_scratch(),
        bt=trio_scratch(),
        bg=pltpu.VMEM((SIDE, BLK, 512), BF),
        sg=pltpu.VMEM((SIDE, 16, LEN), BF),
        sgs=dma(3),
        sgr=dma(3),
        tg=pltpu.VMEM((SIDE, 8, 128), F32),
        tgs=dma(3),
        tgr=dma(3),
        gg=pltpu.VMEM((SIDE, 8, 512), F32),
        ggs=dma(3),
        ggr=dma(3),
        bw=pltpu.VMEM(*low["b"]),
        bp=pltpu.VMEM(*low["b"]),
        sw=pltpu.VMEM(*low["s"]),
        sp=pltpu.VMEM(*low["s"]),
        zw=pltpu.VMEM(*low["z"]),
        zp=pltpu.VMEM(*low["z"]),
        xw=pltpu.VMEM(*low["x"]),
        xp=pltpu.VMEM(*low["x"]),
        wss=dma(4),
        wsr=dma(4),
        small=pltpu.VMEM((SMALL, 512), F32),
        small_p=pltpu.VMEM((SMALL, 512), F32),
        mss=dma(),
        msr=dma(),
    )
    outs = dict(
        dx=((BLK, 512), F32),
        total=((SMALL, 512), F32),
        bo=low["b"],
        bq=low["b"],
        so=low["s"],
        sq=low["s"],
        zo=low["z"],
        zq=low["z"],
        xo=low["x"],
        xq=low["x"],
    )
    ins = dict(da=da, db=db, ds=ds, wa=wa, wb=wb, ws=ws, x=x, s1=s1, gain=gain, dx1=dx1, n1=n1)
    ins.update(ffn_grad=ffn_grad, dconv=dconv, dgain=dgain, dhead=dhead, dstates=dstates)
    return launch(project_back, ins, outs, scratch, 8)


def per_head(values):
    lane = iota((1, HW), 1)
    first = jnp.where(lane < HDIM, values[0], values[1])
    return jnp.where(lane < 2 * HDIM, first, values[2])


def head_select():
    return jnp.where(iota((8, HW), 1) // HDIM == iota((8, HW), 0), 1.0, 0.0).astype(F32)


def scalar_rows(ref):
    sub = iota((8, 1), 0)
    return jnp.where(sub == 0, ref[0], jnp.where(sub == 1, ref[1], jnp.where(sub == 2, ref[2], 0.0)))


def triangle():
    return jnp.where(iota((BLK, BLK), 0) <= iota((BLK, BLK), 1), 1.0, 0.0).astype(F32)


def fill_padded(R):
    R.xpad[0:8] = jnp.zeros((8, HW), F32)
    R.xpad[8 : 8 + LEN] = R.xr[...]


def conv_block(R, b):
    start = pl.multiple_of(b * BLK, BLK)
    chunk = R.xpad[pl.ds(start, BLK + 8)]
    taps = [chunk[5 + j : 5 + j + BLK] for j in range(4)]
    pre = taps[0] * R.wc[0:1]
    for j in (1, 2, 3):
        pre = pre + taps[j] * R.wc[j : j + 1]
    return pre, taps


def step_block(R, b):
    at = pl.ds(pl.multiple_of(b * BLK, BLK), BLK)
    raw = R.sr[:, at] + scalar_rows(R.bias)
    dt = softplus(raw)
    rate = -dt * jnp.exp(scalar_rows(R.decay))
    within = dot_nn(rate, triangle(), HIGHEST)
    return raw, dt, rate, within, jnp.transpose(dt), jnp.transpose(within)


def rope_turn(v, cosine, sine):
    return v * cosine + pltpu.roll(v, ADIM // 2, axis=1) * sine


def rope_tables():
    half = ADIM // 2
    freqs = np.float32(ROPE_BASE) ** (-np.arange(half, dtype=np.float32) / np.float32(half))
    angles = np.arange(LEN, dtype=np.float32)[:, None] * freqs.astype(np.float32)
    angles = angles.astype(np.float32).astype(np.float64)
    cosine, sine = np.cos(angles), np.sin(angles)
    return (
        np.concatenate([cosine, cosine], axis=1).astype(np.float32),
        np.concatenate([-sine, sine], axis=1).astype(np.float32),
    )


def key_scores(q, keys, c):
    s = dot_nt(q, keys) * SCALE
    return jnp.where(iota(s.shape, 1) <= c * BLK + iota(s.shape, 0), s, NEGATIVE)


def state_cols(R, kind, b):
    g = R.g
    return jnp.concatenate([g[2 * kind, b], g[2 * kind + 1, b]], axis=1).astype(F32)


def lower_decay(within_c, within_r, h):
    gaps = within_c[:, h : h + 1] - within_r[h : h + 1]
    return jnp.exp(jnp.where(iota((BLK, BLK), 1) <= iota((BLK, BLK), 0), gaps, NEGATIVE))


def head_mask(v, h):
    return jnp.where(iota((1, HW), 1) // HDIM == h, v, jnp.zeros_like(v))


def column_heads(cols):
    return per_head([cols[:, h : h + 1] for h in range(HH)])


def mixers_kernel(z, xr, br, sr, wc, wcs, bias, decay, skip, gain, cosine, sine, cot, wd):
    def mixers(R):
        r, c = here()
        greet(r, c, grid=True)
        g = R.g
        br = R.br
        pre = br[13 : 13 + BLK, 0:128] * R.wcs[0:1]
        for j in (1, 2, 3):
            pre = pre + br[13 + j : 13 + j + BLK, 0:128] * R.wcs[j : j + 1]
        g[r, c] = (pre * sigmoid(pre)).astype(BF)
        at = pl.ds(pl.multiple_of(c * BLK, BLK), BLK)
        cos, sin = R.cos[at], R.sin[at]
        kv = br[HALO : HALO + BLK, 384:512].astype(BF)
        turned = rope_turn(kv.astype(F32), cos, sin).astype(BF)
        kind, head = lax.div(r, 2), lax.rem(r, 2)
        kvb = R.kvb
        kvb[...] = jnp.where(kind == 0, turned, kv)
        slot = SIDE + kind

        @pl.when(head == kind)
        def _():
            g[slot, c] = kvb[...]

        def bc_hop(d):
            return hop(g.at[r, c], g.at[r, c], R.zs.at[d - 1], R.zr.at[d - 1], row=flip(r, d))

        def kv_hop(d):
            return hop(kvb, g.at[slot, c], R.ys.at[d - 1], R.yr.at[d - 1], row=flip(r, d))

        for d in (1, 2, 3):
            bc_hop(d).start()

            @pl.when(lax.div(flip(r, d), 2) == head)
            def _():
                kv_hop(d).start()

        rows_at(R.p.g, r)[...] = R.cot[...].astype(BF)
        gather_rows(R.p, r)
        fill_padded(R)
        for d in (1, 2, 3):
            bc_hop(d).wait_recv()

            @pl.when(lax.rem(flip(r, d), 2) == kind)
            def _():
                kv_hop(d).wait_recv()

        g_hops = trio(R.gt, c, lambda j: g.at[:, j])
        g_hops[0].start()
        g_hops[1].start()
        for h in range(2):
            q = br[HALO : HALO + BLK, 128 + 128 * h : 256 + 128 * h].astype(BF).astype(F32)
            R.qr[h] = rope_turn(q, cos, sin).astype(BF)
        trio_end(g_hops)

        state = R.state
        state[...] = jnp.zeros_like(state)
        st = R.n.st
        st[r, c] = jnp.zeros((8, BLK), F32)
        skip_row = per_head([R.skip[h] for h in range(HH)])

        def block(b, carry):
            at = pl.ds(pl.multiple_of(b * BLK, BLK), BLK)
            pre, _ = conv_block(R, b)
            u = pre * sigmoid(pre)
            _, _, _, within, dt_c, within_c = step_block(R, b)
            bb, cb = state_cols(R, 0, b), state_cols(R, 1, b)
            x = u * column_heads(dt_c)
            xb = x
            scores = dot_nt(cb, bb, HIGHEST)
            y = jnp.exp(column_heads(within_c)) * dot_nn(cb, state[...], HIGHEST)
            for h in range(HH):
                a = (scores * lower_decay(within_c, within, h))
                y = y + dot_nn(a, head_mask(xb, h), HIGHEST)
            last = per_head([within[h : h + 1, BLK - 1 : BLK] for h in range(HH)])
            keep = jnp.exp(last - column_heads(within_c))
            R.states[b] = state[...]
            state[...] = state[...] * jnp.exp(last) + dot_tn(bb, (x * keep), HIGHEST)
            y = y + skip_row * u
            zb = R.z[at]
            gated = y * zb * sigmoid(zb)
            R.y[at] = y
            R.gs[at] = gated
            sums = row_sums(gated * gated)
            st[r, c] = jnp.where(iota((8, BLK), 0) == b, sums, st[r, c])
            return carry

        lax.fori_loop(0, SIDE, block, 0)
        close = grid_sum(R.n, r, c)

        def hidden_back(rows, j):
            return dot_nt(rows, R.wd[pl.ds(pl.multiple_of(j * BLK, BLK), BLK)])

        def finish(block, v):
            R.dh[pl.ds(pl.multiple_of(block * BLK, BLK), BLK)] = v

        close_h = scatter_cols(R.a, R.p, r, c, hidden_back, 0, finish, True)
        keys = g[4].reshape(LEN, ADIM)
        values = g[5].reshape(LEN, ADIM)
        for h in range(2):
            s = key_scores(R.qr[h], keys, c)
            top = jnp.max(s, axis=1, keepdims=True)
            lse = top + jnp.log(jnp.sum(jnp.exp(s - top), axis=1, keepdims=True))
            R.lse[h] = jnp.broadcast_to(lse, (BLK, 128))
            probs = jnp.exp(s - lse).astype(BF)
            R.o[:, 128 * h : 128 * h + 128] = dot_nn(probs, values).astype(BF)

        total = close()
        R.s3[...] = total
        scales = jnp.transpose(lax.rsqrt(total / (HEADS * HDIM) + EPSILON))

        def scaled(b, carry):
            at = pl.ds(pl.multiple_of(b * BLK, BLK), BLK)
            R.m[at] = (R.gs[at] * pick_column(scales, b) * R.gain[...]).astype(BF)
            return carry

        lax.fori_loop(0, SIDE, scaled, 0)
        R.g_o[...] = g[...]
        R.dy[...] = R.p.g[...]
        close_h()
        wait_rows_sent(R.p, r)
        for d in (1, 2, 3):
            bc_hop(d).wait_send()

            @pl.when(lax.div(flip(r, d), 2) == head)
            def _():
                kv_hop(d).wait_send()

        for one in g_hops:
            one.wait_send()

    scratch = dict(
        n=grid_scratch(),
        p=rows_scratch(),
        a=cols_scratch(256),
        g=pltpu.VMEM((6, SIDE, BLK, 128), BF),
        kvb=pltpu.VMEM((BLK, 128), BF),
        xpad=pltpu.VMEM((LEN + 8, HW), F32),
        gs=pltpu.VMEM((LEN, HW), F32),
        state=pltpu.VMEM((STATE, HW), F32),
        zs=dma(3),
        zr=dma(3),
        ys=dma(3),
        yr=dma(3),
        gt=trio_scratch(),
    )
    outs = dict(
        m=((LEN, HW), BF),
        o=((BLK, 256), BF),
        y=((LEN, HW), F32),
        s3=((8, BLK), F32),
        lse=((2, BLK, 128), F32),
        states=((SIDE, STATE, HW), F32),
        g_o=((6, SIDE, BLK, 128), BF),
        qr=((2, BLK, 128), BF),
        dy=((LEN, 512), BF),
        dh=((LEN, 256), F32),
    )
    ins = dict(z=z, xr=xr, br=br, sr=sr, wc=wc, wcs=wcs, gain=gain, cos=cosine, sin=sine, cot=cot, wd=wd)
    return launch(mixers, ins, outs, scratch, 9, dict(bias=bias, decay=decay, skip=skip))


def mixers_back_kernel(
    dm, do, z, xr, br, sr, y, s3, states, g, qr, lse, wc, wcs, bias, decay, skip, gain, cosine, sine, hid, wd, x1, dy, m, o, dx
):
    n = BLK + HALO

    def mixers_back(R):
        r, c = here()
        greet(r, c, grid=True)
        R.hc.g[c] = R.hid[...]
        gather_cols(R.hc, r, c)
        g = R.g
        fill_padded(R)
        st = R.n.st
        st[r, c] = jnp.zeros((8, BLK), F32)
        gain = R.gain[...]

        def inner(b, carry):
            at = pl.ds(pl.multiple_of(b * BLK, BLK), BLK)
            zb = R.z[at]
            sums = row_sums(R.dm[at] * gain * R.y[at] * zb * sigmoid(zb))
            st[r, c] = jnp.where(iota((8, BLK), 0) == b, sums, st[r, c])
            return carry

        lax.fori_loop(0, SIDE, inner, 0)
        close = grid_sum(R.n, r, c)

        tb = R.tb
        tb[:, pl.ds(LEN, HALO)] = jnp.zeros((6, HALO, 128), F32)
        keys = g[4].reshape(LEN, ADIM)
        values = g[5].reshape(LEN, ADIM)
        at = pl.ds(pl.multiple_of(c * BLK, BLK), BLK)
        cos, sin = R.cos[at], R.sin[at]
        for h in range(2):
            q = R.qr[h]
            dob = R.do[:, 128 * h : 128 * h + 128]
            p = jnp.exp(key_scores(q, keys, c) - R.lse[h][:, :1])
            dv = dot_tn(p.astype(BF), dob)
            dp = dot_nt(dob, values)
            ds = (p * (dp - jnp.sum(dp * p, axis=1, keepdims=True)) * SCALE).astype(BF)
            dk = dot_tn(ds, q)
            if h == 0:
                tb[4, 0:LEN] = dk
                tb[5, 0:LEN] = dv
            else:
                tb[4, 0:LEN] = tb[4, 0:LEN] + dk
                tb[5, 0:LEN] = tb[5, 0:LEN] + dv
            dq = dot_nn(ds, keys)
            R.db[:, 128 + 128 * h : 256 + 128 * h] = rope_turn(dq, cos, -sin).astype(BF)

        scales = jnp.transpose(lax.rsqrt(R.s3[...] / (HEADS * HDIM) + EPSILON))
        inners = jnp.transpose(close())

        def down(t):
            total = dot_nn(col_part(R.hc, 0, t)[...], R.wd[0:256])
            for j in (1, 2, 3):
                total = total + dot_nn(col_part(R.hc, j, t)[...], R.wd[256 * j : 256 * j + 256])
            return total

        close_d = scatter_rows(R.s, r, down, lambda d: wait_cols(R.hc, r, c, d))
        dstate, dpre_pad = R.dstate, R.dpre
        dstate[...] = jnp.zeros_like(dstate)
        dpre_pad[LEN : LEN + 8] = jnp.zeros((8, HW), F32)
        select = head_select()
        skip_row = per_head([R.skip[h] for h in range(HH)])
        rate_of = jnp.exp(scalar_rows(R.decay))
        for ref in (R.dgain, R.dskip, R.dconv, R.dhead, R.ds):
            ref[...] = jnp.zeros_like(ref)
        upto = jnp.where(iota((BLK, BLK), 0) >= iota((BLK, BLK), 1), 1.0, 0.0).astype(F32)

        def block(i, carry):
            b = 3 - i
            at = pl.ds(pl.multiple_of(b * BLK, BLK), BLK)
            pre, taps = conv_block(R, b)
            sig = sigmoid(pre)
            u = pre * sig
            raw, dt, rate, within, dt_c, within_c = step_block(R, b)
            bb, cb = state_cols(R, 0, b), state_cols(R, 1, b)
            zb, yb, dm = R.z[at], R.y[at], R.dm[at]
            zsig = sigmoid(zb)
            zact = zb * zsig
            gated = yb * zact
            scale = pick_column(scales, b)
            dgated = scale * dm * gain - gated * (scale * scale * scale * pick_column(inners, b) / (HEADS * HDIM))
            R.dgain[...] += jnp.sum(dm * gated * scale, axis=0, keepdims=True)
            dy = dgated * zact
            R.da[at, 0:HW] = (dgated * yb * zsig * (1.0 + zb * (1.0 - zsig))).astype(BF)
            R.dskip[...] += jnp.sum(dy * u, axis=0, keepdims=True)
            dyb = dy
            dyr = dyb.astype(F32)
            wide = column_heads(within_c)
            grow = jnp.exp(wide)
            last = per_head([within[h : h + 1, BLK - 1 : BLK] for h in range(HH)])
            keep = jnp.exp(last - wide)
            dt_w = column_heads(dt_c)
            x = u * dt_w
            xb = x
            scores = dot_nt(cb, bb, HIGHEST)
            state = R.states[b]
            stb = state
            yin = jnp.zeros((BLK, HW), F32)
            dx = jnp.zeros((BLK, HW), F32)
            dscores = jnp.zeros((BLK, BLK), F32)
            for h in range(HH):
                decay_h = lower_decay(within_c, within, h)
                a = (scores * decay_h)
                xh = head_mask(xb, h)
                yin = yin + dot_nn(a, xh, HIGHEST)
                dx = dx + dot_tn(a, head_mask(dyb, h), HIGHEST)
                dscores = dscores + dot_nt(dyb, xh, HIGHEST) * decay_h
            dsb = dscores
            dyg = dyr * grow
            dygb = dyg
            xk = x * keep
            dst = dstate[...]
            dstb = dst
            dc = dot_nn(dsb, bb, HIGHEST) + dot_nt(dygb, stb, HIGHEST)
            db = dot_tn(dsb, cb, HIGHEST) + dot_nt(xk, dstb, HIGHEST)
            tb[0, at] = db[:, :128]
            tb[1, at] = db[:, 128:]
            tb[2, at] = dc[:, :128]
            tb[3, at] = dc[:, 128:]
            dxk = dot_nn(bb, dstb, HIGHEST)
            carried = dxk * xk
            turn = dyr * yin - xb.astype(F32) * dx + dyg * dot_nn(cb, stb, HIGHEST) - carried
            dx = dx + dxk * keep
            elast = jnp.exp(last)
            ends = jnp.sum(carried, axis=0, keepdims=True) + jnp.sum(dst * state, axis=0, keepdims=True) * elast
            dlast = dot_nt(select, jnp.broadcast_to(ends, (8, HW)), HIGHEST)[:, :1]
            drate = dot_nn(dot_nt(select, turn, HIGHEST), upto, HIGHEST) + dlast
            ddt = dot_nt(select, dx * u, HIGHEST) - drate * rate_of
            draw = ddt * sigmoid(raw)
            R.ds[0:8, at] = draw.astype(BF)
            lane = iota((8, 128), 1)
            R.dhead[...] += jnp.where(
                lane == 0,
                jnp.sum(draw, axis=1, keepdims=True),
                jnp.where(lane == 1, jnp.sum(drate * rate, axis=1, keepdims=True), 0.0),
            )
            dstate[...] = dst * elast + dot_tn(cb, dygb, HIGHEST)
            du = dx * dt_w + dy * skip_row
            dpre = du * sig * (1.0 + pre * (1.0 - sig))
            dpre_pad[at] = dpre
            for j in range(4):
                R.dconv[j : j + 1] += jnp.sum(dpre * taps[j], axis=0, keepdims=True)
            chunk = dpre_pad[pl.ds(pl.multiple_of(b * BLK, BLK), BLK + 8)]
            dxr = chunk[3 : 3 + BLK] * R.wc[0:1]
            for j in (1, 2, 3):
                dxr = dxr + chunk[3 - j : 3 - j + BLK] * R.wc[j : j + 1]
            R.da[at, HW : 2 * HW] = dxr.astype(BF)
            return carry

        lax.fori_loop(0, SIDE, block, 0)
        R.dhead[...] += jnp.where(
            iota((8, 128), 1) == 2,
            dot_nt(select, jnp.broadcast_to(R.dskip[...], (8, HW)), HIGHEST)[:, :1],
            0.0,
        )

        def token_rows(j):
            return tb[:, pl.ds(pl.multiple_of(j * BLK, BLK), n)]

        close_t = scatter_tokens(R.t, c, token_rows)
        for j in range(SIDE):
            R.down_w[256 * j : 256 * j + 256] = dot_tn(R.hc.g[j], R.dy[...]).astype(BF)
        total = close_t()
        tob = R.tob
        tob[...] = total.astype(BF)
        mine = R.mine
        mine[...] = total
        kind, head = lax.div(r, 2), lax.rem(r, 2)

        def bc_hop(d):
            return hop(tob.at[flip(r, d)], R.zbr.at[d - 1], R.zs.at[d - 1], R.zr.at[d - 1], row=flip(r, d))

        def kv_hop(d):
            to = flip(r, d)
            return hop(
                tob.at[SIDE + lax.div(to, 2), pl.ds(0, BLK)],
                R.zkr.at[d - 1],
                R.ys.at[d - 1],
                R.yr.at[d - 1],
                row=to,
            )

        for d in (1, 2, 3):
            bc_hop(d).start()

            @pl.when(lax.rem(flip(r, d), 2) == kind)
            def _():
                kv_hop(d).start()

        for j in range(SIDE):
            R.out_w[HW * j : HW * j + HW] = dot_tn(R.m[j], R.dx[...]).astype(BF)
        R.attn_w[...] = dot_tn(R.o[...].reshape(LEN, 256), R.dx[...]).astype(BF)
        dpost = mine[r]
        dkv = R.dkv
        dkv[...] = jnp.zeros_like(dkv)

        @pl.when(head == kind)
        def _():
            dkv[...] = mine[SIDE + kind, 0:BLK]

        for d in (1, 2, 3):
            bc_hop(d).wait_recv()
            dpost = dpost + R.zbr[d - 1].astype(F32)

            @pl.when(lax.div(flip(r, d), 2) == head)
            def _():
                kv_hop(d).wait_recv()
                dkv[...] = dkv[...] + R.zkr[d - 1].astype(F32)

        br = R.br
        pre = br[13 : 13 + n, 0:128] * R.wcs[0:1]
        for j in (1, 2, 3):
            pre = pre + br[13 + j : 13 + j + n, 0:128] * R.wcs[j : j + 1]
        sig = sigmoid(pre)
        dpre = dpost * sig * (1.0 + pre * (1.0 - sig))
        dbc = dpre[3 : 3 + BLK] * R.wcs[0:1]
        for j in (1, 2, 3):
            dbc = dbc + dpre[3 - j : 3 - j + BLK] * R.wcs[j : j + 1]
        R.db[:, 0:128] = dbc.astype(BF)
        for j in range(4):
            R.dstates[j : j + 1] = jnp.sum(dpre[0:BLK] * br[13 + j : 13 + j + BLK, 0:128], axis=0, keepdims=True)
        R.out[...] = (R.x1[...] + close_d()).astype(BF)
        wait_cols_sent(R.hc, r, c)
        dkv_v = dkv[...]
        R.db[:, 384:512] = jnp.where(kind == 0, rope_turn(dkv_v, cos, -sin), dkv_v).astype(BF)
        for d in (1, 2, 3):
            bc_hop(d).wait_send()

            @pl.when(lax.rem(flip(r, d), 2) == kind)
            def _():
                kv_hop(d).wait_send()

    scratch = dict(
        n=grid_scratch(),
        hc=gcols_scratch(256),
        s=srows_scratch(),
        t=tokens_scratch(6, n, 128, low=BF),
        xpad=pltpu.VMEM((LEN + 8, HW), F32),
        dpre=pltpu.VMEM((LEN + 8, HW), F32),
        dstate=pltpu.VMEM((STATE, HW), F32),
        dskip=pltpu.VMEM((1, HW), F32),
        tb=pltpu.VMEM((6, LEN + HALO, 128), F32),
        tob=pltpu.VMEM((6, n, 128), BF),
        mine=pltpu.VMEM((6, n, 128), F32),
        dkv=pltpu.VMEM((BLK, 128), F32),
        zbr=pltpu.VMEM((3, n, 128), BF),
        zkr=pltpu.VMEM((3, BLK, 128), BF),
        zs=dma(3),
        zr=dma(3),
        ys=dma(3),
        yr=dma(3),
    )
    outs = dict(
        da=((LEN, 2 * HW), BF),
        db=((BLK, 512), BF),
        ds=((16, LEN), BF),
        dgain=((1, HW), F32),
        dconv=((4, HW), F32),
        dstates=((4, 128), F32),
        dhead=((8, 128), F32),
        out=((BLK, 512), BF),
        down_w=((LEN, 512), BF),
        out_w=((SIDE * HW, 512), BF),
        attn_w=((256, 512), BF),
    )
    ins = dict(dm=dm, do=do, z=z, xr=xr, br=br, sr=sr, y=y, s3=s3, states=states, g=g, qr=qr, lse=lse, wc=wc, wcs=wcs)
    ins.update(gain=gain, cos=cosine, sin=sine, hid=hid, wd=wd, x1=x1, dy=dy, m=m, o=o, dx=dx)
    return launch(mixers_back, ins, outs, scratch, 10, dict(bias=bias, decay=decay, skip=skip))


def dp_total(parts):
    if lax.axis_size("dp") == 2:
        peers = [lax.ppermute(p, "dp", ((0, 1), (1, 0))) for p in parts]
        return [p.astype(F32) + q.astype(F32) for p, q in zip(parts, peers)]
    return list(lax.psum(tuple(p.astype(F32) for p in parts), "dp"))


def on_device(
    block_input,
    mixer_gain,
    ssm_gate_weight,
    ssm_input_weight,
    ssm_bc_weight,
    ssm_step_weight,
    query_weight,
    keyval_weight,
    conv_input,
    conv_states,
    step_bias,
    decay_log,
    skip_gain,
    ssm_norm_gain,
    ssm_out_weight,
    attn_out_weight,
    ffn_gain,
    gate_up_weight,
    down_weight,
    cotangent,
):
    cosine, sine = (jnp.asarray(table) for table in rope_tables())
    step_w = jnp.pad(ssm_step_weight.T.reshape(SIDE, HH, -1), ((0, 0), (0, 16 - HH), (0, 0))).reshape(16 * SIDE, -1)
    wg, wu = gate_up_weight[:, 0], gate_up_weight[:, 1]
    mixer_row, ffn_row, ssm_row = mixer_gain[None], ffn_gain[None], ssm_norm_gain[None]
    wo, wt, wd = ssm_out_weight, attn_out_weight, down_weight

    p = project_kernel(
        block_input,
        mixer_row,
        ssm_gate_weight,
        ssm_input_weight,
        ssm_bc_weight,
        query_weight,
        keyval_weight,
        step_w,
        conv_states,
    )
    heads = (conv_input, p.wcs, step_bias, decay_log, skip_gain, ssm_row, cosine, sine)
    m = mixers_kernel(p.z, p.xr, p.br, p.sr, *heads, cotangent, wd)
    f = forward_kernel(m.m, m.o, block_input, ffn_row, wo, wt, wg, wu, m.dh)
    b = backward_kernel(f.dgu, wg, wu, f.x1, f.s2, ffn_row, cotangent, f.n2_all, wo, wt)
    gate_grad, up_grad = dp_total([b.gate_w, b.up_w])
    mixed = (p.z, p.xr, p.br, p.sr, m.y, m.s3, m.states, m.g_o, m.qr, m.lse)
    k = mixers_back_kernel(b.dm, b.do, *mixed, *heads, f.hid, wd, f.x1, m.dy, f.m_all, f.o_all, b.dx_all)
    down_grad, out_grad, attn_grad = dp_total([k.down_w, k.out_w, k.attn_w])
    q = project_back_kernel(
        k.da,
        k.db,
        k.ds,
        p.wa_o,
        p.wb_o,
        step_w,
        block_input,
        p.s1,
        mixer_row,
        b.dx1,
        p.n1,
        b.dgain,
        k.dconv,
        k.dgain,
        k.dhead,
        k.dstates,
    )
    pairs = ((q.zo, q.zq), (q.xo, q.xq), (q.bo, q.bq), (q.so, q.sq))
    sums = [own.astype(F32) + their.astype(F32) for own, their in pairs]
    total = q.total
    if lax.axis_size("dp") != 2:
        sums, total = lax.psum((sums, total), "dp")
    z_grad, x_grad, b_grad, step_grad = sums
    step_grad = step_grad.reshape(SIDE, 16, -1)[:, :HH].reshape(SIDE * HH, -1).T
    states_grad = lax.dynamic_slice(total, (24, lax.axis_index("col") * 32), (4, 32))
    return (
        k.out,
        q.dx,
        total[0],
        z_grad,
        x_grad,
        b_grad[:, 0:128],
        step_grad,
        b_grad[:, 128:384],
        b_grad[:, 384:512],
        total[8:12, 0:HW],
        states_grad,
        total[16 : 16 + HH, 0],
        total[16 : 16 + HH, 1],
        total[16 : 16 + HH, 2],
        total[12, 0:HW],
        out_grad,
        attn_grad,
        total[1],
        jnp.stack([gate_grad, up_grad], axis=1),
        down_grad,
    )


def solution(mesh):
    placed = (
        P(("dp", "row"), "col"),
        P("col"),
        P("col", "row"),
        P("col", "row"),
        P("col", "row"),
        P("col", "row"),
        P("col", "row"),
        P("col", "row"),
        P(None, ("row", "col")),
        P(None, ("row", "col")),
        P(("row", "col")),
        P(("row", "col")),
        P(("row", "col")),
        P(("row", "col")),
        P("row", "col"),
        P("row", "col"),
        P("col"),
        P("col", None, "row"),
        P("row", "col"),
        P(("dp", "row"), "col"),
    )
    return jax.shard_map(
        on_device,
        mesh=mesh,
        in_specs=placed,
        out_specs=(
            P(("dp", "row"), "col"),
            P(("dp", "row"), "col"),
            P("col"),
            P("col", "row"),
            P("col", "row"),
            P("col", "row"),
            P("col", "row"),
            P("col", "row"),
            P("col", "row"),
            P(None, ("row", "col")),
            P(None, ("row", "col")),
            P(("row", "col")),
            P(("row", "col")),
            P(("row", "col")),
            P(("row", "col")),
            P("row", "col"),
            P("row", "col"),
            P("col"),
            P("col", None, "row"),
            P("row", "col"),
        ),
        check_vma=False,
    )
```

```python
import types

import jax
import jax.numpy as jnp
import numpy as np
from jax import lax
from jax.experimental import pallas as pl
from jax.experimental.pallas import tpu as pltpu
from jax.sharding import PartitionSpec as P

D = 2048
HEADS = 48
HDIM = 64
STATE = 256
ADIM = 128
LEN = 1024
SPAN = 256
SIDE = 4
BLK = LEN // SIDE
HALO = 16
HH = 3
HW = HH * HDIM
EPSILON = 1e-05
ROPE_BASE = 100000000000.0
HIGHEST = lax.Precision.HIGHEST
NEGATIVE = -1e30
LETTERS = "abcd"
BF = jnp.bfloat16
F32 = jnp.float32
MESH = pl.DeviceIdType.MESH
SCALE = ADIM ** (-0.5)


def dot_nn(a, b, precision=None):
    return lax.dot_general(a, b, (((1,), (0,)), ((), ())), precision=precision, preferred_element_type=F32)


def dot_nt(a, b, precision=None):
    return lax.dot_general(a, b, (((1,), (1,)), ((), ())), precision=precision, preferred_element_type=F32)


def dot_tn(a, b, precision=None):
    return lax.dot_general(a, b, (((0,), (0,)), ((), ())), precision=precision, preferred_element_type=F32)


def halves(v):
    high = v.astype(BF)
    return high, (v - high.astype(F32)).astype(BF)


def fine(dot, a, b):
    a = a if isinstance(a, tuple) else (a,)
    b = b if isinstance(b, tuple) else (b,)
    total = dot(a[0], b[0])
    if len(b) > 1:
        total = total + dot(a[0], b[1])
    if len(a) > 1:
        total = total + dot(a[1], b[0])
    return total


def sigmoid(v):
    return 1.0 / (1.0 + jnp.exp(-v))


def softplus(v):
    return jnp.maximum(v, 0.0) + jnp.log1p(jnp.exp(-jnp.abs(v)))


def iota(shape, axis):
    return lax.broadcasted_iota(jnp.int32, shape, axis)


def flip(v, d):
    v0, v1 = lax.rem(v, 2), lax.div(v, 2)
    if isinstance(d, int):
        d0, d1 = d % 2, d // 2
    else:
        d0, d1 = lax.rem(d, 2), lax.div(d, 2)
    return 2 * (v1 + d1 - 2 * v1 * d1) + (v0 + d0 - 2 * v0 * d0)


def here():
    return lax.axis_index("row"), lax.axis_index("col")


def greet(r, c, rows=False, cols=(), grid=False, dp=False):
    sem = pltpu.get_barrier_semaphore()
    peers = []
    if grid:
        for d in range(SIDE):
            for e in range(SIDE):
                if d or e:
                    peers.append({"row": flip(r, d), "col": flip(c, e)})
    else:
        if rows:
            peers += [{"row": flip(r, d)} for d in (1, 2, 3)]
        peers += [{"col": flip(c, e)} for e in cols]
    if dp:
        peers.append({"dp": 1 - lax.axis_index("dp")})
    for peer in peers:
        pl.semaphore_signal(sem, inc=1, device_id=peer, device_id_type=MESH)
    pl.semaphore_wait(sem, len(peers))


def hop(src, dst, ssem, rsem, **where):
    return pltpu.make_async_remote_copy(
        src_ref=src, dst_ref=dst, send_sem=ssem, recv_sem=rsem, device_id=where, device_id_type=MESH
    )


def rows_at(ref, block, pad=0):
    return ref.at[pl.ds(pl.multiple_of(block * BLK + pad, 16), BLK)]


def dma(*shape):
    return pltpu.SemaphoreType.DMA(shape)


def launch(body, ins, outs, scratch, cid, smem=None):
    smem = smem or {}
    shapes = []
    for item in scratch.values():
        shapes += list(item.values()) if isinstance(item, dict) else [item]

    def kernel(*refs):
        refs = list(refs)
        found = {}
        for key in (*ins, *smem, *outs):
            found[key] = refs.pop(0)
        for key, item in scratch.items():
            if isinstance(item, dict):
                found[key] = types.SimpleNamespace(**{name: refs.pop(0) for name in item})
            else:
                found[key] = refs.pop(0)
        body(types.SimpleNamespace(**found))

    vector = pl.BlockSpec(memory_space=pltpu.VMEM)
    results = pl.pallas_call(
        kernel,
        out_shape=[jax.ShapeDtypeStruct(*o) for o in outs.values()],
        in_specs=[vector] * len(ins) + [pl.BlockSpec(memory_space=pltpu.SMEM)] * len(smem),
        out_specs=[vector] * len(outs),
        scratch_shapes=shapes,
        compiler_params=pltpu.CompilerParams(
            collective_id=cid, has_side_effects=True, vmem_limit_bytes=58 << 20
        ),
        name=body.__name__,
    )(*ins.values(), *smem.values())
    return types.SimpleNamespace(**dict(zip(outs, results)))


def rows_scratch(padded=False):
    size = LEN + 2 * HALO if padded else LEN
    return dict(g=pltpu.VMEM((size, D // SIDE), BF), zs=dma(SIDE), zr=dma(3))


def inner(r):
    return lax.rem(r, 3) != 0


def swapped(i):
    return 2 * lax.rem(i, 2) + lax.div(i, 2)


def row_hop(S, r, d, pad=0):
    own = rows_at(S.g, r, pad)
    return hop(own, own, S.zs.at[d - 1], S.zr.at[d - 1], row=flip(r, d))


def pass_hop(S, r, pad=0):
    part = rows_at(S.g, flip(r, 2), pad)
    return hop(part, part, S.zs.at[3], S.zr.at[2], row=flip(r, 1))


def gather_rows(S, r, pad=0):
    row_hop(S, r, 2, pad).start()
    row_hop(S, r, 1, pad).start()

    @pl.when(inner(r))
    def _():
        row_hop(S, r, 3, pad).start()


def wait_rows(S, r, d, pad=0):
    part = rows_at(S.g, flip(r, d), pad)
    hop(part, part, S.zs.at[d - 1], S.zr.at[d - 1], row=flip(r, d)).wait_recv()

    @pl.when((d == 2) & inner(r))
    def _():
        pass_hop(S, r, pad).start()


def wait_rows_sent(S, r, pad=0):
    row_hop(S, r, 2, pad).wait_send()
    row_hop(S, r, 1, pad).wait_send()

    @pl.when(inner(r))
    def _():
        row_hop(S, r, 3, pad).wait_send()
        pass_hop(S, r, pad).wait_send()


def cols_scratch(w):
    return dict(
        cs=pltpu.VMEM((SIDE, 2, BLK, w), F32),
        cr=pltpu.VMEM((SIDE, 2, BLK, w), F32),
        xs=pltpu.VMEM((SIDE, BLK, w), BF),
        xr=pltpu.VMEM((SIDE, BLK, w), BF),
        acc=pltpu.VMEM((SIDE, BLK, w), F32),
        mine=pltpu.VMEM((SIDE, BLK, w), F32),
        ks=dma(SIDE),
        kr=dma(SIDE),
        ss=dma(SIDE),
        sr=dma(SIDE),
    )


def scatter_cols(S, G, r, c, product, finish, pad=0):
    cs, cr, xs, xr, acc = (S.cs, S.cr, S.xs, S.xr, S.acc)

    def core_hop(d):
        return hop(cs.at[d], cr.at[d], S.ks.at[d], S.kr.at[d], col=flip(c, 1))

    def x_hop(d):
        return hop(xs.at[d], xr.at[d], S.ss.at[d], S.sr.at[d], col=flip(c, 2))

    def first(i):
        d = swapped(i)

        @pl.when(i > 0)
        def _():
            wait_rows(G, r, d, pad)

        rows = rows_at(G.g, flip(r, d), pad)[...]
        cs[d, 1] = product(rows, flip(c, 3))
        cs[d, 0] = product(rows, flip(c, 1))
        core_hop(d).start()
        S.mine[d] = product(rows, flip(c, 2))
        acc[d] = product(rows, c)

    def second(i):
        d = swapped(i)
        core_hop(d).wait_recv()
        xs[d] = (S.mine[d] + cr[d, 1]).astype(BF)
        x_hop(d).start()
        acc[d] = acc[d] + cr[d, 0]

    def end(i, carry):
        d = swapped(i)
        x_hop(d).wait_recv()
        finish(flip(r, d), acc[d] + xr[d].astype(F32))
        x_hop(d).wait_send()
        core_hop(d).wait_send()
        return carry

    def close():
        lax.fori_loop(0, SIDE, end, 0)

    return first, second, close


def each(*phases):
    def step(i, carry):
        for phase in phases:
            phase(i)
        return carry

    lax.fori_loop(0, SIDE, step, 0)


def tokens_scratch(*shape, low=F32):
    return dict(
        cs=pltpu.VMEM((2, *shape), low),
        cr=pltpu.VMEM((2, *shape), low),
        xs=pltpu.VMEM(shape, low),
        xr=pltpu.VMEM(shape, low),
        acc=pltpu.VMEM(shape, F32),
        ks=dma(),
        kr=dma(),
        ss=dma(),
        sr=dma(),
    )


def scatter_tokens(S, c, product):
    low = S.xs.dtype
    core = hop(S.cs, S.cr, S.ks, S.kr, col=flip(c, 1))
    over = hop(S.xs, S.xr, S.ss, S.sr, col=flip(c, 2))
    S.cs[1] = product(flip(c, 3)).astype(low)
    S.cs[0] = product(flip(c, 1)).astype(low)
    core.start()
    mine = product(flip(c, 2))
    S.acc[...] = product(c)
    core.wait_recv()
    S.xs[...] = (mine + S.cr[1].astype(F32)).astype(low)
    over.start()
    S.acc[...] = S.acc[...] + S.cr[0].astype(F32)

    def close():
        over.wait_recv()
        total = S.acc[...] + S.xr[...].astype(F32)
        over.wait_send()
        core.wait_send()
        return total

    return close


def trio_scratch():
    return dict(xs=dma(), xr=dma(), ks=dma(), kr=dma(), fs=dma(), fr=dma())


def trio(S, c, part):
    own, over = part(c), part(flip(c, 2))
    return (
        hop(own, own, S.xs, S.xr, col=flip(c, 2)),
        hop(own, own, S.ks, S.kr, col=flip(c, 1)),
        hop(over, over, S.fs, S.fr, col=flip(c, 1)),
    )


def trio_end(hops):
    over, core, forward = hops
    over.wait_recv()
    forward.start()
    core.wait_recv()
    forward.wait_recv()


def gcols_scratch(w):
    return dict(
        g=pltpu.VMEM((SIDE, LEN, w), BF),
        xs=dma(SIDE),
        xr=dma(SIDE),
        ks=dma(SIDE),
        kr=dma(SIDE),
        fs=dma(SIDE),
        fr=dma(SIDE),
    )


def col_part(S, j, t):
    return S.g.at[j, pl.ds(pl.multiple_of(t * BLK, BLK), BLK)]


def col_hop(S, c, kind, t, d):
    part = col_part(S, flip(c, 2) if kind == "f" else c, t)
    to = flip(c, 2) if kind == "x" else flip(c, 1)
    return hop(part, part, getattr(S, kind + "s").at[d], getattr(S, kind + "r").at[d], col=to)


def gather_cols(S, r, c, order=(3, 1, 2, 0)):
    for d in order:
        t = flip(r, d)
        col_hop(S, c, "x", t, d).start()
        col_hop(S, c, "k", t, d).start()


def wait_cols(S, r, c, d):
    t = flip(r, d)
    col_hop(S, c, "x", t, d).wait_recv()
    col_hop(S, c, "f", t, d).start()
    col_hop(S, c, "k", t, d).wait_recv()
    col_hop(S, c, "f", t, d).wait_recv()


def wait_cols_sent(S, r, c):
    def step(d, carry):
        t = flip(r, d)
        for kind in "xkf":
            col_hop(S, c, kind, t, d).wait_send()
        return carry

    lax.fori_loop(0, SIDE, step, 0)


def srows_scratch():
    w = D // SIDE
    return dict(
        ps=pltpu.VMEM((3, BLK, w), BF),
        pr=pltpu.VMEM((3, BLK, w), BF),
        fr=pltpu.VMEM((BLK, w), BF),
        pa=pltpu.VMEM((BLK, w), F32),
        rs=dma(3),
        rr=dma(3),
        frs=dma(),
    )


def scatter_rows(S, r, product, ready):
    ps, pr, acc = S.ps, S.pr, S.pa

    def direct(d):
        return hop(ps.at[d - 1], pr.at[d - 1], S.rs.at[d - 1], S.rr.at[d - 1], row=flip(r, d))

    def aside():
        return hop(ps.at[2], S.fr, S.rs.at[2], S.frs, row=flip(r, 1))

    def step(i):
        d = 3 - swapped(i)
        ready(d)
        acc[...] = product(flip(r, d))

        @pl.when((d == 2) & inner(r))
        def _():
            aside().wait_recv()
            acc[...] = acc[...] + S.fr[...].astype(F32)

        @pl.when(d > 0)
        def _():
            ps[d - 1] = acc[...].astype(BF)

        @pl.when((d == 3) & jnp.logical_not(inner(r)))
        def _():
            aside().start()

        @pl.when((d > 0) & ((d < 3) | inner(r)))
        def _():
            direct(d).start()

    def close():
        for d in (1, 2):
            direct(d).wait_recv()
            acc[...] = acc[...] + pr[d - 1].astype(F32)

        @pl.when(inner(r))
        def _():
            direct(3).wait_recv()
            acc[...] = acc[...] + pr[2].astype(F32)

        for d in (1, 2, 3):
            direct(d).wait_send()
        return acc[...]

    return step, close


def pair_scratch(*shapes):
    found = dict(ss=dma(len(shapes)), sr=dma(len(shapes)))
    for k, shape in enumerate(shapes):
        found[LETTERS[k]] = pltpu.VMEM(shape, BF)
        found[LETTERS[k].upper()] = pltpu.VMEM(shape, BF)
    return found


def pair_hop(S, k, own=None):
    src = getattr(S, LETTERS[k]) if own is None else own
    dst = getattr(S, LETTERS[k].upper())
    return hop(src, dst, S.ss.at[k], S.sr.at[k], dp=1 - lax.axis_index("dp"))


def paired():
    return lax.axis_size("dp") == 2


def row_sums(v):
    return dot_nt(jnp.ones((8, v.shape[1]), F32), v, HIGHEST)


def stat_scratch():
    return dict(st=pltpu.VMEM((SIDE, 8, BLK), F32), sts=dma(3), str=dma(3))


def col_sum(S, c, v):
    st = S.st
    st[c] = v
    hops = [
        hop(st.at[c], st.at[c], S.sts.at[e - 1], S.str.at[e - 1], col=flip(c, e)) for e in (1, 2, 3)
    ]
    for one in hops:
        one.start()
    for one in hops:
        one.wait_recv()
    total = (st[0] + st[1]) + (st[2] + st[3])
    for one in hops:
        one.wait_send()
    return total


def grid_scratch():
    return dict(st=pltpu.VMEM((SIDE, SIDE, 8, BLK), F32), sts=dma(16), str=dma(16))


def grid_sum(S, r, c):
    st = S.st
    hops = []
    for d in range(SIDE):
        for e in range(SIDE):
            if d or e:
                k = SIDE * d + e
                hops.append(
                    hop(
                        st.at[r, c],
                        st.at[r, c],
                        S.sts.at[k],
                        S.str.at[k],
                        row=flip(r, d),
                        col=flip(c, e),
                    )
                )
    for one in hops:
        one.start()

    def close():
        for one in hops:
            one.wait_recv()
        total = jnp.zeros((8, BLK), F32)
        for d in range(SIDE):
            for e in range(SIDE):
                total = total + st[d, e]
        for one in hops:
            one.wait_send()
        return total

    return close


def to_column(v):
    return jnp.transpose(v)[:, :1]


def pick_column(v, b):
    return jnp.sum(jnp.where(iota(v.shape, 1) == b, v, 0.0), axis=1, keepdims=True)


def cut(v, j, w):
    return v[:, j * w : (j + 1) * w]


def cut(v, j, w):
    return v[:, j * w : (j + 1) * w]


def project_kernel(x, gain, wz, wx, wbc, wq, wkv, ws, cw):
    def project(R):
        r, c = here()
        greet(r, c, rows=True, cols=(1, 2, 3))
        tap_hops = [
            hop(R.taps.at[c], R.taps.at[c], R.tss.at[e - 1], R.tsr.at[e - 1], col=flip(c, e)) for e in (1, 2, 3)
        ]
        R.taps[c] = jnp.zeros((8, 128), F32)
        R.taps[c, 0:4, 0:32] = R.cw[...]
        for one in tap_hops:
            one.start()
        x = R.x[...].astype(F32)
        total = col_sum(R.n, c, row_sums(x * x))
        scale = to_column(lax.rsqrt(total / D + EPSILON))
        g = R.p.g
        g[pl.ds(0, HALO)] = jnp.zeros((HALO, D // SIDE), BF)
        g[pl.ds(LEN + HALO, HALO)] = jnp.zeros((HALO, D // SIDE), BF)
        rows_at(g, r, HALO)[...] = (x * scale * R.gain[...]).astype(BF)
        gather_rows(R.p, r, HALO)
        wa, wb = R.wa, R.wb
        for j in range(SIDE):
            wa[j, :, 0:HW] = cut(R.wz, j, HW)
            wa[j, :, HW : 2 * HW] = cut(R.wx, j, HW)
        wb[:, 0:128] = R.wbc[...]
        wb[:, 128:384] = R.wq[...]
        wb[:, 384:512] = R.wkv[...]

        def finish(block, v):
            at = pl.ds(pl.multiple_of(block * BLK, BLK), BLK)
            R.z[at] = v[:, 0:HW]
            R.xr[at] = v[:, HW : 2 * HW]

        first, second, close_a = scatter_cols(R.a, R.p, r, c, lambda rows, j: dot_nn(rows, wa[j]), finish, HALO)
        each(first, second)
        steps = dot_nt(R.ws[...], g[pl.ds(HALO, LEN)])
        for j in range(SIDE):
            R.ps[j] = steps[16 * j : 16 * j + 8]
        step_hops = [
            hop(
                R.ps.at[flip(c, e)],
                R.pr.at[e - 1],
                R.pss.at[e - 1],
                R.psr.at[e - 1],
                col=flip(c, e),
            )
            for e in (1, 2, 3)
        ]
        for one in step_hops:
            one.start()

        def token_rows(j):
            return dot_nn(g[pl.ds(pl.multiple_of(j * BLK, BLK), BLK + 2 * HALO)], wb[...])

        close_b = scatter_tokens(R.b, c, token_rows)
        R.n1[...] = g[pl.ds(HALO, LEN)]
        R.s1[...] = total
        R.wa_o[...] = wa[...]
        R.wb_o[...] = wb[...]
        close_a()
        for one in step_hops:
            one.wait_recv()
        R.sr[...] = (R.ps[c] + R.pr[0]) + (R.pr[1] + R.pr[2])
        for one in step_hops:
            one.wait_send()
        R.br[...] = close_b()
        for one in tap_hops:
            one.wait_recv()
        R.wcs[...] = jnp.concatenate([R.taps[j, 0:4, 0:32] for j in range(SIDE)], axis=1)
        for one in tap_hops:
            one.wait_send()
        wait_rows_sent(R.p, r, HALO)

    n = BLK + 2 * HALO
    scratch = dict(
        p=rows_scratch(True),
        n=stat_scratch(),
        a=cols_scratch(2 * HW),
        b=tokens_scratch(n, 512),
        wa=pltpu.VMEM((SIDE, 512, 2 * HW), BF),
        wb=pltpu.VMEM((512, 512), BF),
        ps=pltpu.VMEM((SIDE, 8, LEN), F32),
        pr=pltpu.VMEM((3, 8, LEN), F32),
        pss=dma(3),
        psr=dma(3),
        taps=pltpu.VMEM((SIDE, 8, 128), F32),
        tss=dma(3),
        tsr=dma(3),
    )
    outs = dict(
        n1=((LEN, 512), BF),
        s1=((8, BLK), F32),
        z=((LEN, HW), F32),
        xr=((LEN, HW), F32),
        br=((n, 512), F32),
        sr=((8, LEN), F32),
        wa_o=((SIDE, 512, 2 * HW), BF),
        wb_o=((512, 512), BF),
        wcs=((4, 128), F32),
    )
    ins = dict(x=x, gain=gain, wz=wz, wx=wx, wbc=wbc, wq=wq, wkv=wkv, ws=ws, cw=cw)
    return launch(project, ins, outs, scratch, 1)


SMALL = 32


def forward_kernel(m, o, x, gain, wo, wt, wg, wu, dh):
    def forward(R):
        r, c = here()
        greet(r, c, rows=True, cols=(1, 2, 3))
        R.mc.g[c] = R.m[...]
        og = R.og
        og[c] = R.o[...]
        o_hops = trio(R.ot, c, lambda j: og.at[j])
        o_hops[0].start()
        o_hops[1].start()
        gather_cols(R.mc, r, c)
        trio_end(o_hops)

        def product(t):
            total = dot_nn(og[t], R.wt[...])
            for j in range(SIDE):
                total = total + dot_nn(col_part(R.mc, j, t)[...], R.wo[j * HW : (j + 1) * HW])
            return total

        step, close = scatter_rows(R.s, r, product, lambda d: wait_cols(R.mc, r, c, d))
        each(step)
        R.m_all[...] = R.mc.g[...]
        R.o_all[...] = og[...]
        x1 = R.x[...].astype(F32) + close()
        R.x1[...] = x1
        total = col_sum(R.n, c, row_sums(x1 * x1))
        R.s2[...] = total
        scale = to_column(lax.rsqrt(total / D + EPSILON))
        rows_at(R.p.g, r)[...] = (R.x1[...] * scale * R.gain[...]).astype(BF)
        gather_rows(R.p, r)

        def gate_up(rows, j):
            at = pl.ds(pl.multiple_of(j * BLK, BLK), BLK)
            return jnp.concatenate([dot_nn(rows, R.wg[:, at]), dot_nn(rows, R.wu[:, at])], axis=1)

        def finish(block, v):
            at = pl.ds(pl.multiple_of(block * BLK, BLK), BLK)
            gate, up = v[:, :256], v[:, 256:]
            sig = sigmoid(gate)
            act = gate * sig
            dh = R.dh[at]
            R.hid[at] = (act * up).astype(BF)
            R.dgu[at, 0:256] = (dh * up * sig * (1.0 + gate * (1.0 - sig))).astype(BF)
            R.dgu[at, 256:512] = (dh * act).astype(BF)

        first, second, close = scatter_cols(R.a, R.p, r, c, gate_up, finish)
        each(first, second)
        R.n2_all[...] = R.p.g[...]
        close()
        for one in o_hops:
            one.wait_send()
        wait_cols_sent(R.mc, r, c)
        wait_rows_sent(R.p, r)

    scratch = dict(
        mc=gcols_scratch(HW),
        s=srows_scratch(),
        n=stat_scratch(),
        og=pltpu.VMEM((SIDE, BLK, 256), BF),
        ot=trio_scratch(),
        p=rows_scratch(),
        a=cols_scratch(512),
    )
    outs = dict(
        x1=((BLK, 512), F32),
        s2=((8, BLK), F32),
        m_all=((SIDE, LEN, HW), BF),
        o_all=((SIDE, BLK, 256), BF),
        n2_all=((LEN, 512), BF),
        hid=((LEN, 256), BF),
        dgu=((LEN, 512), BF),
    )
    return launch(forward, dict(m=m, o=o, x=x, gain=gain, wo=wo, wt=wt, wg=wg, wu=wu, dh=dh), outs, scratch, 3)


def norm_back(S, c, dn, v, scale, gain):
    gain_grad = jnp.sum(dn * v * scale, axis=0, keepdims=True)
    weighted = dn * gain
    total = col_sum(S, c, row_sums(weighted * v))
    inner = to_column(total)
    return scale * weighted - v * (scale * scale * scale * inner / D), gain_grad


def backward_kernel(dgu, wg, wu, x1, s2, gain, cot, n2, wo, wt, hid, wd, dy, m, o):
    def backward(R):
        r, c = here()
        greet(r, c, rows=True, cols=(1, 2, 3), dp=paired())
        R.gc.g[c] = R.dgu[...]
        R.hc.g[c] = R.hid[...]
        gather_cols(R.gc, r, c)

        def product(t):
            total = jnp.zeros((BLK, 512), F32)
            for j in range(SIDE):
                part = col_part(R.gc, j, t)[...]
                total = total + dot_nt(part[:, :256], R.wg[:, 256 * j : 256 * j + 256])
                total = total + dot_nt(part[:, 256:], R.wu[:, 256 * j : 256 * j + 256])
            return total

        step, close = scatter_rows(R.s, r, product, lambda d: wait_cols(R.gc, r, c, d))
        each(step)
        gather_cols(R.hc, r, c)

        def grads(j):
            at = pl.ds(pl.multiple_of(j * BLK, BLK), BLK)
            both = dot_tn(R.n2[...], R.gc.g[j])
            R.y.a[:, at] = both[:, :256].astype(BF)
            R.y.b[:, at] = both[:, 256:].astype(BF)

        each(grads)
        y_hops = [pair_hop(R.y, k) for k in range(2)] if paired() else []
        for one in y_hops:
            one.start()
        R.gate_w[...] = R.y.a[...]
        R.up_w[...] = R.y.b[...]
        dn = close()
        scale = to_column(lax.rsqrt(R.s2[...] / D + EPSILON))
        dv, dgain = norm_back(R.n, c, dn, R.x1[...], scale, R.gain[...])
        dx1 = R.cot[...] + dv
        rows_at(R.p.g, r)[...] = dx1.astype(BF)
        gather_rows(R.p, r)
        R.dx1[...] = dx1
        R.dgain[...] = dgain

        def down(i):
            wait_cols(R.hc, r, c, 3 - swapped(i))
            t = flip(r, 3 - swapped(i))
            total = dot_nn(col_part(R.hc, 0, t)[...], R.wd[0:256])
            for j in (1, 2, 3):
                total = total + dot_nn(col_part(R.hc, j, t)[...], R.wd[256 * j : 256 * j + 256])
            R.down[t] = total

        each(down)

        def down_grads(j):
            R.down_w[pl.ds(pl.multiple_of(j * BLK, BLK), BLK)] = dot_tn(R.hc.g[j], R.dy[...]).astype(BF)

        each(down_grads)

        def out_back(rows, j):
            return dot_nt(rows, R.wo[pl.ds(pl.multiple_of(j * HW, 64), HW)])

        def finish(block, v):
            R.dm[pl.ds(pl.multiple_of(block * BLK, BLK), BLK)] = v

        first, second, close_a = scatter_cols(R.a, R.p, r, c, out_back, finish)
        each(first, second)
        close_b = scatter_tokens(R.b, c, lambda j: dot_nt(rows_at(R.p.g, j)[...], R.wt[...]))

        def out_grads(j):
            R.out_w[pl.ds(pl.multiple_of(j * HW, 64), HW)] = dot_tn(R.m[j], R.p.g[...]).astype(BF)

        each(out_grads)
        R.attn_w[...] = dot_tn(R.o[...].reshape(LEN, 256), R.p.g[...]).astype(BF)
        close_a()
        R.do[...] = close_b().astype(BF)
        wait_cols_sent(R.gc, r, c)
        wait_cols_sent(R.hc, r, c)
        wait_rows_sent(R.p, r)
        for one, theirs, out in zip(y_hops, (R.y.A, R.y.B), (R.gate_p, R.up_p) if y_hops else ()):
            one.wait_recv()
            out[...] = theirs[...]
            one.wait_send()

    scratch = dict(
        gc=gcols_scratch(512),
        hc=gcols_scratch(256),
        s=srows_scratch(),
        n=stat_scratch(),
        p=rows_scratch(),
        a=cols_scratch(HW),
        b=tokens_scratch(BLK, 256, low=BF),
        y=pair_scratch((512, 1024), (512, 1024)),
    )
    outs = dict(
        gate_w=((512, 1024), BF),
        up_w=((512, 1024), BF),
        dx1=((BLK, 512), F32),
        dgain=((1, 512), F32),
        dm=((LEN, HW), F32),
        do=((BLK, 256), BF),
        down=((SIDE, BLK, 512), F32),
        down_w=((LEN, 512), BF),
        out_w=((SIDE * HW, 512), BF),
        attn_w=((256, 512), BF),
    )
    if paired():
        outs.update(gate_p=((512, 1024), BF), up_p=((512, 1024), BF))
    ins = dict(dgu=dgu, wg=wg, wu=wu, x1=x1, s2=s2, gain=gain, cot=cot, n2=n2, wo=wo, wt=wt)
    ins.update(hid=hid, wd=wd, dy=dy, m=m, o=o)
    return launch(backward, ins, outs, scratch, 6)


def project_back_kernel(da, db, ds, wa, wb, ws, x, s1, gain, dx1, n1, ffn_grad, dconv, dgain, dhead, dstates):
    pair = paired()

    def project_back(R):
        r, c = here()
        greet(r, c, rows=True, cols=(1, 2, 3), dp=pair)
        R.ac.g[c] = R.da[...]
        bg, sg, tg = R.bg, R.sg, R.tg
        bg[c] = R.db[...]
        sg[c] = R.ds[...]
        tg[c] = jnp.zeros((8, 128), F32)
        tg[c, 0:4] = R.dstates[...]
        b_hops = trio(R.bt, c, lambda j: bg.at[j])
        s_hops = []
        for e in (1, 2, 3):
            to = flip(c, e)
            s_hops.append(hop(sg.at[c], sg.at[c], R.sgs.at[e - 1], R.sgr.at[e - 1], col=to))
            s_hops.append(hop(tg.at[c], tg.at[c], R.tgs.at[e - 1], R.tgr.at[e - 1], col=to))
        b_hops[0].start()
        b_hops[1].start()
        for one in s_hops:
            one.start()
        gather_cols(R.ac, r, c)

        y = R.y
        w_hops = [pair_hop(y, k) for k in range(4)] if pair else []

        trio_end(b_hops)
        for one in s_hops:
            one.wait_recv()
        y.a[...] = dot_tn(R.n1[...], bg[...].reshape(LEN, 512)).astype(BF)
        y.b[...] = dot_nn(sg[...].reshape(16 * SIDE, LEN), R.n1[...]).astype(BF)
        if pair:
            w_hops[0].start()
            w_hops[1].start()

        def product(t):
            total = dot_nt(bg[t], R.wb[...])
            at = pl.ds(pl.multiple_of(t * BLK, BLK), BLK)
            for j in range(SIDE):
                total = total + dot_nt(col_part(R.ac, j, t)[...], R.wa[j])
                total = total + dot_tn(sg[j, :, at], R.ws[16 * j : 16 * j + 16])
            return total

        step, close = scatter_rows(R.s, r, product, lambda d: wait_cols(R.ac, r, c, d))
        each(step)
        for j in range(SIDE):
            both = dot_tn(R.n1[...], R.ac.g[j]).astype(BF)
            y.c[:, j * HW : (j + 1) * HW] = both[:, :HW]
            y.d[:, j * HW : (j + 1) * HW] = both[:, HW:]
        if pair:
            w_hops[2].start()
            w_hops[3].start()
        dn = close()
        scale = to_column(lax.rsqrt(R.s1[...] / D + EPSILON))
        dv, mixer_grad = norm_back(R.n, c, dn, R.x[...].astype(F32), scale, R.gain[...])
        gg = R.gg
        gg[r] = jnp.zeros((8, 512), F32)
        gg[r, 0:1] = mixer_grad
        gg[r, 1:2] = R.ffn_grad[...]
        g_hops = [hop(gg.at[r], gg.at[r], R.ggs.at[d - 1], R.ggr.at[d - 1], row=flip(r, d)) for d in (1, 2, 3)]
        for one in g_hops:
            one.start()
        R.dx[...] = R.dx1[...] + dv
        small = R.small
        small[...] = jnp.zeros((SMALL, 512), F32)
        small[8:12, 0:HW] = R.dconv[...]
        small[12:13, 0:HW] = R.dgain[...]
        small[16:24, 0:128] = R.dhead[...]
        small[24:32, 0:128] = (tg[0] + tg[1]) + (tg[2] + tg[3])
        for one in g_hops:
            one.wait_recv()
        small[0:8] = (gg[0] + gg[1]) + (gg[2] + gg[3])
        if pair:
            small_hop = hop(small, R.small_p, R.mss, R.msr, dp=1 - lax.axis_index("dp"))
            small_hop.start()
        for one in (*b_hops, *s_hops, *g_hops):
            one.wait_send()
        wait_cols_sent(R.ac, r, c)
        total = small[...]
        if pair:
            small_hop.wait_recv()
            total = total + R.small_p[...]
            small_hop.wait_send()
        R.o_mixer[...] = total[0:1]
        R.o_ffn[...] = total[1:2]
        R.o_conv[...] = total[8:12, 0:HW]
        R.o_gain[...] = total[12:13, 0:HW]
        heads = jnp.transpose(total[16:24, 0:128])
        R.o_bias[...] = heads[0:1, 0:HH]
        R.o_decay[...] = heads[1:2, 0:HH]
        R.o_skip[...] = heads[2:3, 0:HH]
        taps = jnp.zeros((4, 32), F32)
        for j in range(SIDE):
            taps = taps + jnp.where(c == j, total[24:28, 32 * j : 32 * j + 32], 0.0)
        R.o_states[...] = taps
        for own, out in zip((y.a, y.b, y.c, y.d), (R.bo, R.so, R.zo, R.xo)):
            out[...] = own[...]
        if pair:
            for one, theirs, out in zip(w_hops, (y.A, y.B, y.C, y.D), (R.bq, R.sq, R.zq, R.xq)):
                one.wait_recv()
                out[...] = theirs[...]
                one.wait_send()

    scratch = dict(
        ac=gcols_scratch(2 * HW),
        s=srows_scratch(),
        n=stat_scratch(),
        bt=trio_scratch(),
        bg=pltpu.VMEM((SIDE, BLK, 512), BF),
        sg=pltpu.VMEM((SIDE, 16, LEN), BF),
        sgs=dma(3),
        sgr=dma(3),
        tg=pltpu.VMEM((SIDE, 8, 128), F32),
        tgs=dma(3),
        tgr=dma(3),
        gg=pltpu.VMEM((SIDE, 8, 512), F32),
        ggs=dma(3),
        ggr=dma(3),
        y=pair_scratch((512, 512), (16 * SIDE, 512), (512, 768), (512, 768)),
        small=pltpu.VMEM((SMALL, 512), F32),
        small_p=pltpu.VMEM((SMALL, 512), F32),
        mss=dma(),
        msr=dma(),
    )
    outs = dict(
        dx=((BLK, 512), F32),
        o_mixer=((1, 512), F32),
        o_ffn=((1, 512), F32),
        o_conv=((4, HW), F32),
        o_gain=((1, HW), F32),
        o_bias=((1, HH), F32),
        o_decay=((1, HH), F32),
        o_skip=((1, HH), F32),
        o_states=((4, 32), F32),
        bo=((512, 512), BF),
        so=((16 * SIDE, 512), BF),
        zo=((512, 768), BF),
        xo=((512, 768), BF),
    )
    if pair:
        outs.update(bq=((512, 512), BF), sq=((16 * SIDE, 512), BF), zq=((512, 768), BF), xq=((512, 768), BF))
    ins = dict(da=da, db=db, ds=ds, wa=wa, wb=wb, ws=ws, x=x, s1=s1, gain=gain, dx1=dx1, n1=n1)
    ins.update(ffn_grad=ffn_grad, dconv=dconv, dgain=dgain, dhead=dhead, dstates=dstates)
    return launch(project_back, ins, outs, scratch, 8)


def per_head(values):
    lane = iota((1, HW), 1)
    first = jnp.where(lane < HDIM, values[0], values[1])
    return jnp.where(lane < 2 * HDIM, first, values[2])


def head_select():
    return jnp.where(iota((8, HW), 1) // HDIM == iota((8, HW), 0), 1.0, 0.0).astype(F32)


def scalar_rows(ref):
    sub = iota((8, 1), 0)
    return jnp.where(sub == 0, ref[0], jnp.where(sub == 1, ref[1], jnp.where(sub == 2, ref[2], 0.0)))


def triangle():
    return jnp.where(iota((BLK, BLK), 0) <= iota((BLK, BLK), 1), 1.0, 0.0).astype(F32)


def fill_padded(R):
    R.xpad[0:8] = jnp.zeros((8, HW), F32)
    R.xpad[8 : 8 + LEN] = R.xr[...]


def conv_block(R, b):
    start = pl.multiple_of(b * BLK, BLK)
    chunk = R.xpad[pl.ds(start, BLK + 8)]
    taps = [chunk[5 + j : 5 + j + BLK] for j in range(4)]
    pre = taps[0] * R.wc[0:1]
    for j in (1, 2, 3):
        pre = pre + taps[j] * R.wc[j : j + 1]
    return pre, taps


def step_block(R, b):
    at = pl.ds(pl.multiple_of(b * BLK, BLK), BLK)
    raw = R.sr[:, at] + scalar_rows(R.bias)
    dt = softplus(raw)
    rate = -dt * jnp.exp(scalar_rows(R.decay))
    within = dot_nn(rate, triangle(), HIGHEST)
    return raw, dt, rate, within, jnp.transpose(dt), jnp.transpose(within)


def rope_turn(v, cosine, sine):
    return v * cosine + pltpu.roll(v, ADIM // 2, axis=1) * sine


def rope_tables():
    half = ADIM // 2
    freqs = np.float32(ROPE_BASE) ** (-np.arange(half, dtype=np.float32) / np.float32(half))
    angles = np.arange(LEN, dtype=np.float32)[:, None] * freqs.astype(np.float32)
    angles = angles.astype(np.float32).astype(np.float64)
    cosine, sine = np.cos(angles), np.sin(angles)
    return (
        np.concatenate([cosine, cosine], axis=1).astype(np.float32),
        np.concatenate([-sine, sine], axis=1).astype(np.float32),
    )


def key_scores(q, keys, c):
    s = dot_nt(q, keys) * SCALE
    return jnp.where(iota(s.shape, 1) <= c * BLK + iota(s.shape, 0), s, NEGATIVE)


def state_cols(R, kind, b):
    g = R.g
    return jnp.concatenate([g[2 * kind, b], g[2 * kind + 1, b]], axis=1)


def lower_decay(within_c, within_r, h):
    gaps = within_c[:, h : h + 1] - within_r[h : h + 1]
    return jnp.exp(jnp.where(iota((BLK, BLK), 1) <= iota((BLK, BLK), 0), gaps, NEGATIVE))


def head_mask(v, h):
    return jnp.where(iota((1, HW), 1) // HDIM == h, v, jnp.zeros_like(v))


def head_masks(v, h):
    return head_mask(v[0], h), head_mask(v[1], h)


def column_heads(cols):
    return per_head([cols[:, h : h + 1] for h in range(HH)])


def mixers_kernel(z, xr, br, sr, wc, wcs, bias, decay, skip, gain, cosine, sine, cot, wd):
    def mixers(R):
        r, c = here()
        greet(r, c, grid=True)
        g = R.g
        br = R.br
        pre = br[13 : 13 + BLK, 0:128] * R.wcs[0:1]
        for j in (1, 2, 3):
            pre = pre + br[13 + j : 13 + j + BLK, 0:128] * R.wcs[j : j + 1]
        g[r, c] = (pre * sigmoid(pre)).astype(BF)
        at = pl.ds(pl.multiple_of(c * BLK, BLK), BLK)
        cos, sin = R.cos[at], R.sin[at]
        kv = br[HALO : HALO + BLK, 384:512].astype(BF)
        turned = rope_turn(kv.astype(F32), cos, sin).astype(BF)
        kind, head = lax.div(r, 2), lax.rem(r, 2)
        kvb = R.kvb
        kvb[...] = jnp.where(kind == 0, turned, kv)
        slot = SIDE + kind

        @pl.when(head == kind)
        def _():
            g[slot, c] = kvb[...]

        def bc_hop(d):
            return hop(g.at[r, c], g.at[r, c], R.zs.at[d - 1], R.zr.at[d - 1], row=flip(r, d))

        def kv_hop(d):
            return hop(kvb, g.at[slot, c], R.ys.at[d - 1], R.yr.at[d - 1], row=flip(r, d))

        for d in (1, 2, 3):
            bc_hop(d).start()

            @pl.when(lax.div(flip(r, d), 2) == head)
            def _():
                kv_hop(d).start()

        rows_at(R.p.g, r)[...] = R.cot[...].astype(BF)
        gather_rows(R.p, r)
        fill_padded(R)
        for d in (1, 2, 3):
            bc_hop(d).wait_recv()

            @pl.when(lax.rem(flip(r, d), 2) == kind)
            def _():
                kv_hop(d).wait_recv()

        g_hops = trio(R.gt, c, lambda j: g.at[:, j])
        g_hops[0].start()
        g_hops[1].start()
        for h in range(2):
            q = br[HALO : HALO + BLK, 128 + 128 * h : 256 + 128 * h].astype(BF).astype(F32)
            R.qr[h] = rope_turn(q, cos, sin).astype(BF)
        trio_end(g_hops)

        state = R.state
        state[...] = jnp.zeros_like(state)
        st = R.n.st
        st[r, c] = jnp.zeros((8, BLK), F32)
        skip_row = per_head([R.skip[h] for h in range(HH)])

        def hidden_back(rows, j):
            return dot_nt(rows, R.wd[pl.ds(pl.multiple_of(j * BLK, BLK), BLK)])

        def finish(block, v):
            R.dh[pl.ds(pl.multiple_of(block * BLK, BLK), BLK)] = v

        first, second, close_h = scatter_cols(R.a, R.p, r, c, hidden_back, finish)

        def block(b, carry):
            first(b)
            at = pl.ds(pl.multiple_of(b * BLK, BLK), BLK)
            pre, _ = conv_block(R, b)
            u = pre * sigmoid(pre)
            _, _, _, within, dt_c, within_c = step_block(R, b)
            bb, cb = state_cols(R, 0, b), state_cols(R, 1, b)
            x = u * column_heads(dt_c)
            xb = halves(x)
            scores = dot_nt(cb, bb)
            y = jnp.exp(column_heads(within_c)) * fine(dot_nn, cb, halves(state[...]))
            for h in range(HH):
                a = halves(scores * lower_decay(within_c, within, h))
                y = y + fine(dot_nn, a, head_masks(xb, h))
            last = per_head([within[h : h + 1, BLK - 1 : BLK] for h in range(HH)])
            keep = jnp.exp(last - column_heads(within_c))
            R.states[b] = state[...]
            state[...] = state[...] * jnp.exp(last) + fine(dot_tn, bb, halves(x * keep))
            y = y + skip_row * u
            zb = R.z[at]
            gated = y * zb * sigmoid(zb)
            R.y[at] = y
            R.gs[at] = gated
            sums = row_sums(gated * gated)
            st[r, c] = jnp.where(iota((8, BLK), 0) == b, sums, st[r, c])
            second(b)
            return carry

        lax.fori_loop(0, SIDE, block, 0)
        close = grid_sum(R.n, r, c)

        keys = g[4].reshape(LEN, ADIM)
        values = g[5].reshape(LEN, ADIM)
        for h in range(2):
            s = key_scores(R.qr[h], keys, c)
            top = jnp.max(s, axis=1, keepdims=True)
            lse = top + jnp.log(jnp.sum(jnp.exp(s - top), axis=1, keepdims=True))
            R.lse[h] = jnp.broadcast_to(lse, (BLK, 128))
            probs = jnp.exp(s - lse).astype(BF)
            R.o[:, 128 * h : 128 * h + 128] = dot_nn(probs, values).astype(BF)

        total = close()
        R.s3[...] = total
        scales = jnp.transpose(lax.rsqrt(total / (HEADS * HDIM) + EPSILON))

        def scaled(b, carry):
            at = pl.ds(pl.multiple_of(b * BLK, BLK), BLK)
            R.m[at] = (R.gs[at] * pick_column(scales, b) * R.gain[...]).astype(BF)
            return carry

        lax.fori_loop(0, SIDE, scaled, 0)
        R.g_o[...] = g[...]
        R.dy[...] = R.p.g[...]
        close_h()
        wait_rows_sent(R.p, r)
        for d in (1, 2, 3):
            bc_hop(d).wait_send()

            @pl.when(lax.div(flip(r, d), 2) == head)
            def _():
                kv_hop(d).wait_send()

        for one in g_hops:
            one.wait_send()

    scratch = dict(
        n=grid_scratch(),
        p=rows_scratch(),
        a=cols_scratch(256),
        g=pltpu.VMEM((6, SIDE, BLK, 128), BF),
        kvb=pltpu.VMEM((BLK, 128), BF),
        xpad=pltpu.VMEM((LEN + 8, HW), F32),
        gs=pltpu.VMEM((LEN, HW), F32),
        state=pltpu.VMEM((STATE, HW), F32),
        zs=dma(3),
        zr=dma(3),
        ys=dma(3),
        yr=dma(3),
        gt=trio_scratch(),
    )
    outs = dict(
        m=((LEN, HW), BF),
        o=((BLK, 256), BF),
        y=((LEN, HW), F32),
        s3=((8, BLK), F32),
        lse=((2, BLK, 128), F32),
        states=((SIDE, STATE, HW), F32),
        g_o=((6, SIDE, BLK, 128), BF),
        qr=((2, BLK, 128), BF),
        dy=((LEN, 512), BF),
        dh=((LEN, 256), F32),
    )
    ins = dict(z=z, xr=xr, br=br, sr=sr, wc=wc, wcs=wcs, gain=gain, cos=cosine, sin=sine, cot=cot, wd=wd)
    return launch(mixers, ins, outs, scratch, 9, dict(bias=bias, decay=decay, skip=skip))


def mixers_back_kernel(
    dm, do, z, xr, br, sr, y, s3, states, g, qr, lse, wc, wcs, bias, decay, skip, gain, cosine, sine, x1, down, down_w, out_w, attn_w
):
    n = BLK + HALO

    def mixers_back(R):
        r, c = here()
        greet(r, c, grid=True, dp=paired())
        y_hops = []
        if paired():
            y_hops = [pair_hop(R.yy, k, own) for k, own in enumerate((R.down_w, R.out_w, R.attn_w))]
        for one in y_hops:
            one.start()
        g = R.g
        fill_padded(R)
        st = R.n.st
        st[r, c] = jnp.zeros((8, BLK), F32)
        gain = R.gain[...]

        def inner(b, carry):
            at = pl.ds(pl.multiple_of(b * BLK, BLK), BLK)
            zb = R.z[at]
            sums = row_sums(R.dm[at] * gain * R.y[at] * zb * sigmoid(zb))
            st[r, c] = jnp.where(iota((8, BLK), 0) == b, sums, st[r, c])
            return carry

        lax.fori_loop(0, SIDE, inner, 0)
        close = grid_sum(R.n, r, c)

        tb = R.tb
        tb[:, pl.ds(LEN, HALO)] = jnp.zeros((6, HALO, 128), F32)
        keys = g[4].reshape(LEN, ADIM)
        values = g[5].reshape(LEN, ADIM)
        at = pl.ds(pl.multiple_of(c * BLK, BLK), BLK)
        cos, sin = R.cos[at], R.sin[at]
        for h in range(2):
            q = R.qr[h]
            dob = R.do[:, 128 * h : 128 * h + 128]
            p = jnp.exp(key_scores(q, keys, c) - R.lse[h][:, :1])
            dv = dot_tn(p.astype(BF), dob)
            dp = dot_nt(dob, values)
            ds = (p * (dp - jnp.sum(dp * p, axis=1, keepdims=True)) * SCALE).astype(BF)
            dk = dot_tn(ds, q)
            if h == 0:
                tb[4, 0:LEN] = dk
                tb[5, 0:LEN] = dv
            else:
                tb[4, 0:LEN] = tb[4, 0:LEN] + dk
                tb[5, 0:LEN] = tb[5, 0:LEN] + dv
            dq = dot_nn(ds, keys)
            R.db[:, 128 + 128 * h : 256 + 128 * h] = rope_turn(dq, cos, -sin).astype(BF)

        scales = jnp.transpose(lax.rsqrt(R.s3[...] / (HEADS * HDIM) + EPSILON))
        inners = jnp.transpose(close())

        step, close_d = scatter_rows(R.s, r, lambda t: R.down[t], lambda d: None)
        dstate, dpre_pad = R.dstate, R.dpre
        dstate[...] = jnp.zeros_like(dstate)
        dpre_pad[LEN : LEN + 8] = jnp.zeros((8, HW), F32)
        select = head_select()
        skip_row = per_head([R.skip[h] for h in range(HH)])
        rate_of = jnp.exp(scalar_rows(R.decay))
        for ref in (R.dgain, R.dskip, R.dconv, R.dhead, R.ds):
            ref[...] = jnp.zeros_like(ref)
        upto = jnp.where(iota((BLK, BLK), 0) >= iota((BLK, BLK), 1), 1.0, 0.0).astype(F32)

        def block(i, carry):
            step(i)
            b = 3 - i
            at = pl.ds(pl.multiple_of(b * BLK, BLK), BLK)
            pre, taps = conv_block(R, b)
            sig = sigmoid(pre)
            u = pre * sig
            raw, dt, rate, within, dt_c, within_c = step_block(R, b)
            bb, cb = state_cols(R, 0, b), state_cols(R, 1, b)
            zb, yb, dm = R.z[at], R.y[at], R.dm[at]
            zsig = sigmoid(zb)
            zact = zb * zsig
            gated = yb * zact
            scale = pick_column(scales, b)
            dgated = scale * dm * gain - gated * (scale * scale * scale * pick_column(inners, b) / (HEADS * HDIM))
            R.dgain[...] += jnp.sum(dm * gated * scale, axis=0, keepdims=True)
            dy = dgated * zact
            R.da[at, 0:HW] = (dgated * yb * zsig * (1.0 + zb * (1.0 - zsig))).astype(BF)
            R.dskip[...] += jnp.sum(dy * u, axis=0, keepdims=True)
            dyb = halves(dy)
            wide = column_heads(within_c)
            grow = jnp.exp(wide)
            last = per_head([within[h : h + 1, BLK - 1 : BLK] for h in range(HH)])
            keep = jnp.exp(last - wide)
            dt_w = column_heads(dt_c)
            x = u * dt_w
            xb = halves(x)
            scores = dot_nt(cb, bb)
            state = R.states[b]
            stb = halves(state)
            yin = jnp.zeros((BLK, HW), F32)
            dx = jnp.zeros((BLK, HW), F32)
            dscores = jnp.zeros((BLK, BLK), F32)
            for h in range(HH):
                decay_h = lower_decay(within_c, within, h)
                a = halves(scores * decay_h)
                xh = head_masks(xb, h)
                yin = yin + fine(dot_nn, a, xh)
                dx = dx + fine(dot_tn, a, head_masks(dyb, h))
                dscores = dscores + fine(dot_nt, dyb, xh) * decay_h
            dsb = halves(dscores)
            dyg = dy * grow
            dygb = halves(dyg)
            xk = x * keep
            dst = dstate[...]
            dstb = halves(dst)
            dc = fine(dot_nn, dsb, bb) + fine(dot_nt, dygb, stb)
            db = fine(dot_tn, dsb, cb) + fine(dot_nt, halves(xk), dstb)
            tb[0, at] = db[:, :128]
            tb[1, at] = db[:, 128:]
            tb[2, at] = dc[:, :128]
            tb[3, at] = dc[:, 128:]
            dxk = fine(dot_nn, bb, dstb)
            carried = dxk * xk
            turn = dy * yin - x * dx + dyg * fine(dot_nn, cb, stb) - carried
            dx = dx + dxk * keep
            elast = jnp.exp(last)
            ends = jnp.sum(carried, axis=0, keepdims=True) + jnp.sum(dst * state, axis=0, keepdims=True) * elast
            dlast = dot_nt(select, jnp.broadcast_to(ends, (8, HW)), HIGHEST)[:, :1]
            drate = dot_nn(dot_nt(select, turn, HIGHEST), upto, HIGHEST) + dlast
            ddt = dot_nt(select, dx * u, HIGHEST) - drate * rate_of
            draw = ddt * sigmoid(raw)
            R.ds[0:8, at] = draw.astype(BF)
            lane = iota((8, 128), 1)
            R.dhead[...] += jnp.where(
                lane == 0,
                jnp.sum(draw, axis=1, keepdims=True),
                jnp.where(lane == 1, jnp.sum(drate * rate, axis=1, keepdims=True), 0.0),
            )
            dstate[...] = dst * elast + fine(dot_tn, cb, dygb)
            du = dx * dt_w + dy * skip_row
            dpre = du * sig * (1.0 + pre * (1.0 - sig))
            dpre_pad[at] = dpre
            for j in range(4):
                R.dconv[j : j + 1] += jnp.sum(dpre * taps[j], axis=0, keepdims=True)
            chunk = dpre_pad[pl.ds(pl.multiple_of(b * BLK, BLK), BLK + 8)]
            dxr = chunk[3 : 3 + BLK] * R.wc[0:1]
            for j in (1, 2, 3):
                dxr = dxr + chunk[3 - j : 3 - j + BLK] * R.wc[j : j + 1]
            R.da[at, HW : 2 * HW] = dxr.astype(BF)
            return carry

        lax.fori_loop(0, SIDE, block, 0)
        R.dhead[...] += jnp.where(
            iota((8, 128), 1) == 2,
            dot_nt(select, jnp.broadcast_to(R.dskip[...], (8, HW)), HIGHEST)[:, :1],
            0.0,
        )

        def token_rows(j):
            return tb[:, pl.ds(pl.multiple_of(j * BLK, BLK), n)]

        close_t = scatter_tokens(R.t, c, token_rows)
        total = close_t()
        tob = R.tob
        tob[...] = total.astype(BF)
        mine = R.mine
        mine[...] = total
        kind, head = lax.div(r, 2), lax.rem(r, 2)

        def bc_hop(d):
            return hop(tob.at[flip(r, d)], R.zbr.at[d - 1], R.zs.at[d - 1], R.zr.at[d - 1], row=flip(r, d))

        def kv_hop(d):
            to = flip(r, d)
            return hop(
                tob.at[SIDE + lax.div(to, 2), pl.ds(0, BLK)],
                R.zkr.at[d - 1],
                R.ys.at[d - 1],
                R.yr.at[d - 1],
                row=to,
            )

        for d in (1, 2, 3):
            bc_hop(d).start()

            @pl.when(lax.rem(flip(r, d), 2) == kind)
            def _():
                kv_hop(d).start()

        dpost = mine[r]
        dkv = R.dkv
        dkv[...] = jnp.zeros_like(dkv)

        @pl.when(head == kind)
        def _():
            dkv[...] = mine[SIDE + kind, 0:BLK]

        for d in (1, 2, 3):
            bc_hop(d).wait_recv()
            dpost = dpost + R.zbr[d - 1].astype(F32)

            @pl.when(lax.div(flip(r, d), 2) == head)
            def _():
                kv_hop(d).wait_recv()
                dkv[...] = dkv[...] + R.zkr[d - 1].astype(F32)

        br = R.br
        pre = br[13 : 13 + n, 0:128] * R.wcs[0:1]
        for j in (1, 2, 3):
            pre = pre + br[13 + j : 13 + j + n, 0:128] * R.wcs[j : j + 1]
        sig = sigmoid(pre)
        dpre = dpost * sig * (1.0 + pre * (1.0 - sig))
        dbc = dpre[3 : 3 + BLK] * R.wcs[0:1]
        for j in (1, 2, 3):
            dbc = dbc + dpre[3 - j : 3 - j + BLK] * R.wcs[j : j + 1]
        R.db[:, 0:128] = dbc.astype(BF)
        for j in range(4):
            R.dstates[j : j + 1] = jnp.sum(dpre[0:BLK] * br[13 + j : 13 + j + BLK, 0:128], axis=0, keepdims=True)
        R.out[...] = (R.x1[...] + close_d()).astype(BF)
        dkv_v = dkv[...]
        R.db[:, 384:512] = jnp.where(kind == 0, rope_turn(dkv_v, cos, -sin), dkv_v).astype(BF)
        for d in (1, 2, 3):
            bc_hop(d).wait_send()

            @pl.when(lax.rem(flip(r, d), 2) == kind)
            def _():
                kv_hop(d).wait_send()

        for one, theirs, out in zip(y_hops, (R.yy.A, R.yy.B, R.yy.C), (R.down_p, R.out_p, R.attn_p) if y_hops else ()):
            one.wait_recv()
            out[...] = theirs[...]
            one.wait_send()

    scratch = dict(
        n=grid_scratch(),
        s=srows_scratch(),
        yy=pair_scratch((LEN, 512), (SIDE * HW, 512), (256, 512)),
        t=tokens_scratch(6, n, 128, low=BF),
        xpad=pltpu.VMEM((LEN + 8, HW), F32),
        dpre=pltpu.VMEM((LEN + 8, HW), F32),
        dstate=pltpu.VMEM((STATE, HW), F32),
        dskip=pltpu.VMEM((1, HW), F32),
        tb=pltpu.VMEM((6, LEN + HALO, 128), F32),
        tob=pltpu.VMEM((6, n, 128), BF),
        mine=pltpu.VMEM((6, n, 128), F32),
        dkv=pltpu.VMEM((BLK, 128), F32),
        zbr=pltpu.VMEM((3, n, 128), BF),
        zkr=pltpu.VMEM((3, BLK, 128), BF),
        zs=dma(3),
        zr=dma(3),
        ys=dma(3),
        yr=dma(3),
    )
    outs = dict(
        da=((LEN, 2 * HW), BF),
        db=((BLK, 512), BF),
        ds=((16, LEN), BF),
        dgain=((1, HW), F32),
        dconv=((4, HW), F32),
        dstates=((4, 128), F32),
        dhead=((8, 128), F32),
        out=((BLK, 512), BF),
    )
    if paired():
        outs.update(down_p=((LEN, 512), BF), out_p=((SIDE * HW, 512), BF), attn_p=((256, 512), BF))
    ins = dict(dm=dm, do=do, z=z, xr=xr, br=br, sr=sr, y=y, s3=s3, states=states, g=g, qr=qr, lse=lse, wc=wc, wcs=wcs)
    ins.update(gain=gain, cos=cosine, sin=sine, x1=x1, down=down, down_w=down_w, out_w=out_w, attn_w=attn_w)
    return launch(mixers_back, ins, outs, scratch, 10, dict(bias=bias, decay=decay, skip=skip))


def dp_total(own, theirs):
    if theirs is not None:
        return own.astype(F32) + theirs.astype(F32)
    return lax.psum(own.astype(F32), "dp")


def on_device(
    block_input,
    mixer_gain,
    ssm_gate_weight,
    ssm_input_weight,
    ssm_bc_weight,
    ssm_step_weight,
    query_weight,
    keyval_weight,
    conv_input,
    conv_states,
    step_bias,
    decay_log,
    skip_gain,
    ssm_norm_gain,
    ssm_out_weight,
    attn_out_weight,
    ffn_gain,
    gate_up_weight,
    down_weight,
    cotangent,
):
    cosine, sine = (jnp.asarray(table) for table in rope_tables())
    step_w = jnp.pad(ssm_step_weight.T.reshape(SIDE, HH, -1), ((0, 0), (0, 16 - HH), (0, 0))).reshape(16 * SIDE, -1)
    wg, wu = gate_up_weight[:, 0], gate_up_weight[:, 1]
    mixer_row, ffn_row, ssm_row = mixer_gain[None], ffn_gain[None], ssm_norm_gain[None]
    wo, wt, wd = ssm_out_weight, attn_out_weight, down_weight

    p = project_kernel(
        block_input,
        mixer_row,
        ssm_gate_weight,
        ssm_input_weight,
        ssm_bc_weight,
        query_weight,
        keyval_weight,
        step_w,
        conv_states,
    )
    heads = (conv_input, p.wcs, step_bias, decay_log, skip_gain, ssm_row, cosine, sine)
    m = mixers_kernel(p.z, p.xr, p.br, p.sr, *heads, cotangent, wd)
    f = forward_kernel(m.m, m.o, block_input, ffn_row, wo, wt, wg, wu, m.dh)
    b = backward_kernel(
        f.dgu, wg, wu, f.x1, f.s2, ffn_row, cotangent, f.n2_all, wo, wt, f.hid, wd, m.dy, f.m_all, f.o_all
    )
    mixed = (p.z, p.xr, p.br, p.sr, m.y, m.s3, m.states, m.g_o, m.qr, m.lse)
    k = mixers_back_kernel(b.dm, b.do, *mixed, *heads, f.x1, b.down, b.down_w, b.out_w, b.attn_w)
    q = project_back_kernel(
        k.da,
        k.db,
        k.ds,
        p.wa_o,
        p.wb_o,
        step_w,
        block_input,
        p.s1,
        mixer_row,
        b.dx1,
        p.n1,
        b.dgain,
        k.dconv,
        k.dgain,
        k.dhead,
        k.dstates,
    )
    pair = paired()
    gate_grad = dp_total(b.gate_w, b.gate_p if pair else None)
    up_grad = dp_total(b.up_w, b.up_p if pair else None)
    down_grad = dp_total(b.down_w, k.down_p if pair else None)
    out_grad = dp_total(b.out_w, k.out_p if pair else None)
    attn_grad = dp_total(b.attn_w, k.attn_p if pair else None)
    z_grad = dp_total(q.zo, q.zq if pair else None)
    x_grad = dp_total(q.xo, q.xq if pair else None)
    b_grad = dp_total(q.bo, q.bq if pair else None)
    step_grad = dp_total(q.so, q.sq if pair else None)
    step_grad = step_grad.reshape(SIDE, 16, -1)[:, :HH].reshape(SIDE * HH, -1).T
    small = [q.o_mixer[0], q.o_conv, q.o_states, q.o_bias[0], q.o_decay[0], q.o_skip[0], q.o_gain[0], q.o_ffn[0]]
    if not pair:
        small = lax.psum(small, "dp")
    return (
        k.out,
        q.dx,
        small[0],
        z_grad,
        x_grad,
        b_grad[:, 0:128],
        step_grad,
        b_grad[:, 128:384],
        b_grad[:, 384:512],
        *small[1:7],
        out_grad,
        attn_grad,
        small[7],
        jnp.stack([gate_grad, up_grad], axis=1),
        down_grad,
    )


def solution(mesh):
    placed = (
        P(("dp", "row"), "col"),
        P("col"),
        P("col", "row"),
        P("col", "row"),
        P("col", "row"),
        P("col", "row"),
        P("col", "row"),
        P("col", "row"),
        P(None, ("row", "col")),
        P(None, ("row", "col")),
        P(("row", "col")),
        P(("row", "col")),
        P(("row", "col")),
        P(("row", "col")),
        P("row", "col"),
        P("row", "col"),
        P("col"),
        P("col", None, "row"),
        P("row", "col"),
        P(("dp", "row"), "col"),
    )
    return jax.shard_map(
        on_device,
        mesh=mesh,
        in_specs=placed,
        out_specs=(
            P(("dp", "row"), "col"),
            P(("dp", "row"), "col"),
            P("col"),
            P("col", "row"),
            P("col", "row"),
            P("col", "row"),
            P("col", "row"),
            P("col", "row"),
            P("col", "row"),
            P(None, ("row", "col")),
            P(None, ("row", "col")),
            P(("row", "col")),
            P(("row", "col")),
            P(("row", "col")),
            P(("row", "col")),
            P("row", "col"),
            P("row", "col"),
            P("col"),
            P("col", None, "row"),
            P("row", "col"),
        ),
        check_vma=False,
    )
```

```python
import types

import jax
import jax.numpy as jnp
import numpy as np
from jax import lax
from jax.experimental import pallas as pl
from jax.experimental.pallas import tpu as pltpu
from jax.sharding import PartitionSpec as P

D = 2048
HEADS = 48
HDIM = 64
STATE = 256
ADIM = 128
LEN = 1024
SPAN = 256
SIDE = 4
BLK = LEN // SIDE
HALO = 16
HH = 3
HW = HH * HDIM
EPSILON = 1e-05
ROPE_BASE = 100000000000.0
HIGHEST = lax.Precision.HIGHEST
NEGATIVE = -1e30
LETTERS = "abcd"
BF = jnp.bfloat16
F32 = jnp.float32
MESH = pl.DeviceIdType.MESH
SCALE = ADIM ** (-0.5)


def dot_nn(a, b, precision=None):
    return lax.dot_general(a, b, (((1,), (0,)), ((), ())), precision=precision, preferred_element_type=F32)


def dot_nt(a, b, precision=None):
    return lax.dot_general(a, b, (((1,), (1,)), ((), ())), precision=precision, preferred_element_type=F32)


def dot_tn(a, b, precision=None):
    return lax.dot_general(a, b, (((0,), (0,)), ((), ())), precision=precision, preferred_element_type=F32)


def halves(v):
    high = v.astype(BF)
    return high, (v - high.astype(F32)).astype(BF)


def fine(dot, a, b):
    a = a if isinstance(a, tuple) else (a,)
    b = b if isinstance(b, tuple) else (b,)
    total = dot(a[0], b[0])
    if len(b) > 1:
        total = total + dot(a[0], b[1])
    if len(a) > 1:
        total = total + dot(a[1], b[0])
    return total


def sigmoid(v):
    return 1.0 / (1.0 + jnp.exp(-v))


def softplus(v):
    return jnp.maximum(v, 0.0) + jnp.log1p(jnp.exp(-jnp.abs(v)))


def iota(shape, axis):
    return lax.broadcasted_iota(jnp.int32, shape, axis)


def flip(v, d):
    v0, v1 = lax.rem(v, 2), lax.div(v, 2)
    if isinstance(d, int):
        d0, d1 = d % 2, d // 2
    else:
        d0, d1 = lax.rem(d, 2), lax.div(d, 2)
    return 2 * (v1 + d1 - 2 * v1 * d1) + (v0 + d0 - 2 * v0 * d0)


def here():
    return lax.axis_index("row"), lax.axis_index("col")


def greet(r, c, rows=False, cols=(), grid=False, dp=False):
    sem = pltpu.get_barrier_semaphore()
    peers = []
    if grid:
        for d in range(SIDE):
            for e in range(SIDE):
                if d or e:
                    peers.append({"row": flip(r, d), "col": flip(c, e)})
    else:
        if rows:
            peers += [{"row": flip(r, d)} for d in (1, 2, 3)]
        peers += [{"col": flip(c, e)} for e in cols]
    if dp:
        peers.append({"dp": 1 - lax.axis_index("dp")})
    for peer in peers:
        pl.semaphore_signal(sem, inc=1, device_id=peer, device_id_type=MESH)
    pl.semaphore_wait(sem, len(peers))


def hop(src, dst, ssem, rsem, **where):
    return pltpu.make_async_remote_copy(
        src_ref=src, dst_ref=dst, send_sem=ssem, recv_sem=rsem, device_id=where, device_id_type=MESH
    )


def rows_at(ref, block, pad=0):
    return ref.at[pl.ds(pl.multiple_of(block * BLK + pad, 16), BLK)]


def dma(*shape):
    return pltpu.SemaphoreType.DMA(shape)


def launch(body, ins, outs, scratch, cid, smem=None, late=None, early=None):
    smem, late, early = smem or {}, late or {}, early or {}
    shapes = [pltpu.VMEM(v.shape, v.dtype) for v in late.values()]
    shapes += [dma(max(len(late), 1)), dma(max(len(early), 1))]
    for item in scratch.values():
        shapes += list(item.values()) if isinstance(item, dict) else [item]

    def kernel(*refs):
        refs = list(refs)
        found = {}
        for key in (*ins, *smem):
            found[key] = refs.pop(0)
        sources = [refs.pop(0) for _ in late]
        for key in (*outs, *early):
            found[key] = refs.pop(0)
        places = [refs.pop(0) for _ in late]
        late_sems, early_sems = refs.pop(0), refs.pop(0)
        incoming, outgoing = [], []
        for k, (key, src, dst) in enumerate(zip(late, sources, places)):
            found[key] = dst
            incoming.append((dst, pltpu.make_async_copy(src, dst, late_sems.at[k])))
            incoming[-1][1].start()
        for key, item in scratch.items():
            if isinstance(item, dict):
                found[key] = types.SimpleNamespace(**{name: refs.pop(0) for name in item})
            else:
                found[key] = refs.pop(0)

        def arrive(*wanted):
            for one in wanted:
                for k, (dst, copy) in enumerate(incoming):
                    if dst is one:
                        copy.wait()
                        del incoming[k]
                        break

        def leave(dst, src):
            outgoing.append(pltpu.make_async_copy(src, dst, early_sems.at[len(outgoing)]))
            outgoing[-1].start()

        body(types.SimpleNamespace(arrive=arrive, leave=leave, **found))
        for _, copy in incoming:
            copy.wait()
        for copy in outgoing:
            copy.wait()

    vector = pl.BlockSpec(memory_space=pltpu.VMEM)
    anywhere = pl.BlockSpec(memory_space=pl.ANY)
    results = pl.pallas_call(
        kernel,
        out_shape=[jax.ShapeDtypeStruct(*o) for o in (*outs.values(), *early.values())],
        in_specs=[vector] * len(ins)
        + [pl.BlockSpec(memory_space=pltpu.SMEM)] * len(smem)
        + [anywhere] * len(late),
        out_specs=[vector] * len(outs) + [anywhere] * len(early),
        scratch_shapes=shapes,
        compiler_params=pltpu.CompilerParams(
            collective_id=cid, has_side_effects=True, vmem_limit_bytes=58 << 20
        ),
        name=body.__name__,
    )(*ins.values(), *smem.values(), *late.values())
    return types.SimpleNamespace(**dict(zip((*outs, *early), results)))


def rows_scratch(padded=False):
    size = LEN + 2 * HALO if padded else LEN
    return dict(g=pltpu.VMEM((size, D // SIDE), BF), zs=dma(SIDE), zr=dma(3))


def inner(r):
    return lax.rem(r, 3) != 0


def swapped(i):
    return 2 * lax.rem(i, 2) + lax.div(i, 2)


def row_hop(S, r, d, pad=0):
    own = rows_at(S.g, r, pad)
    return hop(own, own, S.zs.at[d - 1], S.zr.at[d - 1], row=flip(r, d))


def pass_hop(S, r, pad=0):
    part = rows_at(S.g, flip(r, 2), pad)
    return hop(part, part, S.zs.at[3], S.zr.at[2], row=flip(r, 1))


def gather_rows(S, r, pad=0):
    row_hop(S, r, 2, pad).start()
    row_hop(S, r, 1, pad).start()

    @pl.when(inner(r))
    def _():
        row_hop(S, r, 3, pad).start()


def wait_rows(S, r, d, pad=0):
    part = rows_at(S.g, flip(r, d), pad)
    hop(part, part, S.zs.at[d - 1], S.zr.at[d - 1], row=flip(r, d)).wait_recv()

    @pl.when(jnp.logical_and(d == 2, inner(r)))
    def _():
        pass_hop(S, r, pad).start()


def wait_rows_sent(S, r, pad=0):
    row_hop(S, r, 2, pad).wait_send()
    row_hop(S, r, 1, pad).wait_send()

    @pl.when(inner(r))
    def _():
        row_hop(S, r, 3, pad).wait_send()
        pass_hop(S, r, pad).wait_send()


def cols_scratch(w):
    return dict(
        cs=pltpu.VMEM((SIDE, 2, BLK, w), F32),
        cr=pltpu.VMEM((SIDE, 2, BLK, w), F32),
        xs=pltpu.VMEM((SIDE, BLK, w), BF),
        xr=pltpu.VMEM((SIDE, BLK, w), BF),
        acc=pltpu.VMEM((SIDE, BLK, w), F32),
        mine=pltpu.VMEM((SIDE, BLK, w), F32),
        ks=dma(SIDE),
        kr=dma(SIDE),
        ss=dma(SIDE),
        sr=dma(SIDE),
    )


def scatter_cols(S, G, r, c, product, finish, pad=0, moving=True):
    cs, cr, xs, xr, acc = (S.cs, S.cr, S.xs, S.xr, S.acc)

    def core_hop(d):
        return hop(cs.at[d], cr.at[d], S.ks.at[d], S.kr.at[d], col=flip(c, 1))

    def x_hop(d):
        return hop(xs.at[d], xr.at[d], S.ss.at[d], S.sr.at[d], col=flip(c, 2))

    def first(i):
        d = swapped(i)

        if moving:

            @pl.when(i > 0)
            def _():
                wait_rows(G, r, d, pad)

        rows = rows_at(G.g, flip(r, d), pad)[...]
        cs[d, 1] = product(rows, flip(c, 3))
        cs[d, 0] = product(rows, flip(c, 1))
        core_hop(d).start()
        S.mine[d] = product(rows, flip(c, 2))
        acc[d] = product(rows, c)

    def second(i):
        d = swapped(i)
        core_hop(d).wait_recv()
        xs[d] = (S.mine[d] + cr[d, 1]).astype(BF)
        x_hop(d).start()
        acc[d] = acc[d] + cr[d, 0]

    def end(i):
        d = swapped(i)
        x_hop(d).wait_recv()
        finish(flip(r, d), acc[d] + xr[d].astype(F32))

    def sent(i):
        x_hop(swapped(i)).wait_send()
        core_hop(swapped(i)).wait_send()

    def before(i):
        @pl.when(i > 0)
        def _():
            end(i - 1)

    def close():
        end(SIDE - 1)
        each(sent)

    return first, second, before, close


def each(*phases):
    def step(i, carry):
        for phase in phases:
            phase(i)
        return carry

    lax.fori_loop(0, SIDE, step, 0)


def tokens_scratch(*shape, low=F32):
    return dict(
        cs=pltpu.VMEM((2, *shape), low),
        cr=pltpu.VMEM((2, *shape), low),
        xs=pltpu.VMEM(shape, low),
        xr=pltpu.VMEM(shape, low),
        acc=pltpu.VMEM(shape, F32),
        ks=dma(),
        kr=dma(),
        ss=dma(),
        sr=dma(),
    )


def scatter_tokens(S, c, product):
    low = S.xs.dtype
    core = hop(S.cs, S.cr, S.ks, S.kr, col=flip(c, 1))
    over = hop(S.xs, S.xr, S.ss, S.sr, col=flip(c, 2))
    S.cs[1] = product(flip(c, 3)).astype(low)
    S.cs[0] = product(flip(c, 1)).astype(low)
    core.start()
    mine = product(flip(c, 2))
    S.acc[...] = product(c)
    core.wait_recv()
    S.xs[...] = (mine + S.cr[1].astype(F32)).astype(low)
    over.start()
    S.acc[...] = S.acc[...] + S.cr[0].astype(F32)

    def close():
        over.wait_recv()
        total = S.acc[...] + S.xr[...].astype(F32)
        over.wait_send()
        core.wait_send()
        return total

    return close


def trio_scratch():
    return dict(xs=dma(), xr=dma(), ks=dma(), kr=dma(), fs=dma(), fr=dma())


def trio(S, c, part):
    own, over = part(c), part(flip(c, 2))
    return (
        hop(own, own, S.xs, S.xr, col=flip(c, 2)),
        hop(own, own, S.ks, S.kr, col=flip(c, 1)),
        hop(over, over, S.fs, S.fr, col=flip(c, 1)),
    )


def trio_end(hops):
    over, core, forward = hops
    over.wait_recv()
    forward.start()
    core.wait_recv()
    forward.wait_recv()


def gcols_scratch(w):
    return dict(
        g=pltpu.VMEM((SIDE, LEN, w), BF),
        xs=dma(SIDE),
        xr=dma(SIDE),
        ks=dma(SIDE),
        kr=dma(SIDE),
        fs=dma(SIDE),
        fr=dma(SIDE),
    )


def col_part(S, j, t):
    return S.g.at[j, pl.ds(pl.multiple_of(t * BLK, BLK), BLK)]


def col_hop(S, c, kind, t, d):
    part = col_part(S, flip(c, 2) if kind == "f" else c, t)
    to = flip(c, 2) if kind == "x" else flip(c, 1)
    return hop(part, part, getattr(S, kind + "s").at[d], getattr(S, kind + "r").at[d], col=to)


def gather_cols(S, r, c, order=(3, 1, 2, 0)):
    for d in order:
        t = flip(r, d)
        col_hop(S, c, "x", t, d).start()
        col_hop(S, c, "k", t, d).start()


def wait_cols(S, r, c, d):
    t = flip(r, d)
    col_hop(S, c, "x", t, d).wait_recv()
    col_hop(S, c, "f", t, d).start()
    col_hop(S, c, "k", t, d).wait_recv()
    col_hop(S, c, "f", t, d).wait_recv()


def wait_cols_sent(S, r, c):
    def step(d, carry):
        t = flip(r, d)
        for kind in "xkf":
            col_hop(S, c, kind, t, d).wait_send()
        return carry

    lax.fori_loop(0, SIDE, step, 0)


def srows_scratch():
    w = D // SIDE
    return dict(
        ps=pltpu.VMEM((3, BLK, w), BF),
        pr=pltpu.VMEM((3, BLK, w), BF),
        fr=pltpu.VMEM((BLK, w), BF),
        pa=pltpu.VMEM((BLK, w), F32),
        rs=dma(3),
        rr=dma(3),
        frs=dma(),
    )


def scatter_rows(S, r, product, ready):
    ps, pr, acc = S.ps, S.pr, S.pa

    def direct(d):
        return hop(ps.at[d - 1], pr.at[d - 1], S.rs.at[d - 1], S.rr.at[d - 1], row=flip(r, d))

    def aside():
        return hop(ps.at[2], S.fr, S.rs.at[2], S.frs, row=flip(r, 1))

    def step(i):
        d = 3 - swapped(i)
        ready(d)
        acc[...] = product(flip(r, d))

        @pl.when((d == 2) & inner(r))
        def _():
            aside().wait_recv()
            acc[...] = acc[...] + S.fr[...].astype(F32)

        @pl.when(d > 0)
        def _():
            ps[d - 1] = acc[...].astype(BF)

        @pl.when((d == 3) & jnp.logical_not(inner(r)))
        def _():
            aside().start()

        @pl.when((d > 0) & ((d < 3) | inner(r)))
        def _():
            direct(d).start()

    def close():
        for d in (1, 2):
            direct(d).wait_recv()
            acc[...] = acc[...] + pr[d - 1].astype(F32)

        @pl.when(inner(r))
        def _():
            direct(3).wait_recv()
            acc[...] = acc[...] + pr[2].astype(F32)

        for d in (1, 2, 3):
            direct(d).wait_send()
        return acc[...]

    return step, close


def pair_scratch(*shapes):
    found = dict(ss=dma(len(shapes)), sr=dma(len(shapes)))
    for k, shape in enumerate(shapes):
        found[LETTERS[k]] = pltpu.VMEM(shape, BF)
        found[LETTERS[k].upper()] = pltpu.VMEM(shape, BF)
    return found


def pair_hop(S, k, own=None, rows=None):
    src = getattr(S, LETTERS[k]) if own is None else own
    dst = getattr(S, LETTERS[k].upper())
    if rows is not None:
        src, dst = src.at[rows], dst.at[rows]
    return hop(src, dst, S.ss.at[k], S.sr.at[k], dp=1 - lax.axis_index("dp"))


def paired():
    return lax.axis_size("dp") == 2


def row_sums(v):
    return dot_nt(jnp.ones((8, v.shape[1]), F32), v, HIGHEST)


def stat_scratch():
    return dict(st=pltpu.VMEM((SIDE, 8, BLK), F32), sts=dma(3), str=dma(3))


def col_sum(S, c, v):
    st = S.st
    st[c] = v
    hops = [
        hop(st.at[c], st.at[c], S.sts.at[e - 1], S.str.at[e - 1], col=flip(c, e)) for e in (1, 2, 3)
    ]
    for one in hops:
        one.start()
    for one in hops:
        one.wait_recv()
    total = (st[0] + st[1]) + (st[2] + st[3])
    for one in hops:
        one.wait_send()
    return total


def grid_scratch():
    return dict(st=pltpu.VMEM((SIDE, SIDE, 8, BLK), F32), sts=dma(16), str=dma(16))


def grid_sum(S, r, c):
    st = S.st
    hops = []
    for d in range(SIDE):
        for e in range(SIDE):
            if d or e:
                k = SIDE * d + e
                hops.append(
                    hop(
                        st.at[r, c],
                        st.at[r, c],
                        S.sts.at[k],
                        S.str.at[k],
                        row=flip(r, d),
                        col=flip(c, e),
                    )
                )
    for one in hops:
        one.start()

    def close():
        for one in hops:
            one.wait_recv()
        total = jnp.zeros((8, BLK), F32)
        for d in range(SIDE):
            for e in range(SIDE):
                total = total + st[d, e]
        for one in hops:
            one.wait_send()
        return total

    return close


def to_column(v):
    return jnp.transpose(v)[:, :1]


def pick_column(v, b):
    return jnp.sum(jnp.where(iota(v.shape, 1) == b, v, 0.0), axis=1, keepdims=True)


def cut(v, j, w):
    return v[:, j * w : (j + 1) * w]


def cut(v, j, w):
    return v[:, j * w : (j + 1) * w]


def project_kernel(x, gain, wz, wx, wbc, wq, wkv, ws, cw, cot):
    def project(R):
        r, c = here()
        greet(r, c, rows=True, cols=(1, 2, 3))
        tap_hops = [
            hop(R.taps.at[c], R.taps.at[c], R.tss.at[e - 1], R.tsr.at[e - 1], col=flip(c, e)) for e in (1, 2, 3)
        ]
        R.taps[c] = jnp.zeros((8, 128), F32)
        R.taps[c, 0:4, 0:32] = R.cw[...]
        for one in tap_hops:
            one.start()
        x = R.x[...].astype(F32)
        total = col_sum(R.n, c, row_sums(x * x))
        scale = to_column(lax.rsqrt(total / D + EPSILON))
        g = R.p.g
        g[pl.ds(0, HALO)] = jnp.zeros((HALO, D // SIDE), BF)
        g[pl.ds(LEN + HALO, HALO)] = jnp.zeros((HALO, D // SIDE), BF)
        rows_at(g, r, HALO)[...] = (x * scale * R.gain[...]).astype(BF)
        gather_rows(R.p, r, HALO)
        wa, wb = R.wa, R.wb
        R.arrive(R.wz, R.wx, R.wbc, R.wq, R.wkv)
        for j in range(SIDE):
            wa[j, :, 0:HW] = cut(R.wz, j, HW)
            wa[j, :, HW : 2 * HW] = cut(R.wx, j, HW)
        wb[:, 0:128] = R.wbc[...]
        wb[:, 128:384] = R.wq[...]
        wb[:, 384:512] = R.wkv[...]
        R.leave(R.wb_o, wb)

        def finish(block, v):
            at = pl.ds(pl.multiple_of(block * BLK, BLK), BLK)
            R.zs[at] = v[:, 0:HW]
            R.xs[at] = v[:, HW : 2 * HW]

        first, second, before, close_a = scatter_cols(R.a, R.p, r, c, lambda rows, j: dot_nn(rows, wa[j]), finish, HALO)
        each(first, second, before)
        R.leave(R.n1, g.at[pl.ds(HALO, LEN)])
        R.arrive(R.cot)
        rows_at(R.h.g, r)[...] = R.cot[...].astype(BF)
        gather_rows(R.h, r)
        R.arrive(R.ws)
        steps = dot_nt(R.ws[...], g[pl.ds(HALO, LEN)])
        for j in range(SIDE):
            R.ps[j] = steps[16 * j : 16 * j + 8]
        step_hops = [
            hop(
                R.ps.at[flip(c, e)],
                R.pr.at[e - 1],
                R.pss.at[e - 1],
                R.psr.at[e - 1],
                col=flip(c, e),
            )
            for e in (1, 2, 3)
        ]
        for one in step_hops:
            one.start()

        def token_rows(j):
            return dot_nn(g[pl.ds(pl.multiple_of(j * BLK, BLK), BLK + 2 * HALO)], wb[...])

        close_b = scatter_tokens(R.b, c, token_rows)
        R.s1[...] = total
        wait_rows(R.h, r, 2)
        close_a()
        R.leave(R.z, R.zs)
        R.leave(R.xr, R.xs)
        for one in step_hops:
            one.wait_recv()
        R.sr[...] = (R.ps[c] + R.pr[0]) + (R.pr[1] + R.pr[2])
        for one in step_hops:
            one.wait_send()
        R.br[...] = close_b()
        for one in tap_hops:
            one.wait_recv()
        R.wcs[...] = jnp.concatenate([R.taps[j, 0:4, 0:32] for j in range(SIDE)], axis=1)
        for one in tap_hops:
            one.wait_send()
        wait_rows(R.h, r, 1)
        wait_rows(R.h, r, 3)
        R.leave(R.dy, R.h.g)
        wait_rows_sent(R.p, r, HALO)
        wait_rows_sent(R.h, r)

    n = BLK + 2 * HALO
    scratch = dict(
        p=rows_scratch(True),
        h=rows_scratch(),
        n=stat_scratch(),
        a=cols_scratch(2 * HW),
        b=tokens_scratch(n, 512),
        wa=pltpu.VMEM((SIDE, 512, 2 * HW), BF),
        wb=pltpu.VMEM((512, 512), BF),
        ps=pltpu.VMEM((SIDE, 8, LEN), F32),
        pr=pltpu.VMEM((3, 8, LEN), F32),
        pss=dma(3),
        psr=dma(3),
        taps=pltpu.VMEM((SIDE, 8, 128), F32),
        zs=pltpu.VMEM((LEN, HW), F32),
        xs=pltpu.VMEM((LEN, HW), F32),
        tss=dma(3),
        tsr=dma(3),
    )
    outs = dict(s1=((8, BLK), F32), br=((n, 512), F32), sr=((8, LEN), F32), wcs=((4, 128), F32))
    early = dict(
        n1=((LEN, 512), BF),
        z=((LEN, HW), F32),
        xr=((LEN, HW), F32),
        dy=((LEN, 512), BF),
        wb_o=((512, 512), BF),
    )
    ins = dict(x=x, gain=gain, cw=cw)
    late = dict(wz=wz, wx=wx, wbc=wbc, wq=wq, wkv=wkv, ws=ws, cot=cot)
    return launch(project, ins, outs, scratch, 1, late=late, early=early)


SMALL = 32


def forward_kernel(m, o, x, gain, wo, wt, wg, wu, dh):
    def forward(R):
        r, c = here()
        greet(r, c, rows=True, cols=(1, 2, 3))
        R.mc.g[c] = R.m[...]
        og = R.og
        og[c] = R.o[...]
        o_hops = trio(R.ot, c, lambda j: og.at[j])
        o_hops[0].start()
        o_hops[1].start()
        gather_cols(R.mc, r, c)
        R.arrive(R.wo, R.wt)
        trio_end(o_hops)

        def product(t):
            total = dot_nn(og[t], R.wt[...])
            for j in range(SIDE):
                total = total + dot_nn(col_part(R.mc, j, t)[...], R.wo[j * HW : (j + 1) * HW])
            return total

        step, close = scatter_rows(R.s, r, product, lambda d: wait_cols(R.mc, r, c, d))
        each(step)
        R.leave(R.m_all, R.mc.g)
        R.leave(R.o_all, og)
        R.arrive(R.x, R.wg, R.wu, R.dh)
        x1 = R.x[...].astype(F32) + close()
        R.x1[...] = x1
        total = col_sum(R.n, c, row_sums(x1 * x1))
        R.s2[...] = total
        scale = to_column(lax.rsqrt(total / D + EPSILON))
        rows_at(R.p.g, r)[...] = (R.x1[...] * scale * R.gain[...]).astype(BF)
        gather_rows(R.p, r)

        def gate_up(rows, j):
            at = pl.ds(pl.multiple_of(j * BLK, BLK), BLK)
            return jnp.concatenate([dot_nn(rows, R.wg[:, at]), dot_nn(rows, R.wu[:, at])], axis=1)

        def finish(block, v):
            at = pl.ds(pl.multiple_of(block * BLK, BLK), BLK)
            gate, up = v[:, :256], v[:, 256:]
            sig = sigmoid(gate)
            act = gate * sig
            dh = R.dh[at]
            R.hid[at] = (act * up).astype(BF)
            R.dgu[at, 0:256] = (dh * up * sig * (1.0 + gate * (1.0 - sig))).astype(BF)
            R.dgu[at, 256:512] = (dh * act).astype(BF)

        first, second, before, close = scatter_cols(R.a, R.p, r, c, gate_up, finish)
        each(first, second, before)
        R.leave(R.n2_all, R.p.g)
        close()
        for one in o_hops:
            one.wait_send()
        wait_cols_sent(R.mc, r, c)
        wait_rows_sent(R.p, r)

    scratch = dict(
        mc=gcols_scratch(HW),
        s=srows_scratch(),
        n=stat_scratch(),
        og=pltpu.VMEM((SIDE, BLK, 256), BF),
        ot=trio_scratch(),
        p=rows_scratch(),
        a=cols_scratch(512),
    )
    outs = dict(x1=((BLK, 512), F32), s2=((8, BLK), F32), hid=((LEN, 256), BF), dgu=((LEN, 512), BF))
    early = dict(m_all=((SIDE, LEN, HW), BF), o_all=((SIDE, BLK, 256), BF), n2_all=((LEN, 512), BF))
    late = dict(wo=wo, wt=wt, x=x, wg=wg, wu=wu, dh=dh)
    return launch(forward, dict(m=m, o=o, gain=gain), outs, scratch, 3, late=late, early=early)


def norm_back(S, c, dn, v, scale, gain):
    gain_grad = jnp.sum(dn * v * scale, axis=0, keepdims=True)
    weighted = dn * gain
    total = col_sum(S, c, row_sums(weighted * v))
    inner = to_column(total)
    return scale * weighted - v * (scale * scale * scale * inner / D), gain_grad


def backward_kernel(dgu, wg, wu, x1, s2, gain, cot, n2, wo, wt, hid, wd, dy, m, o):
    def backward(R):
        r, c = here()
        greet(r, c, rows=True, cols=(1, 2, 3), dp=paired())
        R.gc.g[c] = R.dgu[...]
        gather_cols(R.gc, r, c)
        R.arrive(R.wg, R.wu)
        for j in range(SIDE):
            R.wgu[:, 512 * j : 512 * j + 256] = R.wg[:, 256 * j : 256 * j + 256]
            R.wgu[:, 512 * j + 256 : 512 * j + 512] = R.wu[:, 256 * j : 256 * j + 256]

        def product(t):
            parts = [col_part(R.gc, j, t)[...] for j in range(SIDE)]
            return dot_nt(jnp.concatenate(parts, axis=1), R.wgu[...])

        step, close = scatter_rows(R.s, r, product, lambda d: wait_cols(R.gc, r, c, d))
        each(step)
        R.arrive(R.hid, R.n2)
        R.hc.g[c] = R.hid[...]
        gather_cols(R.hc, r, c)

        def grads(j):
            at = pl.ds(pl.multiple_of(j * BLK, BLK), BLK)
            both = dot_tn(R.n2[...], R.gc.g[j])
            R.y.a[:, at] = both[:, :256].astype(BF)
            R.y.b[:, at] = both[:, 256:].astype(BF)

        each(grads)
        y_hops = []
        if paired():
            y_hops = [pair_hop(R.y, 0), pair_hop(R.y, 1, R.y.b.at[pl.ds(0, 256)])]
        for one in y_hops:
            one.start()
        R.leave(R.gate_w, R.y.a)
        R.leave(R.up_w, R.y.b)
        R.arrive(R.x1, R.cot)
        dn = close()
        scale = to_column(lax.rsqrt(R.s2[...] / D + EPSILON))
        dv, dgain = norm_back(R.n, c, dn, R.x1[...], scale, R.gain[...])
        dx1 = R.cot[...] + dv
        rows_at(R.p.g, r)[...] = dx1.astype(BF)
        gather_rows(R.p, r)
        R.dx1[...] = dx1
        R.dgain[...] = dgain

        R.arrive(R.wd, R.dy)

        def down(i):
            wait_cols(R.hc, r, c, 3 - swapped(i))
            t = flip(r, 3 - swapped(i))
            total = dot_nn(col_part(R.hc, 0, t)[...], R.wd[0:256])
            for j in (1, 2, 3):
                total = total + dot_nn(col_part(R.hc, j, t)[...], R.wd[256 * j : 256 * j + 256])
            R.down_s[t] = total

        each(down)

        def down_grads(j):
            R.down_ws[pl.ds(pl.multiple_of(j * BLK, BLK), BLK)] = dot_tn(R.hc.g[j], R.dy[...]).astype(BF)

        each(down_grads)
        R.leave(R.down, R.down_s)
        R.leave(R.down_w, R.down_ws)
        R.arrive(R.wo, R.wt)

        def out_back(rows, j):
            return dot_nt(rows, R.wo[pl.ds(pl.multiple_of(j * HW, 64), HW)])

        def finish(block, v):
            R.dm[pl.ds(pl.multiple_of(block * BLK, BLK), BLK)] = v

        first, second, before, close_a = scatter_cols(R.a, R.p, r, c, out_back, finish)
        each(first, second, before)
        close_b = scatter_tokens(R.b, c, lambda j: dot_nt(rows_at(R.p.g, j)[...], R.wt[...]))

        R.arrive(R.m, R.o)

        def out_grads(j):
            R.out_ws[pl.ds(pl.multiple_of(j * HW, 64), HW)] = dot_tn(R.m[j], R.p.g[...]).astype(BF)

        each(out_grads)
        R.leave(R.out_w, R.out_ws)
        R.attn_w[...] = dot_tn(R.o[...].reshape(LEN, 256), R.p.g[...]).astype(BF)
        close_a()
        R.do[...] = close_b().astype(BF)
        wait_cols_sent(R.gc, r, c)
        wait_cols_sent(R.hc, r, c)
        wait_rows_sent(R.p, r)
        for one, theirs, out in zip(y_hops, (R.y.A, R.y.B), (R.gate_p, R.up_p) if y_hops else ()):
            one.wait_recv()
            R.leave(out, theirs)
            one.wait_send()

    scratch = dict(
        gc=gcols_scratch(512),
        hc=gcols_scratch(256),
        s=srows_scratch(),
        n=stat_scratch(),
        p=rows_scratch(),
        a=cols_scratch(HW),
        b=tokens_scratch(BLK, 256, low=BF),
        y=dict(pair_scratch((512, 1024), (256, 1024)), b=pltpu.VMEM((512, 1024), BF)),
        wgu=pltpu.VMEM((512, 2048), BF),
        down_s=pltpu.VMEM((SIDE, BLK, 512), F32),
        down_ws=pltpu.VMEM((LEN, 512), BF),
        out_ws=pltpu.VMEM((SIDE * HW, 512), BF),
    )
    outs = dict(
        dx1=((BLK, 512), F32),
        dgain=((1, 512), F32),
        dm=((LEN, HW), F32),
        do=((BLK, 256), BF),
        attn_w=((256, 512), BF),
    )
    early = dict(
        gate_w=((512, 1024), BF),
        up_w=((512, 1024), BF),
        down=((SIDE, BLK, 512), F32),
        down_w=((LEN, 512), BF),
        out_w=((SIDE * HW, 512), BF),
    )
    if paired():
        early.update(gate_p=((512, 1024), BF), up_p=((256, 1024), BF))
    late = dict(wg=wg, wu=wu, hid=hid, n2=n2, x1=x1, cot=cot, wd=wd, dy=dy, wo=wo, wt=wt, m=m, o=o)
    return launch(backward, dict(dgu=dgu, s2=s2, gain=gain), outs, scratch, 6, late=late, early=early)


def project_back_kernel(
    da, db, ds, wz, wx, wb, ws, x, s1, gain, dx1, n1, ffn_grad, dconv, dgain, dhead, dstates, dz, z_w
):
    pair = paired()

    def project_back(R):
        r, c = here()
        greet(r, c, rows=True, cols=(1, 2, 3), dp=pair)
        R.ac.g[c] = R.da[...]
        bg, sg, tg = R.bg, R.sg, R.tg
        bg[c] = R.db[...]
        sg[c] = R.ds[...]
        tg[c] = jnp.zeros((8, 128), F32)
        tg[c, 0:4] = R.dstates[...]
        b_hops = trio(R.bt, c, lambda j: bg.at[j])
        s_hops = []
        for e in (1, 2, 3):
            to = flip(c, e)
            s_hops.append(hop(sg.at[c], sg.at[c], R.sgs.at[e - 1], R.sgr.at[e - 1], col=to))
            s_hops.append(hop(tg.at[c], tg.at[c], R.tgs.at[e - 1], R.tgr.at[e - 1], col=to))
        b_hops[0].start()
        b_hops[1].start()
        for one in s_hops:
            one.start()
        gather_cols(R.ac, r, c)

        y = R.y
        w_hops = []
        if pair:
            w_hops = [pair_hop(y, 0, R.z_w), *(pair_hop(y, k) for k in (1, 2, 3))]
            R.arrive(R.z_w)
            w_hops[0].start()

        trio_end(b_hops)
        for one in s_hops:
            one.wait_recv()
        R.arrive(R.n1, R.wb, R.wx, R.wz, R.ws, R.dz)
        y.b[...] = dot_tn(R.n1[...], bg[...].reshape(LEN, 512)).astype(BF)
        y.c[...] = dot_nn(sg[...].reshape(16 * SIDE, LEN), R.n1[...]).astype(BF)
        if pair:
            w_hops[1].start()
            w_hops[2].start()

        def product(t):
            at = pl.ds(pl.multiple_of(t * BLK, BLK), BLK)
            total = dot_nt(bg[t], R.wb[...]) + dot_nt(R.dz[at], R.wz[...])
            total = total + dot_tn(sg[:, :, at].reshape(16 * SIDE, BLK), R.ws[...])
            joined = jnp.concatenate([col_part(R.ac, j, t)[...] for j in range(SIDE)], axis=1)
            R.dx_all[at] = joined
            return total + dot_nt(joined, R.wx[...])

        step, close = scatter_rows(R.s, r, product, lambda d: wait_cols(R.ac, r, c, d))
        each(step)
        y.d[...] = dot_tn(R.n1[...], R.dx_all[...]).astype(BF)
        if pair:
            w_hops[3].start()
        for out, own in zip((R.bo, R.so, R.xo), (y.b, y.c, y.d)):
            R.leave(out, own)
        R.arrive(R.x, R.dx1)
        dn = close()
        scale = to_column(lax.rsqrt(R.s1[...] / D + EPSILON))
        dv, mixer_grad = norm_back(R.n, c, dn, R.x[...].astype(F32), scale, R.gain[...])
        gg = R.gg
        gg[r] = jnp.zeros((8, 512), F32)
        gg[r, 0:1] = mixer_grad
        gg[r, 1:2] = R.ffn_grad[...]
        g_hops = [hop(gg.at[r], gg.at[r], R.ggs.at[d - 1], R.ggr.at[d - 1], row=flip(r, d)) for d in (1, 2, 3)]
        for one in g_hops:
            one.start()
        R.dx[...] = R.dx1[...] + dv
        small = R.small
        small[...] = jnp.zeros((SMALL, 512), F32)
        small[8:12, 0:HW] = R.dconv[...]
        small[12:13, 0:HW] = R.dgain[...]
        small[16:24, 0:128] = R.dhead[...]
        small[24:32, 0:128] = (tg[0] + tg[1]) + (tg[2] + tg[3])
        for one in g_hops:
            one.wait_recv()
        small[0:8] = (gg[0] + gg[1]) + (gg[2] + gg[3])
        if pair:
            small_hop = hop(small, R.small_p, R.mss, R.msr, dp=1 - lax.axis_index("dp"))
            small_hop.start()
        for one in (*b_hops, *s_hops, *g_hops):
            one.wait_send()
        wait_cols_sent(R.ac, r, c)
        total = small[...]
        if pair:
            small_hop.wait_recv()
            total = total + R.small_p[...]
            small_hop.wait_send()
        R.o_mixer[...] = total[0:1]
        R.o_ffn[...] = total[1:2]
        R.o_conv[...] = total[8:12, 0:HW]
        R.o_gain[...] = total[12:13, 0:HW]
        heads = jnp.transpose(total[16:24, 0:128])
        R.o_bias[...] = heads[0:1, 0:HH]
        R.o_decay[...] = heads[1:2, 0:HH]
        R.o_skip[...] = heads[2:3, 0:HH]
        taps = jnp.zeros((4, 32), F32)
        for j in range(SIDE):
            taps = taps + jnp.where(c == j, total[24:28, 32 * j : 32 * j + 32], 0.0)
        R.o_states[...] = taps
        if pair:
            for one, theirs, out in zip(w_hops, (y.A, y.B, y.C, y.D), (R.zq, R.bq, R.sq, R.xq)):
                one.wait_recv()
                R.leave(out, theirs)
                one.wait_send()

    scratch = dict(
        ac=gcols_scratch(HW),
        dx_all=pltpu.VMEM((LEN, 768), BF),
        s=srows_scratch(),
        n=stat_scratch(),
        bt=trio_scratch(),
        bg=pltpu.VMEM((SIDE, BLK, 512), BF),
        sg=pltpu.VMEM((SIDE, 16, LEN), BF),
        sgs=dma(3),
        sgr=dma(3),
        tg=pltpu.VMEM((SIDE, 8, 128), F32),
        tgs=dma(3),
        tgr=dma(3),
        gg=pltpu.VMEM((SIDE, 8, 512), F32),
        ggs=dma(3),
        ggr=dma(3),
        y=pair_scratch((512, 768), (512, 512), (16 * SIDE, 512), (512, 768)),
        small=pltpu.VMEM((SMALL, 512), F32),
        small_p=pltpu.VMEM((SMALL, 512), F32),
        mss=dma(),
        msr=dma(),
    )
    outs = dict(
        dx=((BLK, 512), F32),
        o_mixer=((1, 512), F32),
        o_ffn=((1, 512), F32),
        o_conv=((4, HW), F32),
        o_gain=((1, HW), F32),
        o_bias=((1, HH), F32),
        o_decay=((1, HH), F32),
        o_skip=((1, HH), F32),
        o_states=((4, 32), F32),
    )
    early = dict(
        bo=((512, 512), BF),
        so=((16 * SIDE, 512), BF),
        xo=((512, 768), BF),
    )
    if pair:
        early.update(zq=((512, 768), BF), bq=((512, 512), BF))
        early.update(sq=((16 * SIDE, 512), BF), xq=((512, 768), BF))
    ins = dict(da=da, db=db, ds=ds, s1=s1, gain=gain)
    ins.update(ffn_grad=ffn_grad, dconv=dconv, dgain=dgain, dhead=dhead, dstates=dstates)
    late = dict(z_w=z_w, n1=n1, wb=wb, wx=wx, wz=wz, ws=ws, dz=dz, x=x, dx1=dx1)
    return launch(project_back, ins, outs, scratch, 8, late=late, early=early)


def per_head(values):
    lane = iota((1, HW), 1)
    first = jnp.where(lane < HDIM, values[0], values[1])
    return jnp.where(lane < 2 * HDIM, first, values[2])


def head_select():
    return jnp.where(iota((8, HW), 1) // HDIM == iota((8, HW), 0), 1.0, 0.0).astype(F32)


def scalar_rows(ref):
    sub = iota((8, 1), 0)
    return jnp.where(sub == 0, ref[0], jnp.where(sub == 1, ref[1], jnp.where(sub == 2, ref[2], 0.0)))


def triangle():
    return jnp.where(iota((BLK, BLK), 0) <= iota((BLK, BLK), 1), 1.0, 0.0).astype(F32)


def silu_pair(v):
    sig = sigmoid(v)
    return v * sig, sig * (1.0 + v * (1.0 - sig))


def fill_padded(R):
    R.xpad[0:8] = jnp.zeros((8, HW), F32)
    R.xpad[8 : 8 + LEN] = R.xr[...]


def prepare(R):
    fill_padded(R)
    for b in range(SIDE):
        at = pl.ds(b * BLK, BLK)
        pre = R.xpad[5 + b * BLK : 5 + (b + 1) * BLK] * R.wc[0:1]
        for j in (1, 2, 3):
            pre = pre + R.xpad[5 + j + b * BLK : 5 + j + (b + 1) * BLK] * R.wc[j : j + 1]
        R.u_[at], R.du_[at] = silu_pair(pre)
        R.za_[at], R.dza_[at] = silu_pair(R.z[at])
        _, _, _, within, dt_c, within_c = step_block(R, b)
        R.xdt[at] = R.u_[at] * column_heads(dt_c)
        R.wr[b] = within
        R.wide[at] = column_heads(within_c)
        R.wcol[b] = within_c


def step_block(R, b):
    at = pl.ds(pl.multiple_of(b * BLK, BLK), BLK)
    raw = R.sr[:, at] + scalar_rows(R.bias)
    dt = softplus(raw)
    rate = -dt * jnp.exp(scalar_rows(R.decay))
    within = dot_nn(rate, triangle(), HIGHEST)
    return raw, dt, rate, within, jnp.transpose(dt), jnp.transpose(within)


def rope_turn(v, cosine, sine):
    return v * cosine + pltpu.roll(v, ADIM // 2, axis=1) * sine


def rope_tables():
    half = ADIM // 2
    freqs = np.float32(ROPE_BASE) ** (-np.arange(half, dtype=np.float32) / np.float32(half))
    angles = np.arange(LEN, dtype=np.float32)[:, None] * freqs.astype(np.float32)
    angles = angles.astype(np.float32).astype(np.float64)
    cosine, sine = np.cos(angles), np.sin(angles)
    return (
        np.concatenate([cosine, cosine], axis=1).astype(np.float32),
        np.concatenate([-sine, sine], axis=1).astype(np.float32),
    )


def key_scores(q, keys, c):
    s = dot_nt(q, keys) * SCALE
    return jnp.where(iota(s.shape, 1) <= c * BLK + iota(s.shape, 0), s, NEGATIVE)


def state_cols(R, kind, b):
    g = R.g
    return jnp.concatenate([g[2 * kind, b], g[2 * kind + 1, b]], axis=1)


def lower_decay(within_c, within_r, h):
    gaps = within_c[:, h : h + 1] - within_r[h : h + 1]
    return jnp.exp(jnp.where(iota((BLK, BLK), 1) <= iota((BLK, BLK), 0), gaps, NEGATIVE))


def head_mask(v, h):
    return jnp.where(iota((1, HW), 1) // HDIM == h, v, jnp.zeros_like(v))


def head_masks(v, h):
    return head_mask(v[0], h), head_mask(v[1], h)


def column_heads(cols):
    return per_head([cols[:, h : h + 1] for h in range(HH)])


def mixers_kernel(z, xr, br, sr, wc, wcs, bias, decay, skip, gain, cosine, sine, dy, wd):
    def mixers(R):
        r, c = here()
        greet(r, c, grid=True)
        g = R.g
        br = R.br
        pre = br[13 : 13 + BLK, 0:128] * R.wcs[0:1]
        for j in (1, 2, 3):
            pre = pre + br[13 + j : 13 + j + BLK, 0:128] * R.wcs[j : j + 1]
        g[r, c] = (pre * sigmoid(pre)).astype(BF)
        at = pl.ds(pl.multiple_of(c * BLK, BLK), BLK)
        cos, sin = R.cos[at], R.sin[at]
        kv = br[HALO : HALO + BLK, 384:512].astype(BF)
        turned = rope_turn(kv.astype(F32), cos, sin).astype(BF)
        kind, head = lax.div(r, 2), lax.rem(r, 2)
        kvb = R.kvb
        kvb[...] = jnp.where(kind == 0, turned, kv)
        slot = SIDE + kind

        @pl.when(head == kind)
        def _():
            g[slot, c] = kvb[...]

        def bc_hop(d):
            return hop(g.at[r, c], g.at[r, c], R.zs.at[d - 1], R.zr.at[d - 1], row=flip(r, d))

        def kv_hop(d):
            return hop(kvb, g.at[slot, c], R.ys.at[d - 1], R.yr.at[d - 1], row=flip(r, d))

        for d in (1, 2, 3):
            bc_hop(d).start()

            @pl.when(lax.div(flip(r, d), 2) == head)
            def _():
                kv_hop(d).start()

        R.arrive(R.wd, R.dy)

        def hidden_back(rows, j):
            return dot_nt(rows, R.wd[pl.ds(pl.multiple_of(j * BLK, BLK), BLK)])

        def finish(block, v):
            R.dh[pl.ds(pl.multiple_of(block * BLK, BLK), BLK)] = v

        first, second, before, close_h = scatter_cols(
            R.a, types.SimpleNamespace(g=R.dy), r, c, hidden_back, finish, moving=False
        )
        each(first)
        for d in (1, 2, 3):
            bc_hop(d).wait_recv()

            @pl.when(lax.rem(flip(r, d), 2) == kind)
            def _():
                kv_hop(d).wait_recv()

        g_hops = trio(R.gt, c, lambda j: g.at[:, j])
        g_hops[0].start()
        g_hops[1].start()
        for h in range(2):
            q = br[HALO : HALO + BLK, 128 + 128 * h : 256 + 128 * h].astype(BF).astype(F32)
            R.qr[h] = rope_turn(q, cos, sin).astype(BF)
        each(second)
        R.arrive(R.xr, R.z, R.sr)
        prepare(R)
        for out, own in zip((R.u, R.du, R.za, R.dza), (R.u_, R.du_, R.za_, R.dza_)):
            R.leave(out, own)
        trio_end(g_hops)

        state = R.state
        state[...] = jnp.zeros_like(state)
        st = R.n.st
        st[r, c] = jnp.zeros((8, BLK), F32)
        skip_row = per_head([R.skip[h] for h in range(HH)])

        def block(b, carry):
            at = pl.ds(pl.multiple_of(b * BLK, BLK), BLK)
            within, within_c, wide = R.wr[b], R.wcol[b], R.wide[at]
            bb, cb = state_cols(R, 0, b), state_cols(R, 1, b)
            x = R.xdt[at]
            xb = halves(x)
            scores = dot_nt(cb, bb)
            y = jnp.exp(wide) * fine(dot_nn, cb, halves(state[...]))
            for h in range(HH):
                a = halves(scores * lower_decay(within_c, within, h))
                y = y + fine(dot_nn, a, head_masks(xb, h))
            last = per_head([within[h : h + 1, BLK - 1 : BLK] for h in range(HH)])
            keep = jnp.exp(last - wide)
            R.states_[b] = state[...]
            state[...] = state[...] * jnp.exp(last) + fine(dot_tn, bb, halves(x * keep))
            y = y + skip_row * R.u_[at]
            gated = y * R.za_[at]
            R.ys_[at] = y
            R.gs[at] = gated
            sums = row_sums(gated * gated)
            st[r, c] = jnp.where(iota((8, BLK), 0) == b, sums, st[r, c])
            before(b)
            return carry

        lax.fori_loop(0, SIDE, block, 0)
        close = grid_sum(R.n, r, c)
        R.leave(R.g_o, g)
        R.leave(R.y, R.ys_)
        R.leave(R.states, R.states_)

        keys = g[4].reshape(LEN, ADIM)
        values = g[5].reshape(LEN, ADIM)
        for h in range(2):
            s = key_scores(R.qr[h], keys, c)
            top = jnp.max(s, axis=1, keepdims=True)
            lse = top + jnp.log(jnp.sum(jnp.exp(s - top), axis=1, keepdims=True))
            R.lse[h] = jnp.broadcast_to(lse, (BLK, 128))
            probs = jnp.exp(s - lse).astype(BF)
            R.o[:, 128 * h : 128 * h + 128] = dot_nn(probs, values).astype(BF)

        total = close()
        R.s3[...] = total
        scales = jnp.transpose(lax.rsqrt(total / (HEADS * HDIM) + EPSILON))

        def scaled(b, carry):
            at = pl.ds(pl.multiple_of(b * BLK, BLK), BLK)
            R.m[at] = (R.gs[at] * pick_column(scales, b) * R.gain[...]).astype(BF)
            return carry

        lax.fori_loop(0, SIDE, scaled, 0)
        close_h()
        for d in (1, 2, 3):
            bc_hop(d).wait_send()

            @pl.when(lax.div(flip(r, d), 2) == head)
            def _():
                kv_hop(d).wait_send()

        for one in g_hops:
            one.wait_send()

    scratch = dict(
        n=grid_scratch(),
        a=cols_scratch(256),
        g=pltpu.VMEM((6, SIDE, BLK, 128), BF),
        kvb=pltpu.VMEM((BLK, 128), BF),
        xpad=pltpu.VMEM((LEN + 8, HW), F32),
        wr=pltpu.VMEM((SIDE, 8, BLK), F32),
        wcol=pltpu.VMEM((SIDE, BLK, 8), F32),
        **{key: pltpu.VMEM((LEN, HW), F32) for key in ("u_", "du_", "za_", "dza_", "xdt", "wide")},
        gs=pltpu.VMEM((LEN, HW), F32),
        state=pltpu.VMEM((STATE, HW), F32),
        zs=dma(3),
        zr=dma(3),
        ys=dma(3),
        yr=dma(3),
        gt=trio_scratch(),
        ys_=pltpu.VMEM((LEN, HW), F32),
        states_=pltpu.VMEM((SIDE, STATE, HW), F32),
    )
    outs = dict(
        m=((LEN, HW), BF),
        o=((BLK, 256), BF),
        s3=((8, BLK), F32),
        lse=((2, BLK, 128), F32),
        qr=((2, BLK, 128), BF),
        dh=((LEN, 256), F32),
    )
    early = dict(
        y=((LEN, HW), F32),
        u=((LEN, HW), F32),
        du=((LEN, HW), F32),
        za=((LEN, HW), F32),
        dza=((LEN, HW), F32),
        states=((SIDE, STATE, HW), F32),
        g_o=((6, SIDE, BLK, 128), BF),
    )
    ins = dict(br=br, wc=wc, wcs=wcs, gain=gain, cos=cosine, sin=sine)
    late = dict(xr=xr, z=z, sr=sr, wd=wd, dy=dy)
    smem = dict(bias=bias, decay=decay, skip=skip)
    return launch(mixers, ins, outs, scratch, 9, smem, late, early)


def mixers_back_kernel(
    dm, do, u, du, za, dza, xr, br, sr, y, s3, states, g, qr, lse, wc, wcs, bias, decay, skip, gain, cosine, sine, x1, down, down_w, attn_w, up_w, n1, out_w
):
    n = BLK + HALO

    def mixers_back(R):
        r, c = here()
        greet(r, c, grid=True, dp=paired())
        y_hops = []
        if paired():
            y_hops = [
                pair_hop(R.yy, 0, R.up_w.at[pl.ds(256, 256)]),
                pair_hop(R.yy, 1, R.down_w),
                pair_hop(R.yy, 2, R.attn_w),
                pair_hop(R.yy, 3, R.out_w),
            ]
        R.arrive(R.up_w, R.down_w, R.attn_w, R.out_w)
        for one in y_hops:
            one.start()
        g = R.g
        st = R.n.st
        st[r, c] = jnp.zeros((8, BLK), F32)
        gain = R.gain[...]

        def inner(b, carry):
            at = pl.ds(pl.multiple_of(b * BLK, BLK), BLK)
            sums = row_sums(R.dm[at] * gain * R.y[at] * R.za[at])
            st[r, c] = jnp.where(iota((8, BLK), 0) == b, sums, st[r, c])
            return carry

        lax.fori_loop(0, SIDE, inner, 0)
        close = grid_sum(R.n, r, c)

        R.arrive(R.g, R.qr, R.lse, R.do)
        tb = R.tb
        tb[:, pl.ds(LEN, HALO)] = jnp.zeros((4, HALO, 128), F32)
        dkv_all = R.dkv_all
        keys = g[4].reshape(LEN, ADIM)
        values = g[5].reshape(LEN, ADIM)
        at = pl.ds(pl.multiple_of(c * BLK, BLK), BLK)
        cos, sin = R.cos[at], R.sin[at]
        for h in range(2):
            q = R.qr[h]
            dob = R.do[:, 128 * h : 128 * h + 128]
            p = jnp.exp(key_scores(q, keys, c) - R.lse[h][:, :1])
            dv = dot_tn(p.astype(BF), dob)
            dp = dot_nt(dob, values)
            ds = (p * (dp - jnp.sum(dp * p, axis=1, keepdims=True)) * SCALE).astype(BF)
            dk = dot_tn(ds, q)
            if h == 0:
                dkv_all[0] = dk
                dkv_all[1] = dv
            else:
                dkv_all[0] = dkv_all[0] + dk
                dkv_all[1] = dkv_all[1] + dv
            dq = dot_nn(ds, keys)
            R.db[:, 128 + 128 * h : 256 + 128 * h] = rope_turn(dq, cos, -sin).astype(BF)

        R.arrive(R.xr, R.sr, R.states, R.down, R.u, R.du, R.dza)
        fill_padded(R)
        close_kv = scatter_tokens(R.kv, c, lambda j: dkv_all[:, pl.ds(pl.multiple_of(j * BLK, BLK), BLK)])
        scales = jnp.transpose(lax.rsqrt(R.s3[...] / (HEADS * HDIM) + EPSILON))
        inners = jnp.transpose(close())
        for ref in (R.dgain, R.dskip, R.dconv, R.dhead, R.ds):
            ref[...] = jnp.zeros_like(ref)

        def through_norm(b):
            at = pl.ds(pl.multiple_of(b * BLK, BLK), BLK)
            yb, dm, zact = R.y[at], R.dm[at], R.za[at]
            gated = yb * zact
            scale = pick_column(scales, b)
            dgated = scale * dm * gain - gated * (scale * scale * scale * pick_column(inners, b) / (HEADS * HDIM))
            R.dgain[...] += jnp.sum(dm * gated * scale, axis=0, keepdims=True)
            R.dy[at] = dgated * zact
            R.zc.g[c, at] = (dgated * yb * R.dza[at]).astype(BF)

        each(through_norm)
        gather_cols(R.zc, r, c)

        step, close_d = scatter_rows(R.s, r, lambda t: R.down[t], lambda d: None)
        dstate, dpre_pad = R.dstate, R.dpre
        dstate[...] = jnp.zeros_like(dstate)
        dpre_pad[LEN : LEN + 8] = jnp.zeros((8, HW), F32)
        select = head_select()
        skip_row = per_head([R.skip[h] for h in range(HH)])
        rate_of = jnp.exp(scalar_rows(R.decay))
        upto = jnp.where(iota((BLK, BLK), 0) >= iota((BLK, BLK), 1), 1.0, 0.0).astype(F32)

        t = R.t

        def t_rows(b):
            return tb[:, pl.ds(pl.multiple_of(b * BLK, BLK), n)]

        def t_core(slot):
            return hop(t.cs.at[slot], t.cr.at[slot], t.ks.at[slot], t.kr.at[slot], col=flip(c, 1))

        t_over = hop(t.xs, t.xr, t.ss, t.sr, col=flip(c, 2))

        def leave_block(b):
            e = flip(c, b)

            @pl.when(lax.rem(e, 2) == 1)
            def _():
                slot = lax.div(e, 2)
                t.cs[slot] = t_rows(b).astype(BF)
                t_core(slot).start()

        def pass_block(b):
            @pl.when(flip(c, b) == 2)
            def _():
                t_core(1).wait_recv()
                t.xs[...] = (t_rows(b) + t.cr[1].astype(F32)).astype(BF)
                t_over.start()

        def block(i, carry):
            step(i)
            b = 3 - i

            @pl.when(i > 0)
            def _():
                pass_block(b + 1)

            at = pl.ds(pl.multiple_of(b * BLK, BLK), BLK)
            u = R.u[at]
            raw, dt, rate, within, dt_c, within_c = step_block(R, b)
            bb, cb = state_cols(R, 0, b), state_cols(R, 1, b)
            dy = R.dy[at]
            R.dskip[...] += jnp.sum(dy * u, axis=0, keepdims=True)
            dyb = halves(dy)
            wide = column_heads(within_c)
            grow = jnp.exp(wide)
            last = per_head([within[h : h + 1, BLK - 1 : BLK] for h in range(HH)])
            keep = jnp.exp(last - wide)
            dt_w = column_heads(dt_c)
            x = u * dt_w
            xb = halves(x)
            scores = dot_nt(cb, bb)
            state = R.states[b]
            stb = halves(state)
            yin = jnp.zeros((BLK, HW), F32)
            dx = jnp.zeros((BLK, HW), F32)
            dscores = jnp.zeros((BLK, BLK), F32)
            for h in range(HH):
                decay_h = lower_decay(within_c, within, h)
                a = halves(scores * decay_h)
                xh = head_masks(xb, h)
                yin = yin + fine(dot_nn, a, xh)
                dx = dx + fine(dot_tn, a, head_masks(dyb, h))
                dscores = dscores + fine(dot_nt, dyb, xh) * decay_h
            dsb = halves(dscores)
            dyg = dy * grow
            dygb = halves(dyg)
            xk = x * keep
            dst = dstate[...]
            dstb = halves(dst)
            dc = fine(dot_nn, dsb, bb) + fine(dot_nt, dygb, stb)
            db = fine(dot_tn, dsb, cb) + fine(dot_nt, halves(xk), dstb)
            tb[0, at] = db[:, :128]
            tb[1, at] = db[:, 128:]
            tb[2, at] = dc[:, :128]
            tb[3, at] = dc[:, 128:]
            dxk = fine(dot_nn, bb, dstb)
            carried = dxk * xk
            turn = dy * yin - x * dx + dyg * fine(dot_nn, cb, stb) - carried
            dx = dx + dxk * keep
            elast = jnp.exp(last)
            ends = jnp.sum(carried, axis=0, keepdims=True) + jnp.sum(dst * state, axis=0, keepdims=True) * elast
            dlast = dot_nt(select, jnp.broadcast_to(ends, (8, HW)), HIGHEST)[:, :1]
            drate = dot_nn(dot_nt(select, turn, HIGHEST), upto, HIGHEST) + dlast
            ddt = dot_nt(select, dx * u, HIGHEST) - drate * rate_of
            draw = ddt * sigmoid(raw)
            R.ds[0:8, at] = draw.astype(BF)
            lane = iota((8, 128), 1)
            R.dhead[...] += jnp.where(
                lane == 0,
                jnp.sum(draw, axis=1, keepdims=True),
                jnp.where(lane == 1, jnp.sum(drate * rate, axis=1, keepdims=True), 0.0),
            )
            dstate[...] = dst * elast + fine(dot_tn, cb, dygb)
            du = dx * dt_w + dy * skip_row
            dpre_pad[at] = du * R.du[at]
            leave_block(b)
            wait_cols(R.zc, r, c, 3 - swapped(i))
            return carry

        lax.fori_loop(0, SIDE, block, 0)
        total_kv = close_kv()
        R.kvb[...] = total_kv.astype(BF)
        kvb = R.kvb
        kind, head = lax.div(r, 2), lax.rem(r, 2)

        def kv_hop(d):
            to = flip(r, d)
            return hop(
                kvb.at[lax.div(to, 2)], R.zkr.at[d - 1], R.ys.at[d - 1], R.yr.at[d - 1], row=to
            )

        for d in (1, 2, 3):

            @pl.when(lax.rem(flip(r, d), 2) == kind)
            def _():
                kv_hop(d).start()

        dkv = R.dkv
        dkv[...] = jnp.zeros_like(dkv)

        @pl.when(head == kind)
        def _():
            dkv[...] = jnp.where(kind == 0, total_kv[0], total_kv[1])

        pass_block(0)
        R.dhead[...] += jnp.where(
            iota((8, 128), 1) == 2,
            dot_nt(select, jnp.broadcast_to(R.dskip[...], (8, HW)), HIGHEST)[:, :1],
            0.0,
        )

        for b in range(SIDE):
            dpre = dpre_pad[b * BLK : (b + 1) * BLK]
            dxr = jnp.zeros((BLK, HW), F32)
            for j in range(4):
                dxr = dxr + dpre_pad[3 - j + b * BLK : 3 - j + (b + 1) * BLK] * R.wc[j : j + 1]
                R.dconv[j : j + 1] += jnp.sum(
                    dpre * R.xpad[5 + j + b * BLK : 5 + j + (b + 1) * BLK], axis=0, keepdims=True
                )
            R.dxs[...] = dxr
            R.da[b * BLK : (b + 1) * BLK] = R.dxs[...].astype(BF)

        R.arrive(R.n1)
        for j in range(SIDE):
            R.dz_all[:, j * HW : (j + 1) * HW] = R.zc.g[j]
        R.zw[...] = dot_tn(R.n1[...], R.dz_all[...]).astype(BF)
        R.leave(R.dz_o, R.dz_all)
        R.leave(R.z_w, R.zw)
        t_core(0).wait_recv()
        t_over.wait_recv()
        total = t_rows(c) + t.cr[0].astype(F32) + t.xr[...].astype(F32)
        tob = R.tob
        tob[...] = total.astype(BF)
        mine = R.mine
        mine[...] = total

        def bc_hop(d):
            return hop(tob.at[flip(r, d)], R.zbr.at[d - 1], R.zs.at[d - 1], R.zr.at[d - 1], row=flip(r, d))

        for d in (1, 2, 3):
            bc_hop(d).start()

        dpost = mine[r]
        for d in (1, 2, 3):
            bc_hop(d).wait_recv()
            dpost = dpost + R.zbr[d - 1].astype(F32)

            @pl.when(lax.div(flip(r, d), 2) == head)
            def _():
                kv_hop(d).wait_recv()
                dkv[...] = dkv[...] + R.zkr[d - 1].astype(F32)

        R.arrive(R.br, R.x1)
        br = R.br
        pre = br[13 : 13 + n, 0:128] * R.wcs[0:1]
        for j in (1, 2, 3):
            pre = pre + br[13 + j : 13 + j + n, 0:128] * R.wcs[j : j + 1]
        sig = sigmoid(pre)
        dpre = dpost * sig * (1.0 + pre * (1.0 - sig))
        dbc = dpre[3 : 3 + BLK] * R.wcs[0:1]
        for j in (1, 2, 3):
            dbc = dbc + dpre[3 - j : 3 - j + BLK] * R.wcs[j : j + 1]
        R.db[:, 0:128] = dbc.astype(BF)
        for j in range(4):
            R.dstates[j : j + 1] = jnp.sum(dpre[0:BLK] * br[13 + j : 13 + j + BLK, 0:128], axis=0, keepdims=True)
        R.out[...] = (R.x1[...] + close_d()).astype(BF)
        dkv_v = dkv[...]
        R.db[:, 384:512] = jnp.where(kind == 0, rope_turn(dkv_v, cos, -sin), dkv_v).astype(BF)
        wait_cols_sent(R.zc, r, c)
        t_core(0).wait_send()
        t_core(1).wait_send()
        t_over.wait_send()
        for d in (1, 2, 3):
            bc_hop(d).wait_send()

            @pl.when(lax.rem(flip(r, d), 2) == kind)
            def _():
                kv_hop(d).wait_send()

        for one, theirs, out in zip(y_hops, (R.yy.A, R.yy.B, R.yy.C, R.yy.D), (R.up_p, R.down_p, R.attn_p, R.out_p) if y_hops else ()):
            one.wait_recv()
            R.leave(out, theirs)
            one.wait_send()

    scratch = dict(
        n=grid_scratch(),
        s=srows_scratch(),
        yy=pair_scratch((256, 1024), (LEN, 512), (256, 512), (SIDE * HW, 512)),
        zc=gcols_scratch(HW),
        dy=pltpu.VMEM((LEN, HW), F32),
        dxs=pltpu.VMEM((BLK, HW), F32),
        dz_all=pltpu.VMEM((LEN, 768), BF),
        zw=pltpu.VMEM((512, 768), BF),
        t=dict(
            cs=pltpu.VMEM((2, 4, n, 128), BF),
            cr=pltpu.VMEM((2, 4, n, 128), BF),
            xs=pltpu.VMEM((4, n, 128), BF),
            xr=pltpu.VMEM((4, n, 128), BF),
            ks=dma(2),
            kr=dma(2),
            ss=dma(),
            sr=dma(),
        ),
        kv=tokens_scratch(2, BLK, 128, low=BF),
        dkv_all=pltpu.VMEM((2, LEN, 128), F32),
        kvb=pltpu.VMEM((2, BLK, 128), BF),
        xpad=pltpu.VMEM((LEN + 8, HW), F32),
        dpre=pltpu.VMEM((LEN + 8, HW), F32),
        dstate=pltpu.VMEM((STATE, HW), F32),
        dskip=pltpu.VMEM((1, HW), F32),
        tb=pltpu.VMEM((4, LEN + HALO, 128), F32),
        tob=pltpu.VMEM((4, n, 128), BF),
        mine=pltpu.VMEM((4, n, 128), F32),
        dkv=pltpu.VMEM((BLK, 128), F32),
        zbr=pltpu.VMEM((3, n, 128), BF),
        zkr=pltpu.VMEM((3, BLK, 128), BF),
        zs=dma(3),
        zr=dma(3),
        ys=dma(3),
        yr=dma(3),
    )
    outs = dict(
        da=((LEN, HW), BF),
        db=((BLK, 512), BF),
        ds=((16, LEN), BF),
        dgain=((1, HW), F32),
        dconv=((4, HW), F32),
        dstates=((4, 128), F32),
        dhead=((8, 128), F32),
        out=((BLK, 512), BF),
    )
    early = dict(dz_o=((LEN, 768), BF), z_w=((512, 768), BF))
    if paired():
        early.update(up_p=((256, 1024), BF), down_p=((LEN, 512), BF), attn_p=((256, 512), BF))
        early.update(out_p=((SIDE * HW, 512), BF))
    ins = dict(dm=dm, za=za, y=y, s3=s3, wc=wc, wcs=wcs, gain=gain, cos=cosine, sin=sine)
    late = dict(g=g, qr=qr, lse=lse, do=do, down_w=down_w, up_w=up_w, attn_w=attn_w, out_w=out_w, n1=n1, xr=xr, sr=sr, states=states)
    late.update(u=u, du=du, dza=dza)
    late.update(down=down, br=br, x1=x1)
    smem = dict(bias=bias, decay=decay, skip=skip)
    return launch(mixers_back, ins, outs, scratch, 10, smem, late, early)


def dp_total(own, theirs):
    if theirs is not None:
        return own.astype(F32) + theirs.astype(F32)
    return lax.psum(own.astype(F32), "dp")


def on_device(
    block_input,
    mixer_gain,
    ssm_gate_weight,
    ssm_input_weight,
    ssm_bc_weight,
    ssm_step_weight,
    query_weight,
    keyval_weight,
    conv_input,
    conv_states,
    step_bias,
    decay_log,
    skip_gain,
    ssm_norm_gain,
    ssm_out_weight,
    attn_out_weight,
    ffn_gain,
    gate_up_weight,
    down_weight,
    cotangent,
):
    cosine, sine = (jnp.asarray(table) for table in rope_tables())
    step_w = jnp.pad(ssm_step_weight.T.reshape(SIDE, HH, -1), ((0, 0), (0, 16 - HH), (0, 0))).reshape(16 * SIDE, -1)
    wg, wu = gate_up_weight[:, 0], gate_up_weight[:, 1]
    mixer_row, ffn_row, ssm_row = mixer_gain[None], ffn_gain[None], ssm_norm_gain[None]
    wo, wt, wd = ssm_out_weight, attn_out_weight, down_weight

    p = project_kernel(
        block_input,
        mixer_row,
        ssm_gate_weight,
        ssm_input_weight,
        ssm_bc_weight,
        query_weight,
        keyval_weight,
        step_w,
        conv_states,
        cotangent,
    )
    heads = (conv_input, p.wcs, step_bias, decay_log, skip_gain, ssm_row, cosine, sine)
    m = mixers_kernel(p.z, p.xr, p.br, p.sr, *heads, p.dy, wd)
    f = forward_kernel(m.m, m.o, block_input, ffn_row, wo, wt, wg, wu, m.dh)
    b = backward_kernel(
        f.dgu, wg, wu, f.x1, f.s2, ffn_row, cotangent, f.n2_all, wo, wt, f.hid, wd, p.dy, f.m_all, f.o_all
    )
    mixed = (m.u, m.du, m.za, m.dza, p.xr, p.br, p.sr, m.y, m.s3, m.states, m.g_o, m.qr, m.lse)
    k = mixers_back_kernel(b.dm, b.do, *mixed, *heads, f.x1, b.down, b.down_w, b.attn_w, b.up_w, p.n1, b.out_w)
    q = project_back_kernel(
        k.da,
        k.db,
        k.ds,
        ssm_gate_weight,
        ssm_input_weight,
        p.wb_o,
        step_w,
        block_input,
        p.s1,
        mixer_row,
        b.dx1,
        p.n1,
        b.dgain,
        k.dconv,
        k.dgain,
        k.dhead,
        k.dstates,
        k.dz_o,
        k.z_w,
    )
    pair = paired()
    gate_grad = dp_total(b.gate_w, b.gate_p if pair else None)
    up_grad = dp_total(b.up_w, jnp.concatenate([b.up_p, k.up_p]) if pair else None)
    down_grad = dp_total(b.down_w, k.down_p if pair else None)
    out_grad = dp_total(b.out_w, k.out_p if pair else None)
    attn_grad = dp_total(b.attn_w, k.attn_p if pair else None)
    z_grad = dp_total(k.z_w, q.zq if pair else None)
    x_grad = dp_total(q.xo, q.xq if pair else None)
    b_grad = dp_total(q.bo, q.bq if pair else None)
    step_grad = dp_total(q.so, q.sq if pair else None)
    step_grad = step_grad.reshape(SIDE, 16, -1)[:, :HH].reshape(SIDE * HH, -1).T
    small = [q.o_mixer[0], q.o_conv, q.o_states, q.o_bias[0], q.o_decay[0], q.o_skip[0], q.o_gain[0], q.o_ffn[0]]
    if not pair:
        small = lax.psum(small, "dp")
    return (
        k.out,
        q.dx,
        small[0],
        z_grad,
        x_grad,
        b_grad[:, 0:128],
        step_grad,
        b_grad[:, 128:384],
        b_grad[:, 384:512],
        *small[1:7],
        out_grad,
        attn_grad,
        small[7],
        jnp.stack([gate_grad, up_grad], axis=1),
        down_grad,
    )


def solution(mesh):
    placed = (
        P(("dp", "row"), "col"),
        P("col"),
        P("col", "row"),
        P("col", "row"),
        P("col", "row"),
        P("col", "row"),
        P("col", "row"),
        P("col", "row"),
        P(None, ("row", "col")),
        P(None, ("row", "col")),
        P(("row", "col")),
        P(("row", "col")),
        P(("row", "col")),
        P(("row", "col")),
        P("row", "col"),
        P("row", "col"),
        P("col"),
        P("col", None, "row"),
        P("row", "col"),
        P(("dp", "row"), "col"),
    )
    return jax.shard_map(
        on_device,
        mesh=mesh,
        in_specs=placed,
        out_specs=(
            P(("dp", "row"), "col"),
            P(("dp", "row"), "col"),
            P("col"),
            P("col", "row"),
            P("col", "row"),
            P("col", "row"),
            P("col", "row"),
            P("col", "row"),
            P("col", "row"),
            P(None, ("row", "col")),
            P(None, ("row", "col")),
            P(("row", "col")),
            P(("row", "col")),
            P(("row", "col")),
            P(("row", "col")),
            P("row", "col"),
            P("row", "col"),
            P("col"),
            P("col", None, "row"),
            P("row", "col"),
        ),
        check_vma=False,
    )
```
